32 devices in a mesh: gal: 4 (over y, core), pix: 8 (over z, x).
Axes of the slice: x: 2, y: 2, z: 4, core: 2. Of those that a mesh axis runs over, the one named last changes fastest.
Arguments:
- observed: float32 [8192, 4096], P('pix', 'gal'), may hold values from -6 to 6
- sparse_init: float32 [8192, 4096], P('pix', 'gal'), may hold values from -4 to 4
- dual_init: float32 [8192, 4096], P('pix', 'gal'), may hold values from -4 to 4
- right_init: float32 [64, 4096], P(None, 'gal'), may hold values from -0.09375 to 0.09375
Outputs:
- sparse: float32 [8192, 4096], P('pix', 'gal')
- dual: float32 [8192, 4096], P('pix', 'gal')
- left: float32 [64, 8192], P(None, 'pix')
- right: float32 [64, 4096], P(None, 'gal')
The draws below stay inside these ranges and needn't reach their ends.
All inputs are finite; a program needn't handle non-finite values.
Results may differ from the reference program's by a relative error of at most 0.0003.
Values sent between devices are 32-bit elements; how exact they have to be, the bound alone decides.
No kernel may reach another device: no remote copies, remote signals or barrier semaphores. Data moves between devices by JAX's collectives and lax.ppermute only.
A program may use at most 64 MiB of HBM per device.

```python
import jax
import jax.numpy as jnp
from jax import lax

P_SIZE = 4096
R = 64
ITERS = 2
G = 8192


def block_scale(rng, extent, split, least, top_value):
    def one(dim, shards_of):
        draws = jax.random.uniform(jax.random.fold_in(jax.random.fold_in(rng, 6), dim), (shards_of,), jnp.float32, least / len(split), top_value / len(split))
        return jnp.repeat(jnp.exp(draws), extent[dim] // shards_of).reshape((-1,) + (1,) * (len(extent) - dim - 1))

    loudness = one(*split[0])
    for cut in split[1:]:
        loudness = loudness * one(*cut)
    return loudness


def normal_values(key, dims, spread, bound, cuts=(), held_as=jnp.bfloat16):
    level = block_scale(key, dims, cuts, -0.22, 0.18) if cuts else 1.0
    entries = jax.random.normal(key, dims, jnp.float32) * spread * level
    return jnp.minimum(jnp.maximum(entries, -bound), bound).astype(held_as)


def setup_inputs(seed: int = 0) -> dict:
    splits = jax.random.split(jax.random.key(seed), 5)
    return {
        "observed": normal_values(splits[0], (G, P_SIZE), 1.0, 6.0, ((0, 8), (1, 4)), jnp.float32),
        "sparse_init": normal_values(splits[1], (G, P_SIZE), 0.5, 4.0, ((0, 8), (1, 4)), jnp.float32),
        "dual_init": normal_values(splits[2], (G, P_SIZE), 0.5, 4.0, ((0, 8), (1, 4)), jnp.float32),
        "right_init": normal_values(splits[3], (R, P_SIZE), P_SIZE ** -0.5, 0.09375, ((1, 4),), jnp.float32),
    }


MU = 1.25
TAU = 0.6 / 1.25
HIGH = lax.Precision.HIGHEST

def orth(panel):
    gram = jnp.dot(panel, panel.T, precision=HIGH)
    factor = jnp.linalg.cholesky(gram)
    return jax.scipy.linalg.solve_triangular(factor, panel, lower=True)

def shrink(values):
    return jnp.sign(values) * jnp.maximum(jnp.abs(values) - TAU, 0.0)

def reference(observed, sparse_init, dual_init, right_init):
    sparse, dual, right = (sparse_init, dual_init, right_init)
    left = None
    for step in range(ITERS):
        target = observed - sparse + dual / MU
        panel = jnp.dot(right, target.T, precision=HIGH)
        left = orth(panel)
        wide = jnp.dot(left, target, precision=HIGH)
        lowrank = jnp.dot(left.T, wide, precision=HIGH)
        sparse = shrink(observed - lowrank + dual / MU)
        dual = dual + MU * (observed - lowrank - sparse)
        right = orth(wide)
    return (sparse, dual, left, right)
```

```python
import jax
import jax.numpy as jnp
from jax import lax
from jax.sharding import PartitionSpec as P

ITERS = 2


MU = 1.25
TAU = 0.6 / 1.25
HIGH = lax.Precision.HIGHEST
CORES = 2


def gram_of(panel):
    return lax.dot_general(panel, panel, (((1,), (1,)), ((), ())), precision=HIGH)


def apply_inverse(factor, panel):
    return jax.scipy.linalg.solve_triangular(factor, panel, lower=True)


def sum_exchange(value, axis, n):
    bit = 1
    while bit < n:
        value = value + lax.ppermute(value, axis, [(i, i ^ bit) for i in range(n)])
        bit *= 2
    return value


def sum_over_gal(value, axis, n):
    half = value.shape[0] // CORES
    core = lax.rem(lax.axis_index(axis), CORES)
    twin = [(i, i ^ 1) for i in range(n)]
    away = lax.dynamic_slice_in_dim(value, (1 - core) * half, half, 0)
    mine = lax.dynamic_slice_in_dim(value, core * half, half, 0)
    mine = mine + lax.ppermute(away, axis, twin)
    got = [
        lax.ppermute(mine, axis, [(i, (i + CORES * k) % n) for i in range(n)])
        for k in range(1, n // CORES)
    ]
    for piece in got:
        mine = mine + piece
    other = lax.ppermute(mine, axis, twin)
    first = jnp.where(core == 0, mine, other)
    second = jnp.where(core == 0, other, mine)
    return jnp.concatenate([first, second], axis=0)


def sum_over_pix(value, axis, n):
    part = value.shape[0] // n
    me = lax.axis_index(axis)
    total = lax.dynamic_slice_in_dim(value, me * part, part, 0)
    got = []
    for k in range(1, n):
        peer = lax.rem(me + k, n)
        piece = lax.dynamic_slice_in_dim(value, peer * part, part, 0)
        got.append(lax.ppermute(piece, axis, [(i, (i + k) % n) for i in range(n)]))
    for piece in got:
        total = total + piece
    whole = jnp.zeros_like(value)
    whole = lax.dynamic_update_slice_in_dim(whole, total, me * part, 0)
    for k in range(1, n):
        piece = lax.ppermute(total, axis, [(i, (i + k) % n) for i in range(n)])
        peer = lax.rem(me + n - k, n)
        whole = lax.dynamic_update_slice_in_dim(whole, piece, peer * part, 0)
    return whole


def solution(mesh):
    n_gal, n_pix = mesh.shape["gal"], mesh.shape["pix"]

    def per_device(observed, sparse_init, dual_init, right_init):
        sparse, scaled, right = (None, dual_init / MU, right_init)
        target = observed - sparse_init + scaled
        for step in range(ITERS):
            last = step == ITERS - 1
            partial_left = lax.dot_general(right, target, (((1,), (1,)), ((), ())), precision=HIGH)
            panel = sum_over_gal(partial_left, "gal", n_gal)
            gram_left = sum_exchange(gram_of(panel), "pix", n_pix)
            raw = sum_over_pix(jnp.dot(panel, target, precision=HIGH), "pix", n_pix)
            factor = jnp.linalg.cholesky(gram_left)
            left = apply_inverse(factor, panel)
            wide = apply_inverse(factor, raw)
            if last:
                gram_right = sum_exchange(gram_of(wide), "gal", n_gal)
                right = apply_inverse(jnp.linalg.cholesky(gram_right), wide)
            else:
                right = wide
            lowrank = lax.dot_general(left, wide, (((0,), (0,)), ((), ())), precision=HIGH)
            value = observed - lowrank + scaled
            scaled = jnp.clip(value, -TAU, TAU)
            sparse = value - scaled
            target = observed - sparse + scaled
        return (sparse, MU * scaled, left, right)

    return jax.shard_map(
        per_device,
        mesh=mesh,
        in_specs=(P("pix", "gal"), P("pix", "gal"), P("pix", "gal"), P(None, "gal")),
        out_specs=(P("pix", "gal"), P("pix", "gal"), P(None, "pix"), P(None, "gal")),
        check_vma=False,
    )
```

```python
import jax
import jax.numpy as jnp
from jax import lax
from jax.sharding import PartitionSpec as P

ITERS = 2


MU = 1.25
TAU = 0.6 / 1.25
HIGH = lax.Precision.HIGHEST
CORES = 2


def gram_of(panel):
    return lax.dot_general(panel, panel, (((1,), (1,)), ((), ())), precision=HIGH)


def apply_inverse(factor, panel):
    return jax.scipy.linalg.solve_triangular(factor, panel, lower=True)


def sum_exchange(value, axis, n):
    bit = 1
    while bit < n:
        value = value + lax.ppermute(value, axis, [(i, i ^ bit) for i in range(n)])
        bit *= 2
    return value


def sum_over_gal(value, axis, n):
    half = value.shape[0] // CORES
    core = lax.rem(lax.axis_index(axis), CORES)
    twin = [(i, i ^ 1) for i in range(n)]
    away = lax.dynamic_slice_in_dim(value, (1 - core) * half, half, 0)
    mine = lax.dynamic_slice_in_dim(value, core * half, half, 0)
    mine = mine + lax.ppermute(away, axis, twin)
    got = [
        lax.ppermute(mine, axis, [(i, (i + CORES * k) % n) for i in range(n)])
        for k in range(1, n // CORES)
    ]
    for piece in got:
        mine = mine + piece
    other = lax.ppermute(mine, axis, twin)
    first = jnp.where(core == 0, mine, other)
    second = jnp.where(core == 0, other, mine)
    return jnp.concatenate([first, second], axis=0)


def sum_over_pix(value, axis, n):
    rows, columns = value.shape
    got = lax.all_to_all(value, axis, 0, 0, tiled=True)
    total = jnp.sum(got.reshape(n, rows // n, columns), axis=0)
    total = jnp.broadcast_to(total[None], (n, rows // n, columns))
    return lax.all_to_all(total.reshape(rows, columns), axis, 0, 0, tiled=True)


def solution(mesh):
    n_gal, n_pix = mesh.shape["gal"], mesh.shape["pix"]

    def per_device(observed, sparse_init, dual_init, right_init):
        sparse, scaled, right = (None, dual_init / MU, right_init)
        target = observed - sparse_init + scaled
        for step in range(ITERS):
            last = step == ITERS - 1
            partial_left = lax.dot_general(right, target, (((1,), (1,)), ((), ())), precision=HIGH)
            panel = sum_over_gal(partial_left, "gal", n_gal)
            raw = jnp.dot(panel, target, precision=HIGH)
            both = sum_over_pix(jnp.concatenate([raw, gram_of(panel)], axis=1), "pix", n_pix)
            raw, gram_left = both[:, : raw.shape[1]], both[:, raw.shape[1] :]
            factor = jnp.linalg.cholesky(gram_left)
            left = apply_inverse(factor, panel)
            wide = apply_inverse(factor, raw)
            if last:
                gram_right = sum_exchange(gram_of(wide), "gal", n_gal)
                right = apply_inverse(jnp.linalg.cholesky(gram_right), wide)
            else:
                right = wide
            lowrank = lax.dot_general(left, wide, (((0,), (0,)), ((), ())), precision=HIGH)
            value = observed - lowrank + scaled
            scaled = jnp.clip(value, -TAU, TAU)
            sparse = value - scaled
            target = observed - sparse + scaled
        return (sparse, MU * scaled, left, right)

    return jax.shard_map(
        per_device,
        mesh=mesh,
        in_specs=(P("pix", "gal"), P("pix", "gal"), P("pix", "gal"), P(None, "gal")),
        out_specs=(P("pix", "gal"), P("pix", "gal"), P(None, "pix"), P(None, "gal")),
        check_vma=False,
    )
```

```python
import jax
import jax.numpy as jnp
from jax import lax
from jax.experimental import pallas as pl
from jax.experimental.pallas import tpu as pltpu
from jax.sharding import PartitionSpec as P

ITERS = 2


MU = 1.25
TAU = 0.6 / 1.25
HIGH = lax.Precision.HIGHEST
CORES = 2
LANES = 128
F32, BF16 = jnp.float32, jnp.bfloat16
MIB = 1 << 20


def split(value):
    high = value.astype(BF16)
    return high, (value - high.astype(F32)).astype(BF16)


def dot(a, b, dims, precision=None):
    return lax.dot_general(a, b, (dims, ((), ())), precision=precision, preferred_element_type=F32)


def dot_nt(a, b):
    rows = a[0].shape[0]
    both = dot(jnp.concatenate(a, axis=0), b[0], ((1,), (1,)))
    return both[:rows] + both[rows:] + dot(a[0], b[1], ((1,), (1,)))


def dot_nn(a, b):
    rows = a[0].shape[0]
    both = dot(jnp.concatenate(a, axis=0), b[0], ((1,), (0,)))
    return both[:rows] + both[rows:] + dot(a[0], b[1], ((1,), (0,)))


def call(body, name, scalars, ins, outs, grid, scratch=(), aliases=None, cost=(0, 0), limit=24):
    return pl.pallas_call(
        body,
        name=name,
        grid_spec=pltpu.PrefetchScalarGridSpec(
            num_scalar_prefetch=1,
            grid=grid,
            in_specs=[
                pl.BlockSpec(block, index) if block else pl.BlockSpec(memory_space=pl.ANY)
                for _, block, index in ins
            ],
            out_specs=[pl.BlockSpec(block, index) for _, _, block, index in outs],
            scratch_shapes=list(scratch),
        ),
        out_shape=[jax.ShapeDtypeStruct(shape, dtype) for shape, dtype, _, _ in outs],
        input_output_aliases=aliases or {},
        compiler_params=pltpu.CompilerParams(vmem_limit_bytes=limit * MIB),
        cost_estimate=pl.CostEstimate(flops=cost[0], bytes_accessed=cost[1], transcendentals=0),
    )(scalars, *[array for array, _, _ in ins])


def unstack(ref):
    blocks = ref.shape[0] // 64
    return jnp.concatenate([ref[64 * t : 64 * (t + 1), :] for t in range(blocks)], axis=1)


def solution(mesh):
    n_gal, n_pix = mesh.shape["gal"], mesh.shape["pix"]
    levels = n_pix.bit_length() - 1

    def swap(value, axis, bit):
        n = mesh.shape[axis]
        return lax.ppermute(value, axis, [(i, i ^ bit) for i in range(n)])

    def per_device(observed, sparse_init, dual_init, right_init):
        rank = right_init.shape[0]
        n_rows, n_cols = observed.shape
        half = n_cols // 2
        tall = min(256, n_rows // 2)
        steps = n_rows // tall
        core = lax.rem(lax.axis_index("gal"), CORES)
        side = lax.rem(lax.axis_index("pix"), 2)
        scalars = jnp.stack([core, side]).astype(jnp.int32)
        stack_rows = rank * (half // LANES)
        gram_rows = rank * rank // LANES

        def gal_block(i, s):
            return lax.rem(i + (1 - s[0]) * (steps // 2), steps)

        def natural(p):
            return (tall, half), lambda i, s: (gal_block(i, s), (s[1] + p) % 2)

        block = (tall, half), lambda i, s: (i, 0)
        strip = (rank, tall), lambda i, s: (0, i)

        def whole(shape):
            return shape, lambda i, s: (0, 0)

        def first(right):
            def body(s, o0, o1, s0, s1, d0, d1, r0, r1, h0, l0, h1, l1, part):
                total = None
                for o, sp, d, r, h, l in ((o0, s0, d0, r0, h0, l0), (o1, s1, d1, r1, h1, l1)):
                    pair = split(o[...] - sp[...] + d[...] * (1 / MU))
                    h[...], l[...] = pair
                    term = dot_nt(split(r[...]), pair)
                    total = term if total is None else total + term
                part[...] = total

            def columns(p):
                return (rank, half), lambda i, s: (0, (s[1] + p) % 2)

            ins = [(a, *natural(p)) for a in (observed, sparse_init, dual_init) for p in (0, 1)]
            ins += [(right, *columns(p)) for p in (0, 1)]
            outs = [((n_rows, half), BF16, *block)] * 4 + [((rank, n_rows), F32, *strip)]
            cost = (6 * rank * n_rows * n_cols, 16 * n_rows * n_cols)
            h0, l0, h1, l1, part = call(body, "first", scalars, ins, outs, (steps,), cost=cost)
            return (h0, l0), (h1, l1), part

        def sum_gal(part):
            away, mine = jnp.split(part, 2, axis=1)
            mine = mine + swap(away, "gal", 1)
            got = [
                lax.ppermute(mine, "gal", [(i, (i + CORES * k) % n_gal) for i in range(n_gal)])
                for k in range(1, n_gal // CORES)
            ]
            for piece in got:
                mine = mine + piece
            return jnp.concatenate([swap(mine, "gal", 1), mine], axis=1)

        def multiply(panel, pair, with_gram):
            def body(s, whole_panel, panel, high, low, out, total):
                i = pl.program_id(0)
                term = dot_nn(split(panel[...]), (high[...], low[...]))

                @pl.when(i == 0)
                def _():
                    total[...] = term

                @pl.when(i > 0)
                def _():
                    total[...] += term

                @pl.when(i == steps - 1)
                def _():
                    for t in range(half // LANES):
                        out[rank * t : rank * (t + 1), :] = total[:, LANES * t : LANES * (t + 1)]
                    if with_gram:
                        gram = dot(whole_panel[...], whole_panel[...], ((1,), (1,)), HIGH)
                        packed = jnp.concatenate([gram[:gram_rows], gram[gram_rows:]], axis=1)
                        out[stack_rows : stack_rows + gram_rows, :] = packed

            rows = stack_rows + (gram_rows if with_gram else 0)
            ins = [(panel, *whole(panel.shape)), (panel, *strip), (pair[0], *block), (pair[1], *block)]
            outs = [((rows, LANES), F32, *whole((rows, LANES)))]
            cost = (3 * rank * n_rows * n_cols, 2 * n_rows * n_cols)
            scratch = [pltpu.VMEM((rank, half), F32)]
            return call(body, "multiply", scalars, ins, outs, (steps,), scratch, cost=cost)[0]

        def eliminate(one, two):
            def body(s, one, two, out):
                packed = one[...] + two[...]
                lane = lax.broadcasted_iota(jnp.int32, (8, LANES), 1)
                sub = lax.broadcasted_iota(jnp.int32, (8, LANES), 0)
                turned = pltpu.roll(packed, LANES // 2, 1)
                rows = []
                for j in range(rank // 8):
                    source = packed if 8 * j < gram_rows else turned
                    at = 8 * j % gram_rows
                    eye = jnp.where(lane - rank == sub + 8 * j, 1.0, 0.0)
                    rows.append(jnp.where(lane < rank, source[at : at + 8], eye))
                for k in range(rank):
                    r, at = divmod(k, 8)
                    pivot_row = rows[r][at : at + 1, :]
                    pivot = pivot_row[:, k : k + 1]
                    scaled = pivot_row * (1.0 / pivot)
                    out[k : k + 1, :] = (pivot_row * lax.rsqrt(pivot))[:, rank:]
                    for j in range(r, rank // 8):
                        column = rows[j][:, k : k + 1]
                        if j == r:
                            column = jnp.where(sub[:, :1] > at, column, 0.0)
                        rows[j] = rows[j] - column * scaled

            shape = (gram_rows, LANES)
            ins = [(one, *whole(shape)), (two, *whole(shape))]
            outs = [((rank, rank), F32, *whole((rank, rank)))]
            cost = (10**9, 20 * MIB)
            return call(body, "eliminate", scalars, ins, outs, (1,), cost=cost)[0]

        def sum_pix(send, own):
            got = swap(send, "pix", 1)
            value, gram = own + got[:stack_rows], send[stack_rows:] + got[stack_rows:]
            me = lax.axis_index("pix")
            for level in range(1, levels - 1):
                mine = lax.rem(me >> level, 2)
                rows = value.shape[0] // 2
                away = lax.dynamic_slice_in_dim(value, (1 - mine) * rows, rows, 0)
                value = lax.dynamic_slice_in_dim(value, mine * rows, rows, 0)
                got = swap(jnp.concatenate([away, gram], axis=0), "pix", 1 << level)
                value, gram = value + got[:rows], gram + got[rows:]
            rows = value.shape[0]
            got = swap(jnp.concatenate([value, gram], axis=0), "pix", 1 << (levels - 1))
            value = value + got[:rows]
            inverse = eliminate(gram, got[rows:])
            for level in range(levels - 2, 0, -1):
                mine = lax.rem(me >> level, 2)
                got = swap(value, "pix", 1 << level)
                low = jnp.where(mine == 0, value, got)
                high = jnp.where(mine == 0, got, value)
                value = jnp.concatenate([low, high], axis=0)
            return inverse, value, swap(value, "pix", 1)

        def prepare(s, inverse, panel, stacked, wide):
            @pl.when(pl.program_id(0) == 0)
            def _():
                wide[...] = dot(inverse[...], unstack(stacked), ((1,), (0,)), HIGH)

            left = dot(inverse[...], panel[...], ((1,), (0,)), HIGH)
            left_high, left_low = split(left)
            wide_high, wide_low = split(wide[...])
            lowrank = dot(
                jnp.concatenate([left_high, left_low, left_high], axis=0),
                jnp.concatenate([wide_high, wide_high, wide_low], axis=0),
                ((0,), (0,)),
            )
            return left, (wide_high, wide_low), lowrank

        def middle(p, inverse, panel, stacked, part):
            def body(s, inverse, panel, stacked, o, d, *rest):
                before = rest[0] if p else None
                base, high, low, after, wide = rest[p:]
                _, right, lowrank = prepare(s, inverse, panel, stacked, wide)
                value = o[...] + d[...] * (1 / MU) - lowrank
                scaled = jnp.clip(value, -TAU, TAU)
                base[...] = o[...] + scaled
                pair = split(o[...] + 2.0 * scaled - value)
                high[...], low[...] = pair
                term = dot_nt(right, pair)
                after[...] = before[...] + term if p else term

            ins = [(inverse, *whole(inverse.shape)), (panel, *strip), (stacked, *whole(stacked.shape))]
            ins += [(observed, *natural(p)), (dual_init, *natural(p))]
            ins += [(part, *strip)] * p
            outs = [((n_rows, half), F32, *block)] + [((n_rows, half), BF16, *block)] * 2
            outs += [((rank, n_rows), F32, *strip)]
            cost = (9 * rank * n_rows * n_cols, 8 * n_rows * n_cols)
            scratch = [pltpu.VMEM((rank, half), F32)]
            base, high, low, part = call(body, "middle", scalars, ins, outs, (steps,), scratch, cost=cost)
            return base, (high, low), part

        def final(p, inverse, panel, stacked, base, before):
            def body(s, inverse, panel, stacked, base, *rest):
                sparse, dual, left_out, wide = rest[3 * p :]
                left, _, lowrank = prepare(s, inverse, panel, stacked, wide)
                value = base[...] - lowrank
                scaled = jnp.clip(value, -TAU, TAU)
                sparse[...] = value - scaled
                dual[...] = MU * scaled
                left_out[...] = left

            ins = [(inverse, *whole(inverse.shape)), (panel, *strip), (stacked, *whole(stacked.shape))]
            ins += [(base, *block)]
            out_strip = (rank, tall), lambda i, s: (0, gal_block(i, s))
            outs = [((n_rows, n_cols), F32, *natural(p))] * 2 + [((rank, n_rows), F32, *out_strip)]
            aliases = {}
            if p:
                ins += [(a, None, None) for a in before]
                aliases = {5: 0, 6: 1, 7: 2}
            cost = (3 * rank * n_rows * n_cols, 6 * n_rows * n_cols)
            scratch = [pltpu.VMEM((rank, half), F32)]
            return call(body, "final", scalars, ins, outs, (steps,), scratch, aliases, cost)

        def widen(inverse, own, other):
            def body(s, inverse, own, other, wide, out):
                gram = None
                for p, stacked in enumerate((own, other)):
                    value = dot(inverse[...], unstack(stacked), ((1,), (0,)), HIGH)
                    wide[:, half * p : half * (p + 1)] = value
                    term = dot(value, value, ((1,), (1,)), HIGH)
                    gram = term if gram is None else gram + term
                out[...] = jnp.concatenate([gram[:gram_rows], gram[gram_rows:]], axis=1)

            ins = [(a, *whole(a.shape)) for a in (inverse, own, other)]
            outs = [((rank, n_cols), F32, *whole((rank, n_cols)))]
            outs += [((gram_rows, LANES), F32, *whole((gram_rows, LANES)))]
            return call(body, "widen", scalars, ins, outs, (1,), cost=(10**8, MIB))

        def finish(inverse, wide):
            def body(s, inverse, wide, out):
                for p in (0, 1):
                    at = pl.multiple_of(lax.rem(s[1] + p, 2) * half, half)
                    value = wide[:, half * p : half * (p + 1)]
                    out[:, pl.ds(at, half)] = dot(inverse[...], value, ((1,), (0,)), HIGH)

            ins = [(a, *whole(a.shape)) for a in (inverse, wide)]
            outs = [((rank, n_cols), F32, *whole((rank, n_cols)))]
            return call(body, "finish", scalars, ins, outs, (1,), cost=(10**8, MIB))[0]

        own, other, part = first(right_init)
        base = None
        for step in range(ITERS):
            panel = sum_gal(part)
            send = multiply(panel, other, True)
            inverse, own_wide, other_wide = sum_pix(send, multiply(panel, own, False))
            if step < ITERS - 1:
                base0, own, part = middle(0, inverse, panel, own_wide, None)
                base1, other, part = middle(1, inverse, panel, other_wide, part)
            else:
                outs = final(0, inverse, panel, own_wide, base0, None)
                wide, gram = widen(inverse, own_wide, other_wide)
                bit = 1
                while 2 * bit < n_gal:
                    gram = gram + swap(gram, "gal", bit)
                    bit *= 2
                got = swap(gram, "gal", bit)
                sparse, dual, left = final(1, inverse, panel, other_wide, base1, outs)
                right = finish(eliminate(gram, got), wide)
        return sparse, dual, left, right

    return jax.shard_map(
        per_device,
        mesh=mesh,
        in_specs=(P("pix", "gal"), P("pix", "gal"), P("pix", "gal"), P(None, "gal")),
        out_specs=(P("pix", "gal"), P("pix", "gal"), P(None, "pix"), P(None, "gal")),
        check_vma=False,
    )
```

```python
import jax
import jax.numpy as jnp
from jax import lax
from jax.experimental import pallas as pl
from jax.experimental.pallas import tpu as pltpu
from jax.sharding import PartitionSpec as P

ITERS = 2


MU = 1.25
TAU = 0.6 / 1.25
HIGH = lax.Precision.HIGHEST
CORES = 2
LANES = 128
F32, BF16 = jnp.float32, jnp.bfloat16
MIB = 1 << 20


def split(value):
    high = value.astype(BF16)
    return high, (value - high.astype(F32)).astype(BF16)


def dot(a, b, dims, precision=None):
    return lax.dot_general(a, b, (dims, ((), ())), precision=precision, preferred_element_type=F32)


def dot_nt(a, b):
    rows = a[0].shape[0]
    both = dot(jnp.concatenate(a, axis=0), b[0], ((1,), (1,)))
    return both[:rows] + both[rows:] + dot(a[0], b[1], ((1,), (1,)))


def dot_nn(a, b):
    rows = a[0].shape[0]
    both = dot(jnp.concatenate(a, axis=0), b[0], ((1,), (0,)))
    return both[:rows] + both[rows:] + dot(a[0], b[1], ((1,), (0,)))


def call(body, name, ins, outs, scratch=(), aliases=None, cost=(0, 0), limit=24):
    return pl.pallas_call(
        body,
        name=name,
        in_specs=[pl.BlockSpec(memory_space=space) for _, space in ins],
        out_specs=[pl.BlockSpec(memory_space=space) for _, _, space in outs],
        out_shape=[jax.ShapeDtypeStruct(shape, dtype) for shape, dtype, _ in outs],
        scratch_shapes=list(scratch),
        input_output_aliases=aliases or {},
        compiler_params=pltpu.CompilerParams(vmem_limit_bytes=limit * MIB),
        cost_estimate=pl.CostEstimate(flops=cost[0], bytes_accessed=cost[1], transcendentals=0),
    )(*[pltpu.with_memory_space_constraint(a, pltpu.HBM) if m is pltpu.HBM else a for a, m in ins])


def invert(packed, out):
    gram_rows, rank = packed.shape[0], out.shape[0]
    full = (8, LANES)
    lane = lax.broadcasted_iota(jnp.int32, full, 1)
    sub = lax.broadcasted_iota(jnp.int32, full, 0)
    turned = pltpu.roll(packed, LANES // 2, 1)
    rows = []
    for j in range(rank // 8):
        source = packed if 8 * j < gram_rows else turned
        at = 8 * j % gram_rows
        eye = jnp.where(lane - rank == sub + 8 * j, 1.0, 0.0)
        rows.append(jnp.where(lane < rank, source[at : at + 8], eye))
    wide = 4
    for k in range(0, rank, wide):
        r, at = divmod(k, 8)
        after = range(r if at + wide < 8 else r + 1, rank // 8)
        lines = [jnp.broadcast_to(rows[r][at + p : at + p + 1, :], full) for p in range(wide)]
        core = {
            (p, q): jnp.broadcast_to(lines[p][:, k + q : k + q + 1], full)
            for p in range(wide)
            for q in range(p, wide)
        }
        columns = {
            (j, p): jnp.broadcast_to(rows[j][:, k + p : k + p + 1], full) for j in after for p in range(wide)
        }
        for p in range(wide):
            inverse = 1.0 / core[p, p]
            factors = [core[p, q] * inverse for q in range(p + 1, wide)]
            for q, factor in zip(range(p + 1, wide), factors):
                for t in range(q, wide):
                    core[q, t] = core[q, t] - factor * core[p, t]
            scaled = lines[p] * inverse
            for q in range(p + 1, wide):
                lines[q] = lines[q] - core[p, q] * scaled
            for j in after:
                column = columns[j, p]
                if j == r:
                    column = jnp.where(sub >= at + wide, column, 0.0)
                rows[j] = rows[j] - column * scaled
                for q, factor in zip(range(p + 1, wide), factors):
                    columns[j, q] = columns[j, q] - factor * columns[j, p]
            done = lines[p] * lax.rsqrt(core[p, p])
            out[k + p : k + p + 1, :] = done[0:1, rank:]


def unstack(ref):
    blocks = ref.shape[0] // 64
    return jnp.concatenate([ref[64 * t : 64 * (t + 1), :] for t in range(blocks)], axis=1)


def solution(mesh):
    n_gal, n_pix = mesh.shape["gal"], mesh.shape["pix"]
    levels = n_pix.bit_length() - 1

    def swap(value, axis, bit):
        n = mesh.shape[axis]
        return lax.ppermute(value, axis, [(i, i ^ bit) for i in range(n)])

    def per_device(observed, sparse_init, dual_init, right_init):
        rank = right_init.shape[0]
        n_rows, n_cols = observed.shape
        half = n_cols // 2
        tall = min(256, n_rows // 2)
        steps = n_rows // tall
        core = lax.rem(lax.axis_index("gal"), CORES)
        side = lax.rem(lax.axis_index("pix"), 2)
        scalars = jnp.stack([core, side]).astype(jnp.int32)
        stack_rows = rank * (half // LANES)
        gram_rows = rank * rank // LANES
        where = (scalars, pltpu.SMEM)

        def gal_at(i, s):
            turn = (1 - s[0]) * (steps // 2)
            return pl.multiple_of(lax.rem(i + turn, steps) * tall, tall)

        def pix_at(p, s):
            return pl.multiple_of(lax.rem(s[1] + p, 2) * half, half)

        def chunk(i):
            return slice(tall * i, tall * (i + 1))

        def first(right):
            def body(s, o_in, s_in, d_in, r_in, o0, o1, d0, d1, h0, l0, h1, l1, part, s0, s1, right, r_sem, sems):
                moves = {}
                right_move = pltpu.make_async_copy(r_in, right, r_sem)
                right_move.start()
                for i in range(steps):
                    for p, targets in enumerate(((o0, s0, d0), (o1, s1, d1))):
                        for a, (source, target) in enumerate(zip((o_in, s_in, d_in), targets)):
                            block = source.at[pl.ds(gal_at(i, s), tall), pl.ds(pix_at(p, s), half)]
                            move = pltpu.make_async_copy(block, target.at[chunk(i), :], sems.at[i, p, a])
                            move.start()
                            moves[i, p, a] = move
                right_move.wait()
                rights = [split(right[:, pl.ds(pix_at(p, s), half)]) for p in (0, 1)]
                for i in range(steps):
                    total = None
                    for p, (o, sp, d, h, l) in enumerate(((o0, s0, d0, h0, l0), (o1, s1, d1, h1, l1))):
                        for a in range(3):
                            moves[i, p, a].wait()
                        pair = split(o[chunk(i), :] - sp[chunk(i), :] + d[chunk(i), :] * (1 / MU))
                        h[chunk(i), :], l[chunk(i), :] = pair
                        term = dot_nt(rights[p], pair)
                        total = term if total is None else total + term
                    part[:, chunk(i)] = total

            ins = [where] + [(a, pltpu.HBM) for a in (observed, sparse_init, dual_init, right)]
            outs = [((n_rows, half), F32, pltpu.VMEM)] * 4 + [((n_rows, half), BF16, pltpu.VMEM)] * 4
            outs += [((rank, n_rows), F32, pltpu.VMEM)]
            scratch = [pltpu.VMEM((n_rows, half), F32)] * 2 + [pltpu.VMEM((rank, n_cols), F32)]
            scratch += [pltpu.SemaphoreType.DMA(()), pltpu.SemaphoreType.DMA((steps, 2, 3))]
            cost = (6 * rank * n_rows * n_cols, 16 * n_rows * n_cols)
            got = call(body, "first", ins, outs, scratch, cost=cost)
            return got[0:2], got[2:4], got[4:6], got[6:8], got[8]

        def sum_gal(part):
            away, mine = jnp.split(part, 2, axis=1)
            mine = mine + swap(away, "gal", 1)
            got = [
                lax.ppermute(mine, "gal", [(i, (i + CORES * k) % n_gal) for i in range(n_gal)])
                for k in range(1, n_gal // CORES)
            ]
            for piece in got:
                mine = mine + piece
            return jnp.concatenate([swap(mine, "gal", 1), mine], axis=1)

        def multiply(panel, pair, with_gram):
            def body(panel, high, low, out):
                total = dot_nn(split(panel[...]), (high[...], low[...]))
                for t in range(half // LANES):
                    out[rank * t : rank * (t + 1), :] = total[:, LANES * t : LANES * (t + 1)]
                if with_gram:
                    gram = dot(panel[...], panel[...], ((1,), (1,)), HIGH)
                    packed = jnp.concatenate([gram[:gram_rows], gram[gram_rows:]], axis=1)
                    out[stack_rows : stack_rows + gram_rows, :] = packed

            rows = stack_rows + (gram_rows if with_gram else 0)
            ins = [(panel, pltpu.VMEM), (pair[0], pltpu.VMEM), (pair[1], pltpu.VMEM)]
            outs = [((rows, LANES), F32, pltpu.VMEM)]
            cost = (3 * rank * n_rows * n_cols, 2 * n_rows * n_cols)
            return call(body, "multiply", ins, outs, cost=cost)[0]

        def eliminate(one, two):
            def body(one, two, out):
                invert(one[...] + two[...], out)

            ins = [(one, pltpu.VMEM), (two, pltpu.VMEM)]
            outs = [((rank, rank), F32, pltpu.VMEM)]
            return call(body, "eliminate", ins, outs, cost=(10**8, 8 * MIB))[0]

        def sum_pix(send, own):
            got = swap(send, "pix", 1)
            value, gram = own + got[:stack_rows], send[stack_rows:] + got[stack_rows:]
            me = lax.axis_index("pix")
            for level in range(1, levels - 1):
                mine = lax.rem(me >> level, 2)
                rows = value.shape[0] // 2
                away = lax.dynamic_slice_in_dim(value, (1 - mine) * rows, rows, 0)
                value = lax.dynamic_slice_in_dim(value, mine * rows, rows, 0)
                got = swap(jnp.concatenate([away, gram], axis=0), "pix", 1 << level)
                value, gram = value + got[:rows], gram + got[rows:]
            rows = value.shape[0]
            got = swap(jnp.concatenate([value, gram], axis=0), "pix", 1 << (levels - 1))
            value = value + got[:rows]
            inverse = eliminate(gram, got[rows:])
            for level in range(levels - 2, 0, -1):
                mine = lax.rem(me >> level, 2)
                got = swap(value, "pix", 1 << level)
                low = jnp.where(mine == 0, value, got)
                high = jnp.where(mine == 0, got, value)
                value = jnp.concatenate([low, high], axis=0)
            value, inverse = lax.optimization_barrier((value, inverse))
            return inverse, value, swap(value, "pix", 1)

        def halves(inverse, panel, stacked):
            left = dot(inverse[...], panel[...], ((1,), (0,)), HIGH)
            wide = dot(inverse[...], unstack(stacked), ((1,), (0,)), HIGH)
            left_high, left_low = split(left)
            wide_high, wide_low = split(wide)
            tops = jnp.concatenate([left_high, left_low, left_high], axis=0)
            return left, (wide_high, wide_low), tops, jnp.concatenate([wide_high, wide_high, wide_low], axis=0)

        def middle(inverse, panel, stacked, o, d, before):
            adds = before is not None

            def body(inverse, panel, stacked, o, d, *rest):
                base, high, low, after = rest[adds:]
                _, right, tops, wides = halves(inverse, panel, stacked)
                for i in range(steps):
                    lowrank = dot(tops[:, chunk(i)], wides, ((0,), (0,)))
                    seen = o[chunk(i), :]
                    value = seen + d[chunk(i), :] * (1 / MU) - lowrank
                    scaled = jnp.clip(value, -TAU, TAU)
                    base[chunk(i), :] = seen + scaled
                    pair = split(seen + 2.0 * scaled - value)
                    high[chunk(i), :], low[chunk(i), :] = pair
                    term = dot_nt(right, pair)
                    after[:, chunk(i)] = rest[0][:, chunk(i)] + term if adds else term

            arrays = [inverse, panel, stacked, o, d] + [before] * adds
            outs = [((n_rows, half), F32, pltpu.VMEM)] + [((n_rows, half), BF16, pltpu.VMEM)] * 2
            outs += [((rank, n_rows), F32, pltpu.VMEM)]
            cost = (9 * rank * n_rows * n_cols, 4 * n_rows * n_cols)
            base, high, low, part = call(body, "middle", [(a, pltpu.VMEM) for a in arrays], outs, cost=cost)
            return base, (high, low), part

        def final(p, inverse, panel, stacked, base, before):
            def body(s, inverse, panel, stacked, base, *rest):
                sparse, dual, *outs, sparse_part, dual_part, left_part, sems = rest[2 * p :]
                left, _, tops, wides = halves(inverse, panel, stacked)
                moves = []
                if not p:
                    for i in range(steps):
                        left_part[:, pl.ds(gal_at(i, s), tall)] = left[:, chunk(i)]
                    moves.append(pltpu.make_async_copy(left_part, outs[0], sems.at[steps, 0]))
                    moves[0].start()
                for i in range(steps):
                    value = base[chunk(i), :] - dot(tops[:, chunk(i)], wides, ((0,), (0,)))
                    scaled = jnp.clip(value, -TAU, TAU)
                    sparse_part[chunk(i), :] = value - scaled
                    dual_part[chunk(i), :] = MU * scaled
                    for a, (source, target) in enumerate(((sparse_part, sparse), (dual_part, dual))):
                        block = target.at[pl.ds(gal_at(i, s), tall), pl.ds(pix_at(p, s), half)]
                        move = pltpu.make_async_copy(source.at[chunk(i), :], block, sems.at[i, a])
                        move.start()
                        moves.append(move)
                for move in moves:
                    move.wait()

            ins = [where] + [(a, pltpu.VMEM) for a in (inverse, panel, stacked, base)]
            outs = [((n_rows, n_cols), F32, pltpu.HBM)] * 2
            aliases = {}
            if p:
                ins += [(a, pltpu.HBM) for a in before[:2]]
                aliases = {5: 0, 6: 1}
            else:
                outs += [((rank, n_rows), F32, pltpu.HBM)]
            scratch = [pltpu.VMEM((n_rows, half), F32)] * 2 + [pltpu.VMEM((rank, n_rows), F32)]
            scratch += [pltpu.SemaphoreType.DMA((steps + 1, 2))]
            cost = (3 * rank * n_rows * n_cols, 4 * n_rows * n_cols)
            return call(body, "final", ins, outs, scratch, aliases, cost)

        def widen(inverse, own, other):
            def body(inverse, own, other, wide, out):
                gram = None
                for p, stacked in enumerate((own, other)):
                    value = dot(inverse[...], unstack(stacked), ((1,), (0,)), HIGH)
                    wide[:, half * p : half * (p + 1)] = value
                    term = dot(value, value, ((1,), (1,)), HIGH)
                    gram = term if gram is None else gram + term
                out[...] = jnp.concatenate([gram[:gram_rows], gram[gram_rows:]], axis=1)

            ins = [(a, pltpu.VMEM) for a in (inverse, own, other)]
            outs = [((rank, n_cols), F32, pltpu.VMEM), ((gram_rows, LANES), F32, pltpu.VMEM)]
            return call(body, "widen", ins, outs, cost=(10**8, MIB))

        def finish(one, two, wide):
            def body(s, one, two, wide, out, inverse, right, sem):
                invert(one[...] + two[...], inverse)
                for p in (0, 1):
                    value = wide[:, half * p : half * (p + 1)]
                    right[:, pl.ds(pix_at(p, s), half)] = dot(inverse[...], value, ((1,), (0,)), HIGH)
                move = pltpu.make_async_copy(right, out, sem)
                move.start()
                move.wait()

            ins = [where] + [(a, pltpu.VMEM) for a in (one, two, wide)]
            outs = [((rank, n_cols), F32, pltpu.HBM)]
            scratch = [pltpu.VMEM((rank, rank), F32), pltpu.VMEM((rank, n_cols), F32), pltpu.SemaphoreType.DMA(())]
            return call(body, "finish", ins, outs, scratch, cost=(10**8, 8 * MIB))[0]

        seen, pulls, own, other, part = first(right_init)
        base = [None, None]
        for step in range(ITERS):
            panel = sum_gal(part)
            send = multiply(panel, other, True)
            inverse, own_wide, other_wide = sum_pix(send, multiply(panel, own, False))
            if step < ITERS - 1:
                base[0], own, part = middle(inverse, panel, own_wide, seen[0], pulls[0], None)
                base[1], other, part = middle(inverse, panel, other_wide, seen[1], pulls[1], part)
            else:
                outs = final(0, inverse, panel, own_wide, base[0], None)
                other_wide, outs = lax.optimization_barrier((other_wide, outs))
                wide, gram = widen(inverse, own_wide, other_wide)
                bit = 1
                while 2 * bit < n_gal:
                    gram = gram + swap(gram, "gal", bit)
                    bit *= 2
                got = swap(gram, "gal", bit)
                sparse, dual = final(1, inverse, panel, other_wide, base[1], outs)
                left = outs[2]
                right = finish(gram, got, wide)
        return sparse, dual, left, right

    return jax.shard_map(
        per_device,
        mesh=mesh,
        in_specs=(P("pix", "gal"), P("pix", "gal"), P("pix", "gal"), P(None, "gal")),
        out_specs=(P("pix", "gal"), P("pix", "gal"), P(None, "pix"), P(None, "gal")),
        check_vma=False,
    )
```

```python
import jax
import jax.numpy as jnp
from jax import lax
from jax.experimental import pallas as pl
from jax.experimental.pallas import tpu as pltpu
from jax.sharding import PartitionSpec as P

ITERS = 2


MU = 1.25
TAU = 0.6 / 1.25
HIGH = lax.Precision.HIGHEST
CORES = 2
LANES = 128
F32, BF16 = jnp.float32, jnp.bfloat16
MIB = 1 << 20


def split(value):
    high = value.astype(BF16)
    return high, (value - high.astype(F32)).astype(BF16)


def dot(a, b, dims, precision=None):
    return lax.dot_general(a, b, (dims, ((), ())), precision=precision, preferred_element_type=F32)


def dot_nt(a, b):
    rows = a[0].shape[0]
    both = dot(jnp.concatenate(a, axis=0), b[0], ((1,), (1,)))
    return both[:rows] + both[rows:] + dot(a[0], b[1], ((1,), (1,)))


def dot_nn(a, b):
    rows = a[0].shape[0]
    both = dot(jnp.concatenate(a, axis=0), b[0], ((1,), (0,)))
    return both[:rows] + both[rows:] + dot(a[0], b[1], ((1,), (0,)))


def call(body, name, ins, outs, scratch=(), aliases=None, cost=(0, 0), limit=16):
    return pl.pallas_call(
        body,
        name=name,
        in_specs=[pl.BlockSpec(memory_space=space) for _, space in ins],
        out_specs=[pl.BlockSpec(memory_space=space) for _, _, space in outs],
        out_shape=[jax.ShapeDtypeStruct(shape, dtype) for shape, dtype, _ in outs],
        scratch_shapes=list(scratch),
        input_output_aliases=aliases or {},
        compiler_params=pltpu.CompilerParams(vmem_limit_bytes=limit * MIB),
        cost_estimate=pl.CostEstimate(flops=cost[0], bytes_accessed=cost[1], transcendentals=0),
    )(*[pltpu.with_memory_space_constraint(a, pltpu.HBM) if m is pltpu.HBM else a for a, m in ins])


def invert(packed, out):
    gram_rows, rank = packed.shape[0], out.shape[0]
    full = (8, LANES)
    lane = lax.broadcasted_iota(jnp.int32, full, 1)
    sub = lax.broadcasted_iota(jnp.int32, full, 0)
    turned = pltpu.roll(packed, LANES // 2, 1)
    rows = []
    for j in range(rank // 8):
        source = packed if 8 * j < gram_rows else turned
        at = 8 * j % gram_rows
        eye = jnp.where(lane - rank == sub + 8 * j, 1.0, 0.0)
        rows.append(jnp.where(lane < rank, source[at : at + 8], eye))
    wide = 4
    for k in range(0, rank, wide):
        r, at = divmod(k, 8)
        after = range(r if at + wide < 8 else r + 1, rank // 8)
        lines = [jnp.broadcast_to(rows[r][at + p : at + p + 1, :], full) for p in range(wide)]
        core = {
            (p, q): jnp.broadcast_to(lines[p][:, k + q : k + q + 1], full)
            for p in range(wide)
            for q in range(p, wide)
        }
        columns = {
            (j, p): jnp.broadcast_to(rows[j][:, k + p : k + p + 1], full) for j in after for p in range(wide)
        }
        for p in range(wide):
            inverse = 1.0 / core[p, p]
            factors = [core[p, q] * inverse for q in range(p + 1, wide)]
            for q, factor in zip(range(p + 1, wide), factors):
                for t in range(q, wide):
                    core[q, t] = core[q, t] - factor * core[p, t]
            scaled = lines[p] * inverse
            for q in range(p + 1, wide):
                lines[q] = lines[q] - core[p, q] * scaled
            for j in after:
                column = columns[j, p]
                if j == r:
                    column = jnp.where(sub >= at + wide, column, 0.0)
                rows[j] = rows[j] - column * scaled
                for q, factor in zip(range(p + 1, wide), factors):
                    columns[j, q] = columns[j, q] - factor * columns[j, p]
            done = lines[p] * lax.rsqrt(core[p, p])
            out[k + p : k + p + 1, :] = done[0:1, rank:]


def pack(gram):
    rows = gram.shape[0] // 2
    return jnp.concatenate([gram[:rows], gram[rows:]], axis=1)


def unstack(ref):
    blocks = ref.shape[0] // 64
    return jnp.concatenate([ref[64 * t : 64 * (t + 1), :] for t in range(blocks)], axis=1)


def solution(mesh):
    n_gal, n_pix = mesh.shape["gal"], mesh.shape["pix"]
    levels = n_pix.bit_length() - 1

    def swap(value, axis, bit):
        n = mesh.shape[axis]
        return lax.ppermute(value, axis, [(i, i ^ bit) for i in range(n)])

    def per_device(observed, sparse_init, dual_init, right_init):
        rank = right_init.shape[0]
        n_rows, n_cols = observed.shape
        half = n_cols // 2
        tall = min(256, n_rows // 2)
        steps = n_rows // tall
        core = lax.rem(lax.axis_index("gal"), CORES)
        bits = [lax.rem(lax.axis_index("pix") >> level, 2) for level in range(levels)]
        scalars = jnp.stack([core] + bits).astype(jnp.int32)
        stack_rows = rank * (half // LANES)
        gram_rows = rank * rank // LANES
        where = (scalars, pltpu.SMEM)

        def gal_at(i, s):
            turn = (1 - s[0]) * (steps // 2)
            return pl.multiple_of(lax.rem(i + turn, steps) * tall, tall)

        def pix_at(p, s):
            return pl.multiple_of(lax.rem(s[1] + p, 2) * half, half)

        def chunk(i):
            return slice(tall * i, tall * (i + 1))

        def join(pair):
            return jnp.concatenate([half[...] for half in pair], axis=1)

        def small(body, name, ins, rows, scratch=()):
            outs = [((n, LANES), F32, pltpu.VMEM) for n in rows]
            return call(body, name, ins, outs, scratch, cost=(10**5, 10**6), limit=4)

        def add(*arrays):
            def body(*refs):
                *ins, out = refs
                total = ins[0][...]
                for ref in ins[1:]:
                    total = total + ref[...]
                out[...] = total

            out = (arrays[0].shape, F32, pltpu.VMEM)
            return call(body, "add", [(a, pltpu.VMEM) for a in arrays], [out], cost=(10**5, 10**6), limit=4)[0]

        def first(right):
            def body(s, o_in, s_in, d_in, r_in, o, d, h0, l0, h1, l1, away, mine, sp, right, r_sem, sems):
                right_move = pltpu.make_async_copy(r_in, right, r_sem)
                right_move.start()
                moves = {}
                for i in range(steps):
                    for a, (source, target) in enumerate(((o_in, o), (s_in, sp), (d_in, d))):
                        block = source.at[pl.ds(gal_at(i, s), tall), :]
                        move = pltpu.make_async_copy(block, target.at[chunk(i), :], sems.at[i, a])
                        move.start(priority=(i + a) % 2)
                        moves[i, a] = move
                right_move.wait()
                rights = [split(right[:, pl.ds(pix_at(p, s), half)]) for p in (0, 1)]
                for i in range(steps):
                    total = None
                    for a in range(3):
                        moves[i, a].wait()
                    for p, (h, l) in enumerate(((h0, l0), (h1, l1))):
                        at = chunk(i), pl.ds(pix_at(p, s), half)
                        pair = split(o[at] - sp[at] + d[at] * (1 / MU))
                        h[chunk(i), :], l[chunk(i), :] = pair
                        term = dot_nt(rights[p], pair)
                        total = term if total is None else total + term
                    out = away if i < steps // 2 else mine
                    out[:, chunk(i % (steps // 2))] = total

            ins = [where] + [(a, pltpu.HBM) for a in (observed, sparse_init, dual_init, right)]
            outs = [((n_rows, n_cols), F32, pltpu.VMEM)] * 2 + [((n_rows, half), BF16, pltpu.VMEM)] * 4
            outs += [((rank, n_rows // 2), F32, pltpu.VMEM)] * 2
            scratch = [pltpu.VMEM((n_rows, n_cols), F32), pltpu.VMEM((rank, n_cols), F32)]
            scratch += [pltpu.SemaphoreType.DMA(()), pltpu.SemaphoreType.DMA((steps, 3))]
            cost = (6 * rank * n_rows * n_cols, 16 * n_rows * n_cols)
            got = call(body, "first", ins, outs, scratch, cost=cost)
            return got[0], got[1], got[2:4], got[4:6], got[6:8]

        def sum_gal(part):
            away, mine = part
            mine = add(mine, swap(away, "gal", 1))
            got = [
                lax.ppermute(mine, "gal", [(i, (i + CORES * k) % n_gal) for i in range(n_gal)])
                for k in range(1, n_gal // CORES)
            ]
            mine = add(mine, *got)
            return swap(mine, "gal", 1), mine

        def multiply(panel, pair, with_gram):
            def body(away, mine, high, low, out):
                panel = join((away, mine))
                total = dot_nn(split(panel), (high[...], low[...]))
                for t in range(half // LANES):
                    out[rank * t : rank * (t + 1), :] = total[:, LANES * t : LANES * (t + 1)]
                if with_gram:
                    gram = dot(panel, panel, ((1,), (1,)), HIGH)
                    out[stack_rows : stack_rows + gram_rows, :] = pack(gram)

            rows = stack_rows + (gram_rows if with_gram else 0)
            ins = [(a, pltpu.VMEM) for a in (*panel, *pair)]
            outs = [((rows, LANES), F32, pltpu.VMEM)]
            cost = (3 * rank * n_rows * n_cols, 2 * n_rows * n_cols)
            return call(body, "multiply", ins, outs, cost=cost)[0]

        def eliminate(one, two):
            def body(one, two, out):
                invert(one[-gram_rows:, :] + two[-gram_rows:, :], out)

            ins = [(one, pltpu.VMEM), (two, pltpu.VMEM)]
            outs = [((rank, rank), F32, pltpu.VMEM)]
            return call(body, "eliminate", ins, outs, cost=(10**8, 8 * MIB), limit=4)[0]

        def fold(level, value, sent, got):
            rows = value.shape[0]
            last = level == levels - 1
            keep = rows if last else rows // 2

            def body(s, value, sent, got, *outs):
                message = outs[-1]
                if last:
                    message[:rows, :] = value[...] + got[:rows, :]
                else:
                    for mine, out in ((s[1 + level], outs[0]), (1 - s[1 + level], message)):
                        at = pl.ds(pl.multiple_of(mine * keep, keep), keep)
                        out[:keep, :] = value[at, :] + got[at, :]
                message[keep:, :] = sent[rows_of(sent), :] + got[rows_of(got), :]

            def rows_of(ref):
                return slice(ref.shape[0] - gram_rows, ref.shape[0])

            ins = [where] + [(a, pltpu.VMEM) for a in (value, sent, got)]
            outs = small(body, "fold", ins, [keep + gram_rows] if last else [keep, keep + gram_rows])
            return outs[0], outs[-1]

        def unfold(level, value, got):
            rows = value.shape[0]

            def body(s, value, got, out):
                for mine, ref in ((s[1 + level], value), (1 - s[1 + level], got)):
                    out[pl.ds(pl.multiple_of(mine * rows, rows), rows), :] = ref[...]

            ins = [where, (value, pltpu.VMEM), (got, pltpu.VMEM)]
            return small(body, "unfold", ins, [2 * rows])[0]

        def top(one, two):
            rows = one.shape[0] - gram_rows

            def body(one, two, out):
                out[...] = one[:rows, :] + two[:rows, :]

            return small(body, "top", [(one, pltpu.VMEM), (two, pltpu.VMEM)], [rows])[0]

        def sum_pix(send, own):
            value, sent = own, send
            for level in range(1, levels):
                value, sent = fold(level, value, sent, swap(sent, "pix", 1 << (level - 1)))
            got = swap(sent, "pix", 1 << (levels - 1))
            value = top(sent, got)
            inverse = eliminate(sent, got)
            for level in range(levels - 2, 0, -1):
                value = unfold(level, value, swap(value, "pix", 1 << level))
            value, inverse = lax.optimization_barrier((value, inverse))
            return inverse, value, swap(value, "pix", 1)

        def halves(inverse, panel, stacked):
            left = dot(inverse[...], join(panel), ((1,), (0,)), HIGH)
            wide = dot(inverse[...], unstack(stacked), ((1,), (0,)), HIGH)
            left_high, left_low = split(left)
            wide_high, wide_low = split(wide)
            tops = jnp.concatenate([left_high, left_low, left_high], axis=0)
            return left, wide, (wide_high, wide_low), tops, jnp.concatenate([wide_high, wide_high, wide_low], axis=0)

        def middle(p, inverse, panel, stacked, o, d, before):
            def body(s, inverse, away, mine, stacked, o, d, *rest):
                base, high, low, *after = rest[2 * p :]
                _, _, right, tops, wides = halves(inverse, (away, mine), stacked)
                for i in range(steps):
                    lowrank = dot(tops[:, chunk(i)], wides, ((0,), (0,)))
                    at = chunk(i), pl.ds(pix_at(p, s), half)
                    seen = o[at]
                    value = seen + d[at] * (1 / MU) - lowrank
                    scaled = jnp.clip(value, -TAU, TAU)
                    base[chunk(i), :] = seen + scaled
                    pair = split(seen + 2.0 * scaled - value)
                    high[chunk(i), :], low[chunk(i), :] = pair
                    term = dot_nt(right, pair)
                    side, block = divmod(i, steps // 2)
                    after[side][:, chunk(block)] = rest[side][:, chunk(block)] + term if p else term

            arrays = [inverse, *panel, stacked, o, d] + (list(before) if p else [])
            outs = [((n_rows, half), F32, pltpu.VMEM)] + [((n_rows, half), BF16, pltpu.VMEM)] * 2
            outs += [((rank, n_rows // 2), F32, pltpu.VMEM)] * 2
            cost = (9 * rank * n_rows * n_cols, 4 * n_rows * n_cols)
            ins = [where] + [(a, pltpu.VMEM) for a in arrays]
            base, high, low, *part = call(body, "middle", ins, outs, cost=cost)
            return base, (high, low), part

        def final(p, inverse, panel, stacked, base, before):
            def body(s, inverse, away, mine, stacked, base, *rest):
                sparse, dual, *outs, sparse_part, dual_part, left_part, sems = rest[2 * p :]
                left, wide, _, tops, wides = halves(inverse, (away, mine), stacked)
                moves = []
                if not p:
                    outs[1][...] = wide
                    outs[2][...] = pack(dot(wide, wide, ((1,), (1,)), HIGH))
                    for i in range(steps):
                        left_part[:, pl.ds(gal_at(i, s), tall)] = left[:, chunk(i)]
                    moves.append(pltpu.make_async_copy(left_part, outs[0], sems.at[steps, 0]))
                    moves[0].start()
                for i in range(steps):
                    value = base[chunk(i), :] - dot(tops[:, chunk(i)], wides, ((0,), (0,)))
                    scaled = jnp.clip(value, -TAU, TAU)
                    sparse_part[chunk(i), :] = value - scaled
                    dual_part[chunk(i), :] = MU * scaled
                    for a, (source, target) in enumerate(((sparse_part, sparse), (dual_part, dual))):
                        block = target.at[pl.ds(gal_at(i, s), tall), pl.ds(pix_at(p, s), half)]
                        move = pltpu.make_async_copy(source.at[chunk(i), :], block, sems.at[i, a])
                        move.start(priority=(i + a) % 2)
                        moves.append(move)
                for move in moves:
                    move.wait()

            ins = [where] + [(a, pltpu.VMEM) for a in (inverse, *panel, stacked, base)]
            outs = [((n_rows, n_cols), F32, pltpu.HBM)] * 2
            aliases = {}
            if p:
                ins += [(a, pltpu.HBM) for a in before[:2]]
                aliases = {6: 0, 7: 1}
            else:
                outs += [((rank, n_rows), F32, pltpu.HBM), ((rank, half), F32, pltpu.VMEM)]
                outs += [((gram_rows, LANES), F32, pltpu.VMEM)]
            scratch = [pltpu.VMEM((n_rows, half), F32)] * 2 + [pltpu.VMEM((rank, n_rows), F32)]
            scratch += [pltpu.SemaphoreType.DMA((steps + 1, 2))]
            cost = (3 * rank * n_rows * n_cols, 4 * n_rows * n_cols)
            return call(body, "final", ins, outs, scratch, aliases, cost)

        def widen(inverse, other, gram):
            def body(inverse, stacked, gram, wide, out):
                wide[...] = dot(inverse[...], unstack(stacked), ((1,), (0,)), HIGH)
                out[...] = gram[...] + pack(dot(wide[...], wide[...], ((1,), (1,)), HIGH))

            ins = [(a, pltpu.VMEM) for a in (inverse, other, gram)]
            outs = [((rank, half), F32, pltpu.VMEM), ((gram_rows, LANES), F32, pltpu.VMEM)]
            return call(body, "widen", ins, outs, cost=(10**8, MIB), limit=8)

        def finish(one, two, wide):
            def body(s, one, two, own, other, out, inverse, right, sem):
                invert(one[...] + two[...], inverse)
                for p, value in enumerate((own, other)):
                    right[:, pl.ds(pix_at(p, s), half)] = dot(inverse[...], value[...], ((1,), (0,)), HIGH)
                move = pltpu.make_async_copy(right, out, sem)
                move.start()
                move.wait()

            ins = [where] + [(a, pltpu.VMEM) for a in (one, two, *wide)]
            outs = [((rank, n_cols), F32, pltpu.HBM)]
            scratch = [pltpu.VMEM((rank, rank), F32), pltpu.VMEM((rank, n_cols), F32), pltpu.SemaphoreType.DMA(())]
            return call(body, "finish", ins, outs, scratch, cost=(10**8, 8 * MIB))[0]

        seen, pulls, own, other, part = first(right_init)
        base = [None, None]
        for step in range(ITERS):
            panel = sum_gal(part)
            send = multiply(panel, other, True)
            inverse, own_wide, other_wide = sum_pix(send, multiply(panel, own, False))
            if step < ITERS - 1:
                base[0], own, part = middle(0, inverse, panel, own_wide, seen, pulls, None)
                base[1], other, part = middle(1, inverse, panel, other_wide, seen, pulls, part)
            else:
                outs = final(0, inverse, panel, own_wide, base[0], None)
                other_wide, outs = lax.optimization_barrier((other_wide, outs))
                wide, gram = widen(inverse, other_wide, outs[4])
                bit = 1
                while 2 * bit < n_gal:
                    gram = add(gram, swap(gram, "gal", bit))
                    bit *= 2
                got = swap(gram, "gal", bit)
                sparse, dual = final(1, inverse, panel, other_wide, base[1], outs)
                left = outs[2]
                right = finish(gram, got, (outs[3], wide))
        return sparse, dual, left, right

    return jax.shard_map(
        per_device,
        mesh=mesh,
        in_specs=(P("pix", "gal"), P("pix", "gal"), P("pix", "gal"), P(None, "gal")),
        out_specs=(P("pix", "gal"), P("pix", "gal"), P(None, "pix"), P(None, "gal")),
        check_vma=False,
    )
```

```python
import jax
import jax.numpy as jnp
from jax import lax
from jax.experimental import pallas as pl
from jax.experimental.pallas import tpu as pltpu
from jax.sharding import PartitionSpec as P

ITERS = 2


MU = 1.25
TAU = 0.6 / 1.25
HIGH = lax.Precision.HIGHEST
CORES = 2
LANES = 128
F32, BF16 = jnp.float32, jnp.bfloat16
MIB = 1 << 20


def split(value):
    high = value.astype(BF16)
    return high, (value - high.astype(F32)).astype(BF16)


def dot(a, b, dims, precision=None):
    return lax.dot_general(a, b, (dims, ((), ())), precision=precision, preferred_element_type=F32)


def dot_nt(a, b):
    rows = a[0].shape[0]
    both = dot(jnp.concatenate(a, axis=0), b[0], ((1,), (1,)))
    return both[:rows] + both[rows:] + dot(a[0], b[1], ((1,), (1,)))


def dot_nn(a, b):
    rows = a[0].shape[0]
    both = dot(jnp.concatenate(a, axis=0), b[0], ((1,), (0,)))
    return both[:rows] + both[rows:] + dot(a[0], b[1], ((1,), (0,)))


def call(body, name, ins, outs, scratch=(), aliases=None, cost=(0, 0), limit=16):
    return pl.pallas_call(
        body,
        name=name,
        in_specs=[pl.BlockSpec(memory_space=space) for _, space in ins],
        out_specs=[pl.BlockSpec(memory_space=space) for _, _, space in outs],
        out_shape=[jax.ShapeDtypeStruct(shape, dtype) for shape, dtype, _ in outs],
        scratch_shapes=list(scratch),
        input_output_aliases=aliases or {},
        compiler_params=pltpu.CompilerParams(vmem_limit_bytes=limit * MIB),
        cost_estimate=pl.CostEstimate(flops=cost[0], bytes_accessed=cost[1], transcendentals=0),
    )(*[pltpu.with_memory_space_constraint(a, pltpu.HBM) if m is pltpu.HBM else a for a, m in ins])


def invert(packed, out):
    gram_rows, rank = packed.shape[0], out.shape[0]
    full = (8, LANES)
    lane = lax.broadcasted_iota(jnp.int32, full, 1)
    sub = lax.broadcasted_iota(jnp.int32, full, 0)
    turned = pltpu.roll(packed, LANES // 2, 1)
    rows = []
    for j in range(rank // 8):
        source = packed if 8 * j < gram_rows else turned
        at = 8 * j % gram_rows
        eye = jnp.where(lane - rank == sub + 8 * j, 1.0, 0.0)
        rows.append(jnp.where(lane < rank, source[at : at + 8], eye))
    wide = 4
    for k in range(0, rank, wide):
        r, at = divmod(k, 8)
        after = range(r if at + wide < 8 else r + 1, rank // 8)
        lines = [jnp.broadcast_to(rows[r][at + p : at + p + 1, :], full) for p in range(wide)]
        core = {
            (p, q): jnp.broadcast_to(lines[p][:, k + q : k + q + 1], full)
            for p in range(wide)
            for q in range(p, wide)
        }
        columns = {
            (j, p): jnp.broadcast_to(rows[j][:, k + p : k + p + 1], full) for j in after for p in range(wide)
        }
        for p in range(wide):
            inverse = 1.0 / core[p, p]
            factors = [core[p, q] * inverse for q in range(p + 1, wide)]
            for q, factor in zip(range(p + 1, wide), factors):
                for t in range(q, wide):
                    core[q, t] = core[q, t] - factor * core[p, t]
            scaled = lines[p] * inverse
            for q in range(p + 1, wide):
                lines[q] = lines[q] - core[p, q] * scaled
            for j in after:
                column = columns[j, p]
                if j == r:
                    column = jnp.where(sub >= at + wide, column, 0.0)
                rows[j] = rows[j] - column * scaled
                for q, factor in zip(range(p + 1, wide), factors):
                    columns[j, q] = columns[j, q] - factor * columns[j, p]
            done = lines[p] * lax.rsqrt(core[p, p])
            out[k + p : k + p + 1, :] = done[0:1, rank:]


def pack(gram):
    rows = gram.shape[0] // 2
    return jnp.concatenate([gram[:rows], gram[rows:]], axis=1)


def unstack(ref):
    blocks = ref.shape[0] // 64
    return jnp.concatenate([ref[64 * t : 64 * (t + 1), :] for t in range(blocks)], axis=1)


def solution(mesh):
    n_gal, n_pix = mesh.shape["gal"], mesh.shape["pix"]
    levels = n_pix.bit_length() - 1

    def swap(value, axis, bit):
        n = mesh.shape[axis]
        return lax.ppermute(value, axis, [(i, i ^ bit) for i in range(n)])

    def per_device(observed, sparse_init, dual_init, right_init):
        rank = right_init.shape[0]
        n_rows, n_cols = observed.shape
        half = n_cols // 2
        tall = min(256, n_rows // 2)
        steps = n_rows // tall
        stack_rows = rank * (half // LANES)
        gram_rows = rank * rank // LANES

        def place():
            pix = lax.axis_index("pix")
            return [lax.rem(lax.axis_index("gal"), CORES)] + [lax.rem(pix >> level, 2) for level in range(levels)]

        def gal_at(i, s):
            turn = (1 - s[0]) * (steps // 2)
            return pl.multiple_of(lax.rem(i + turn, steps) * tall, tall)

        def pix_at(p, s):
            return pl.multiple_of(lax.rem(s[1] + p, 2) * half, half)

        def chunk(i):
            return slice(tall * i, tall * (i + 1))

        def join(pair):
            return jnp.concatenate([half[...] for half in pair], axis=1)

        def small(body, name, ins, rows, scratch=()):
            outs = [((n, LANES), F32, pltpu.VMEM) for n in rows]
            return call(body, name, ins, outs, scratch, cost=(10**5, 10**6), limit=4)

        def add(*arrays):
            def body(*refs):
                *ins, out = refs
                total = ins[0][...]
                for ref in ins[1:]:
                    total = total + ref[...]
                out[...] = total

            out = (arrays[0].shape, F32, pltpu.VMEM)
            return call(body, "add", [(a, pltpu.VMEM) for a in arrays], [out], cost=(10**5, 10**6), limit=4)[0]

        def first(right):
            def body(o_in, s_in, d_in, r_in, o, d, h0, l0, h1, l1, away, mine, sp, right, r_sem, sems):
                s = place()
                right_move = pltpu.make_async_copy(r_in, right, r_sem)
                right_move.start()
                moves = {}
                for i in range(steps):
                    for a, (source, target) in enumerate(((o_in, o), (s_in, sp), (d_in, d))):
                        block = source.at[pl.ds(gal_at(i, s), tall), :]
                        move = pltpu.make_async_copy(block, target.at[chunk(i), :], sems.at[i, a])
                        move.start(priority=(i + a) % 2)
                        moves[i, a] = move
                right_move.wait()
                rights = [split(right[:, pl.ds(pix_at(p, s), half)]) for p in (0, 1)]
                for i in range(steps):
                    total = None
                    for a in range(3):
                        moves[i, a].wait()
                    for p, (h, l) in enumerate(((h0, l0), (h1, l1))):
                        at = chunk(i), pl.ds(pix_at(p, s), half)
                        pair = split(o[at] - sp[at] + d[at] * (1 / MU))
                        h[chunk(i), :], l[chunk(i), :] = pair
                        term = dot_nt(rights[p], pair)
                        total = term if total is None else total + term
                    out = away if i < steps // 2 else mine
                    out[:, chunk(i % (steps // 2))] = total

            ins = [(a, pltpu.HBM) for a in (observed, sparse_init, dual_init, right)]
            outs = [((n_rows, n_cols), F32, pltpu.VMEM)] * 2 + [((n_rows, half), BF16, pltpu.VMEM)] * 4
            outs += [((rank, n_rows // 2), F32, pltpu.VMEM)] * 2
            scratch = [pltpu.VMEM((n_rows, n_cols), F32), pltpu.VMEM((rank, n_cols), F32)]
            scratch += [pltpu.SemaphoreType.DMA(()), pltpu.SemaphoreType.DMA((steps, 3))]
            cost = (6 * rank * n_rows * n_cols, 16 * n_rows * n_cols)
            got = call(body, "first", ins, outs, scratch, cost=cost)
            return got[0], got[1], got[2:4], got[4:6], got[6:8]

        def sum_gal(part):
            away, mine = part
            mine = add(mine, swap(away, "gal", 1))
            got = [
                lax.ppermute(mine, "gal", [(i, (i + CORES * k) % n_gal) for i in range(n_gal)])
                for k in range(1, n_gal // CORES)
            ]
            mine = add(mine, *got)
            return swap(mine, "gal", 1), mine

        def multiply(panel, pair, with_gram):
            def body(away, mine, high, low, out):
                panel = join((away, mine))
                total = dot_nn(split(panel), (high[...], low[...]))
                for t in range(half // LANES):
                    out[rank * t : rank * (t + 1), :] = total[:, LANES * t : LANES * (t + 1)]
                if with_gram:
                    gram = dot(panel, panel, ((1,), (1,)), HIGH)
                    out[stack_rows : stack_rows + gram_rows, :] = pack(gram)

            rows = stack_rows + (gram_rows if with_gram else 0)
            ins = [(a, pltpu.VMEM) for a in (*panel, *pair)]
            outs = [((rows, LANES), F32, pltpu.VMEM)]
            cost = (3 * rank * n_rows * n_cols, 2 * n_rows * n_cols)
            return call(body, "multiply", ins, outs, cost=cost)[0]

        def eliminate(one, two):
            def body(one, two, out):
                invert(one[-gram_rows:, :] + two[-gram_rows:, :], out)

            ins = [(one, pltpu.VMEM), (two, pltpu.VMEM)]
            outs = [((rank, rank), F32, pltpu.VMEM)]
            return call(body, "eliminate", ins, outs, cost=(10**8, 8 * MIB), limit=4)[0]

        def fold(level, value, sent, got):
            rows = value.shape[0]
            last = level == levels - 1
            keep = rows if last else rows // 2

            def body(value, sent, got, *outs):
                s = place()
                message = outs[-1]
                if last:
                    message[:rows, :] = value[...] + got[:rows, :]
                else:
                    for mine, out in ((s[1 + level], outs[0]), (1 - s[1 + level], message)):
                        at = pl.ds(pl.multiple_of(mine * keep, keep), keep)
                        out[:keep, :] = value[at, :] + got[at, :]
                message[keep:, :] = sent[rows_of(sent), :] + got[rows_of(got), :]

            def rows_of(ref):
                return slice(ref.shape[0] - gram_rows, ref.shape[0])

            ins = [(a, pltpu.VMEM) for a in (value, sent, got)]
            outs = small(body, "fold", ins, [keep + gram_rows] if last else [keep, keep + gram_rows])
            return outs[0], outs[-1]

        def unfold(level, value, got):
            rows = value.shape[0]

            def body(value, got, out):
                s = place()
                for mine, ref in ((s[1 + level], value), (1 - s[1 + level], got)):
                    out[pl.ds(pl.multiple_of(mine * rows, rows), rows), :] = ref[...]

            ins = [(value, pltpu.VMEM), (got, pltpu.VMEM)]
            return small(body, "unfold", ins, [2 * rows])[0]

        def top(one, two):
            rows = one.shape[0] - gram_rows

            def body(one, two, out):
                out[...] = one[:rows, :] + two[:rows, :]

            return small(body, "top", [(one, pltpu.VMEM), (two, pltpu.VMEM)], [rows])[0]

        def sum_pix(send, own):
            value, sent = own, send
            for level in range(1, levels):
                value, sent = fold(level, value, sent, swap(sent, "pix", 1 << (level - 1)))
            got = swap(sent, "pix", 1 << (levels - 1))
            value = top(sent, got)
            inverse = eliminate(sent, got)
            for level in range(levels - 2, 0, -1):
                value = unfold(level, value, swap(value, "pix", 1 << level))
            value, inverse = lax.optimization_barrier((value, inverse))
            return inverse, value, swap(value, "pix", 1)

        def halves(inverse, panel, stacked):
            left = dot(inverse[...], join(panel), ((1,), (0,)), HIGH)
            wide = dot(inverse[...], unstack(stacked), ((1,), (0,)), HIGH)
            left_high, left_low = split(left)
            wide_high, wide_low = split(wide)
            tops = jnp.concatenate([left_high, left_low, left_high], axis=0)
            return left, wide, (wide_high, wide_low), tops, jnp.concatenate([wide_high, wide_high, wide_low], axis=0)

        def middle(p, inverse, panel, stacked, o, d, before):
            def body(inverse, away, mine, stacked, o, d, *rest):
                s = place()
                base, high, low, *after = rest[2 * p :]
                _, _, right, tops, wides = halves(inverse, (away, mine), stacked)
                for i in range(steps):
                    lowrank = dot(tops[:, chunk(i)], wides, ((0,), (0,)))
                    at = chunk(i), pl.ds(pix_at(p, s), half)
                    seen = o[at]
                    value = seen + d[at] * (1 / MU) - lowrank
                    scaled = jnp.clip(value, -TAU, TAU)
                    base[chunk(i), :] = seen + scaled
                    pair = split(seen + 2.0 * scaled - value)
                    high[chunk(i), :], low[chunk(i), :] = pair
                    term = dot_nt(right, pair)
                    side, block = divmod(i, steps // 2)
                    after[side][:, chunk(block)] = rest[side][:, chunk(block)] + term if p else term

            arrays = [inverse, *panel, stacked, o, d] + (list(before) if p else [])
            outs = [((n_rows, half), F32, pltpu.VMEM)] + [((n_rows, half), BF16, pltpu.VMEM)] * 2
            outs += [((rank, n_rows // 2), F32, pltpu.VMEM)] * 2
            cost = (9 * rank * n_rows * n_cols, 4 * n_rows * n_cols)
            ins = [(a, pltpu.VMEM) for a in arrays]
            base, high, low, *part = call(body, "middle", ins, outs, cost=cost)
            return base, (high, low), part

        def final(p, inverse, panel, stacked, base, before):
            def body(inverse, away, mine, stacked, base, *rest):
                s = place()
                sparse, dual, *outs, sparse_part, dual_part, left_part, sems = rest[2 * p :]
                left, wide, _, tops, wides = halves(inverse, (away, mine), stacked)
                moves = []
                if not p:
                    outs[1][...] = wide
                    outs[2][...] = pack(dot(wide, wide, ((1,), (1,)), HIGH))
                    for i in range(steps):
                        left_part[:, pl.ds(gal_at(i, s), tall)] = left[:, chunk(i)]
                    moves.append(pltpu.make_async_copy(left_part, outs[0], sems.at[steps, 0]))
                    moves[0].start()
                for i in range(steps):
                    value = base[chunk(i), :] - dot(tops[:, chunk(i)], wides, ((0,), (0,)))
                    scaled = jnp.clip(value, -TAU, TAU)
                    sparse_part[chunk(i), :] = value - scaled
                    dual_part[chunk(i), :] = MU * scaled
                    for a, (source, target) in enumerate(((sparse_part, sparse), (dual_part, dual))):
                        block = target.at[pl.ds(gal_at(i, s), tall), pl.ds(pix_at(p, s), half)]
                        move = pltpu.make_async_copy(source.at[chunk(i), :], block, sems.at[i, a])
                        move.start(priority=(i + a) % 2)
                        moves.append(move)
                for move in moves:
                    move.wait()

            ins = [(a, pltpu.VMEM) for a in (inverse, *panel, stacked, base)]
            outs = [((n_rows, n_cols), F32, pltpu.HBM)] * 2
            aliases = {}
            if p:
                ins += [(a, pltpu.HBM) for a in before[:2]]
                aliases = {5: 0, 6: 1}
            else:
                outs += [((rank, n_rows), F32, pltpu.HBM), ((rank, half), F32, pltpu.VMEM)]
                outs += [((gram_rows, LANES), F32, pltpu.VMEM)]
            scratch = [pltpu.VMEM((n_rows, half), F32)] * 2 + [pltpu.VMEM((rank, n_rows), F32)]
            scratch += [pltpu.SemaphoreType.DMA((steps + 1, 2))]
            cost = (3 * rank * n_rows * n_cols, 4 * n_rows * n_cols)
            return call(body, "final", ins, outs, scratch, aliases, cost)

        def widen(inverse, other, gram):
            def body(inverse, stacked, gram, wide, out):
                wide[...] = dot(inverse[...], unstack(stacked), ((1,), (0,)), HIGH)
                out[...] = gram[...] + pack(dot(wide[...], wide[...], ((1,), (1,)), HIGH))

            ins = [(a, pltpu.VMEM) for a in (inverse, other, gram)]
            outs = [((rank, half), F32, pltpu.VMEM), ((gram_rows, LANES), F32, pltpu.VMEM)]
            return call(body, "widen", ins, outs, cost=(10**8, MIB), limit=8)

        def finish(one, two, wide):
            def body(one, two, own, other, out, inverse, right, sem):
                s = place()
                invert(one[...] + two[...], inverse)
                for p, value in enumerate((own, other)):
                    right[:, pl.ds(pix_at(p, s), half)] = dot(inverse[...], value[...], ((1,), (0,)), HIGH)
                move = pltpu.make_async_copy(right, out, sem)
                move.start()
                move.wait()

            ins = [(a, pltpu.VMEM) for a in (one, two, *wide)]
            outs = [((rank, n_cols), F32, pltpu.HBM)]
            scratch = [pltpu.VMEM((rank, rank), F32), pltpu.VMEM((rank, n_cols), F32), pltpu.SemaphoreType.DMA(())]
            return call(body, "finish", ins, outs, scratch, cost=(10**8, 8 * MIB))[0]

        seen, pulls, own, other, part = first(right_init)
        base = [None, None]
        for step in range(ITERS):
            panel = sum_gal(part)
            send = multiply(panel, other, True)
            inverse, own_wide, other_wide = sum_pix(send, multiply(panel, own, False))
            if step < ITERS - 1:
                base[0], own, part = middle(0, inverse, panel, own_wide, seen, pulls, None)
                base[1], other, part = middle(1, inverse, panel, other_wide, seen, pulls, part)
            else:
                outs = final(0, inverse, panel, own_wide, base[0], None)
                other_wide, outs = lax.optimization_barrier((other_wide, outs))
                wide, gram = widen(inverse, other_wide, outs[4])
                bit = 1
                while 2 * bit < n_gal:
                    gram = add(gram, swap(gram, "gal", bit))
                    bit *= 2
                got = swap(gram, "gal", bit)
                sparse, dual = final(1, inverse, panel, other_wide, base[1], outs)
                left = outs[2]
                right = finish(gram, got, (outs[3], wide))
        return sparse, dual, left, right

    return jax.shard_map(
        per_device,
        mesh=mesh,
        in_specs=(P("pix", "gal"), P("pix", "gal"), P("pix", "gal"), P(None, "gal")),
        out_specs=(P("pix", "gal"), P("pix", "gal"), P(None, "pix"), P(None, "gal")),
        check_vma=False,
    )
```

```python
import jax
import jax.numpy as jnp
from jax import lax
from jax.experimental import pallas as pl
from jax.experimental.pallas import tpu as pltpu
from jax.sharding import PartitionSpec as P

ITERS = 2


MU = 1.25
TAU = 0.6 / 1.25
HIGH = lax.Precision.HIGHEST
CORES = 2
STREAMS = 2
LANES = 128
F32, BF16 = jnp.float32, jnp.bfloat16
MIB = 1 << 20


def split(value):
    high = value.astype(BF16)
    return high, (value - high.astype(F32)).astype(BF16)


def dot(a, b, dims, precision=None):
    return lax.dot_general(a, b, (dims, ((), ())), precision=precision, preferred_element_type=F32)


def dot_nt(a, b):
    rows = a[0].shape[0]
    both = dot(jnp.concatenate(a, axis=0), b[0], ((1,), (1,)))
    return both[:rows] + both[rows:] + dot(a[0], b[1], ((1,), (1,)))


def dot_nn(a, b):
    rows = a[0].shape[0]
    both = dot(jnp.concatenate(a, axis=0), b[0], ((1,), (0,)))
    return both[:rows] + both[rows:] + dot(a[0], b[1], ((1,), (0,)))


def call(body, name, ins, outs, scratch=(), aliases=None, cost=(0, 0), limit=16):
    return pl.pallas_call(
        body,
        name=name,
        in_specs=[pl.BlockSpec(memory_space=space) for _, space in ins],
        out_specs=[pl.BlockSpec(memory_space=space) for _, _, space in outs],
        out_shape=[jax.ShapeDtypeStruct(shape, dtype) for shape, dtype, _ in outs],
        scratch_shapes=list(scratch),
        input_output_aliases=aliases or {},
        compiler_params=pltpu.CompilerParams(vmem_limit_bytes=limit * MIB),
        cost_estimate=pl.CostEstimate(flops=cost[0], bytes_accessed=cost[1], transcendentals=0),
    )(*[pltpu.with_memory_space_constraint(a, pltpu.HBM) if m is pltpu.HBM else a for a, m in ins])


def invert(packed, out):
    gram_rows, rank = packed.shape[0], out.shape[0]
    full = (8, LANES)
    lane = lax.broadcasted_iota(jnp.int32, full, 1)
    sub = lax.broadcasted_iota(jnp.int32, full, 0)
    turned = pltpu.roll(packed, LANES // 2, 1)
    rows = []
    for j in range(rank // 8):
        source = packed if 8 * j < gram_rows else turned
        at = 8 * j % gram_rows
        eye = jnp.where(lane - rank == sub + 8 * j, 1.0, 0.0)
        rows.append(jnp.where(lane < rank, source[at : at + 8], eye))
    wide = 4
    for k in range(0, rank, wide):
        r, at = divmod(k, 8)
        after = range(r if at + wide < 8 else r + 1, rank // 8)
        lines = [jnp.broadcast_to(rows[r][at + p : at + p + 1, :], full) for p in range(wide)]
        core = {
            (p, q): jnp.broadcast_to(lines[p][:, k + q : k + q + 1], full)
            for p in range(wide)
            for q in range(p, wide)
        }
        columns = {
            (j, p): jnp.broadcast_to(rows[j][:, k + p : k + p + 1], full) for j in after for p in range(wide)
        }
        for p in range(wide):
            inverse = 1.0 / core[p, p]
            factors = [core[p, q] * inverse for q in range(p + 1, wide)]
            for q, factor in zip(range(p + 1, wide), factors):
                for t in range(q, wide):
                    core[q, t] = core[q, t] - factor * core[p, t]
            scaled = lines[p] * inverse
            for q in range(p + 1, wide):
                lines[q] = lines[q] - core[p, q] * scaled
            for j in after:
                column = columns[j, p]
                if j == r:
                    column = jnp.where(sub >= at + wide, column, 0.0)
                rows[j] = rows[j] - column * scaled
                for q, factor in zip(range(p + 1, wide), factors):
                    columns[j, q] = columns[j, q] - factor * columns[j, p]
            done = lines[p] * lax.rsqrt(core[p, p])
            out[k + p : k + p + 1, :] = done[0:1, rank:]


def pack(gram):
    rows = gram.shape[0] // 2
    return jnp.concatenate([gram[:rows], gram[rows:]], axis=1)


def unstack(ref, rank):
    part, rows = rank // STREAMS, ref.shape[0] // STREAMS
    parts = []
    for at in range(0, STREAMS * rows, rows):
        blocks = [ref[at + t : at + t + part, :] for t in range(0, rows, part)]
        parts.append(jnp.concatenate(blocks, axis=1))
    return jnp.concatenate(parts, axis=0)


def solution(mesh):
    n_gal, n_pix = mesh.shape["gal"], mesh.shape["pix"]
    levels = n_pix.bit_length() - 1

    def swap(value, axis, bit):
        n = mesh.shape[axis]
        return lax.ppermute(value, axis, [(i, i ^ bit) for i in range(n)])

    def per_device(observed, sparse_init, dual_init, right_init):
        rank = right_init.shape[0]
        n_rows, n_cols = observed.shape
        half = n_cols // 2
        tall = min(256, n_rows // 2)
        steps = n_rows // tall
        part_rank = rank // STREAMS
        part_rows = part_rank * (half // LANES)
        gram_rows = rank * rank // LANES

        def place():
            pix = lax.axis_index("pix")
            return [lax.rem(lax.axis_index("gal"), CORES)] + [lax.rem(pix >> level, 2) for level in range(levels)]

        def gal_at(i, s):
            turn = (1 - s[0]) * (steps // 2)
            return pl.multiple_of(lax.rem(i + turn, steps) * tall, tall)

        def pix_at(p, s):
            return pl.multiple_of(lax.rem(s[1] + p, 2) * half, half)

        def chunk(i):
            return slice(tall * i, tall * (i + 1))

        def join(pair):
            rows = [jnp.concatenate([pair[at][...], pair[at + 1][...]], axis=1) for at in range(0, len(pair), 2)]
            return jnp.concatenate(rows, axis=0)

        def part_of(k):
            return slice(part_rank * k, part_rank * (k + 1))

        def small(body, name, ins, rows, scratch=()):
            outs = [((n, LANES), F32, pltpu.VMEM) for n in rows]
            return call(body, name, ins, outs, scratch, cost=(10**5, 10**6), limit=4)

        def add(*arrays):
            def body(*refs):
                *ins, out = refs
                total = ins[0][...]
                for ref in ins[1:]:
                    total = total + ref[...]
                out[...] = total

            out = (arrays[0].shape, F32, pltpu.VMEM)
            return call(body, "add", [(a, pltpu.VMEM) for a in arrays], [out], cost=(10**5, 10**6), limit=4)[0]

        def first(right):
            def body(o_in, s_in, d_in, r_in, o, d, h0, l0, h1, l1, *rest):
                s = place()
                *parts, sp, right, r_sem, sems = rest
                right_move = pltpu.make_async_copy(r_in, right, r_sem)
                right_move.start()
                moves = {}
                for i in range(steps):
                    for a, (source, target) in enumerate(((o_in, o), (s_in, sp), (d_in, d))):
                        block = source.at[pl.ds(gal_at(i, s), tall), :]
                        move = pltpu.make_async_copy(block, target.at[chunk(i), :], sems.at[i, a])
                        move.start(priority=(i + a) % 2)
                        moves[i, a] = move
                right_move.wait()
                rights = [split(right[:, pl.ds(pix_at(p, s), half)]) for p in (0, 1)]
                for i in range(steps):
                    total = None
                    for a in range(3):
                        moves[i, a].wait()
                    for p, (h, l) in enumerate(((h0, l0), (h1, l1))):
                        at = chunk(i), pl.ds(pix_at(p, s), half)
                        pair = split(o[at] - sp[at] + d[at] * (1 / MU))
                        h[chunk(i), :], l[chunk(i), :] = pair
                        term = dot_nt(rights[p], pair)
                        total = term if total is None else total + term
                    side, block = divmod(i, steps // 2)
                    for k in range(STREAMS):
                        parts[2 * k + side][:, chunk(block)] = total[part_of(k)]

            ins = [(a, pltpu.HBM) for a in (observed, sparse_init, dual_init, right)]
            outs = [((n_rows, n_cols), F32, pltpu.VMEM)] * 2 + [((n_rows, half), BF16, pltpu.VMEM)] * 4
            outs += [((part_rank, n_rows // 2), F32, pltpu.VMEM)] * (2 * STREAMS)
            scratch = [pltpu.VMEM((n_rows, n_cols), F32), pltpu.VMEM((rank, n_cols), F32)]
            scratch += [pltpu.SemaphoreType.DMA(()), pltpu.SemaphoreType.DMA((steps, 3))]
            cost = (6 * rank * n_rows * n_cols, 16 * n_rows * n_cols)
            got = call(body, "first", ins, outs, scratch, cost=cost)
            return got[0], got[1], got[2:4], got[4:6], got[6:]

        def sum_gal(part):
            if len(part) > 2:
                return *sum_gal(part[:2]), *sum_gal(part[2:])
            away, mine = part
            mine = add(mine, swap(away, "gal", 1))
            got = [
                lax.ppermute(mine, "gal", [(i, (i + CORES * k) % n_gal) for i in range(n_gal)])
                for k in range(1, n_gal // CORES)
            ]
            mine = add(mine, *got)
            return swap(mine, "gal", 1), mine

        def multiply(panel, pair, streams, gram_too, after=()):
            def body(*refs):
                *parts, high, low = refs[: len(panel) + 2]
                outs = refs[len(panel) + 2 + len(after) :]
                total = dot_nn(split(join(parts[-2 * streams :])), (high[...], low[...]))
                for k, out in enumerate(outs):
                    for t in range(half // LANES):
                        out[part_of(t), :] = total[part_of(k), LANES * t : LANES * (t + 1)]
                if gram_too:
                    whole = join(parts)
                    outs[-1][part_rows:, :] = pack(dot(whole, whole, ((1,), (1,)), HIGH))

            ins = [(a, pltpu.VMEM) for a in (*panel, *pair, *after)]
            outs = [((part_rows, LANES), F32, pltpu.VMEM)] * streams
            if gram_too:
                outs[-1] = ((part_rows + gram_rows, LANES), F32, pltpu.VMEM)
            cost = (3 * rank * n_rows * n_cols, 2 * n_rows * n_cols)
            return call(body, "multiply", ins, outs, cost=cost)

        def eliminate(one, two):
            def body(one, two, out):
                invert(one[-gram_rows:, :] + two[-gram_rows:, :], out)

            ins = [(one, pltpu.VMEM), (two, pltpu.VMEM)]
            outs = [((rank, rank), F32, pltpu.VMEM)]
            return call(body, "eliminate", ins, outs, cost=(10**8, 8 * MIB), limit=4)[0]

        def fold(level, value, sent, got):
            rows = value.shape[0]
            extra = sent.shape[0] - got_rows(level)
            last = level == levels - 1
            keep = rows if last else rows // 2

            def body(value, sent, got, *outs):
                s = place()
                message = outs[-1]
                if last:
                    message[:rows, :] = value[...] + got[:rows, :]
                else:
                    for mine, out in ((s[1 + level], outs[0]), (1 - s[1 + level], message)):
                        at = pl.ds(pl.multiple_of(mine * keep, keep), keep)
                        out[:keep, :] = value[at, :] + got[at, :]
                if extra:
                    message[keep:, :] = sent[rows:, :] + got[rows:, :]

            ins = [(a, pltpu.VMEM) for a in (value, sent, got)]
            outs = small(body, "fold", ins, [keep + extra] if last else [keep, keep + extra])
            return outs[0], outs[-1]

        def got_rows(level):
            return part_rows >> (level - 1)

        def merge(sent, got):
            rows = got_rows(levels - 1)

            def body(*refs):
                *ins, out = refs
                for k in range(STREAMS):
                    out[rows * k : rows * (k + 1), :] = ins[2 * k][:rows, :] + ins[2 * k + 1][:rows, :]

            ins = [(a, pltpu.VMEM) for pair in zip(sent, got) for a in pair]
            return small(body, "merge", ins, [rows * STREAMS])[0]

        def unfold(level, value, got):
            rows = value.shape[0] // STREAMS

            def body(value, got, out):
                s = place()
                for mine, ref in ((s[1 + level], value), (1 - s[1 + level], got)):
                    for k in range(STREAMS):
                        at = pl.multiple_of(mine * rows + 2 * rows * k, rows)
                        out[pl.ds(at, rows), :] = ref[rows * k : rows * (k + 1), :]

            ins = [(value, pltpu.VMEM), (got, pltpu.VMEM)]
            return small(body, "unfold", ins, [2 * STREAMS * rows])[0]

        def sum_pix(sends, owns):
            values, sents = list(owns), list(sends)
            for level in range(1, levels):
                for k in range(STREAMS):
                    got = swap(sents[k], "pix", 1 << (level - 1))
                    values[k], sents[k] = fold(level, values[k], sents[k], got)
            gots = [swap(sent, "pix", 1 << (levels - 1)) for sent in sents]
            value = merge(sents, gots)
            inverse = eliminate(sents[-1], gots[-1])
            for level in range(levels - 2, 0, -1):
                value = unfold(level, value, swap(value, "pix", 1 << level))
            value, inverse = lax.optimization_barrier((value, inverse))
            return inverse, value, swap(value, "pix", 1)

        def halves(inverse, panel, stacked):
            left = dot(inverse[...], join(panel), ((1,), (0,)), HIGH)
            wide = dot(inverse[...], unstack(stacked, rank), ((1,), (0,)), HIGH)
            left_high, left_low = split(left)
            wide_high, wide_low = split(wide)
            tops = jnp.concatenate([left_high, left_low, left_high], axis=0)
            return left, wide, (wide_high, wide_low), tops, jnp.concatenate([wide_high, wide_high, wide_low], axis=0)

        def middle(p, inverse, panel, stacked, o, d, before):
            n = len(panel)

            def body(inverse, *rest):
                s = place()
                parts, (stacked, o, d, *rest) = rest[:n], rest[n:]
                base, high, low, *after = rest[n * p :]
                _, _, right, tops, wides = halves(inverse, parts, stacked)
                for i in range(steps):
                    lowrank = dot(tops[:, chunk(i)], wides, ((0,), (0,)))
                    at = chunk(i), pl.ds(pix_at(p, s), half)
                    seen = o[at]
                    value = seen + d[at] * (1 / MU) - lowrank
                    scaled = jnp.clip(value, -TAU, TAU)
                    base[chunk(i), :] = seen + scaled
                    pair = split(seen + 2.0 * scaled - value)
                    high[chunk(i), :], low[chunk(i), :] = pair
                    term = dot_nt(right, pair)
                    side, block = divmod(i, steps // 2)
                    for k in range(STREAMS):
                        at = 2 * k + side, (slice(None), chunk(block))
                        new = term[part_of(k)]
                        after[at[0]][at[1]] = rest[at[0]][at[1]] + new if p else new

            arrays = [inverse, *panel, stacked, o, d] + (list(before) if p else [])
            outs = [((n_rows, half), F32, pltpu.VMEM)] + [((n_rows, half), BF16, pltpu.VMEM)] * 2
            outs += [((part_rank, n_rows // 2), F32, pltpu.VMEM)] * n
            cost = (9 * rank * n_rows * n_cols, 4 * n_rows * n_cols)
            ins = [(a, pltpu.VMEM) for a in arrays]
            base, high, low, *part = call(body, "middle", ins, outs, cost=cost)
            return base, (high, low), part

        def final(p, inverse, panel, stacked, base, before):
            n = len(panel)

            def body(inverse, *rest):
                s = place()
                parts, (stacked, base, *rest) = rest[:n], rest[n:]
                sparse, dual, *outs, sparse_part, dual_part, left_part, sems = rest[2 * p :]
                left, wide, _, tops, wides = halves(inverse, parts, stacked)
                moves = []
                if not p:
                    outs[1][...] = wide
                    outs[2][...] = pack(dot(wide, wide, ((1,), (1,)), HIGH))
                    for i in range(steps):
                        left_part[:, pl.ds(gal_at(i, s), tall)] = left[:, chunk(i)]
                    moves.append(pltpu.make_async_copy(left_part, outs[0], sems.at[steps, 0]))
                    moves[0].start()
                for i in range(steps):
                    value = base[chunk(i), :] - dot(tops[:, chunk(i)], wides, ((0,), (0,)))
                    scaled = jnp.clip(value, -TAU, TAU)
                    sparse_part[chunk(i), :] = value - scaled
                    dual_part[chunk(i), :] = MU * scaled
                    for a, (source, target) in enumerate(((sparse_part, sparse), (dual_part, dual))):
                        block = target.at[pl.ds(gal_at(i, s), tall), pl.ds(pix_at(p, s), half)]
                        move = pltpu.make_async_copy(source.at[chunk(i), :], block, sems.at[i, a])
                        move.start(priority=(i + a) % 2)
                        moves.append(move)
                for move in moves:
                    move.wait()

            ins = [(a, pltpu.VMEM) for a in (inverse, *panel, stacked, base)]
            outs = [((n_rows, n_cols), F32, pltpu.HBM)] * 2
            aliases = {}
            if p:
                ins += [(a, pltpu.HBM) for a in before[:2]]
                aliases = {n + 3: 0, n + 4: 1}
            else:
                outs += [((rank, n_rows), F32, pltpu.HBM), ((rank, half), F32, pltpu.VMEM)]
                outs += [((gram_rows, LANES), F32, pltpu.VMEM)]
            scratch = [pltpu.VMEM((n_rows, half), F32)] * 2 + [pltpu.VMEM((rank, n_rows), F32)]
            scratch += [pltpu.SemaphoreType.DMA((steps + 1, 2))]
            cost = (3 * rank * n_rows * n_cols, 4 * n_rows * n_cols)
            return call(body, "final", ins, outs, scratch, aliases, cost)

        def widen(inverse, other, gram):
            def body(inverse, stacked, gram, wide, out):
                wide[...] = dot(inverse[...], unstack(stacked, rank), ((1,), (0,)), HIGH)
                out[...] = gram[...] + pack(dot(wide[...], wide[...], ((1,), (1,)), HIGH))

            ins = [(a, pltpu.VMEM) for a in (inverse, other, gram)]
            outs = [((rank, half), F32, pltpu.VMEM), ((gram_rows, LANES), F32, pltpu.VMEM)]
            return call(body, "widen", ins, outs, cost=(10**8, MIB), limit=8)

        def finish(one, two, wide):
            def body(one, two, own, other, out, inverse, right, sem):
                s = place()
                invert(one[...] + two[...], inverse)
                for p, value in enumerate((own, other)):
                    right[:, pl.ds(pix_at(p, s), half)] = dot(inverse[...], value[...], ((1,), (0,)), HIGH)
                move = pltpu.make_async_copy(right, out, sem)
                move.start()
                move.wait()

            ins = [(a, pltpu.VMEM) for a in (one, two, *wide)]
            outs = [((rank, n_cols), F32, pltpu.HBM)]
            scratch = [pltpu.VMEM((rank, rank), F32), pltpu.VMEM((rank, n_cols), F32), pltpu.SemaphoreType.DMA(())]
            return call(body, "finish", ins, outs, scratch, cost=(10**8, 8 * MIB))[0]

        seen, pulls, own, other, part = first(right_init)
        base = [None, None]
        for step in range(ITERS):
            panel = sum_gal(part)
            sends = multiply(panel[:2], other, 1, False)
            sends += multiply(panel, other, 1, True, sends)
            inverse, own_wide, other_wide = sum_pix(sends, multiply(panel, own, STREAMS, False))
            if step < ITERS - 1:
                base[0], own, part = middle(0, inverse, panel, own_wide, seen, pulls, None)
                base[1], other, part = middle(1, inverse, panel, other_wide, seen, pulls, part)
            else:
                outs = final(0, inverse, panel, own_wide, base[0], None)
                other_wide, outs = lax.optimization_barrier((other_wide, outs))
                wide, gram = widen(inverse, other_wide, outs[4])
                bit = 1
                while 2 * bit < n_gal:
                    gram = add(gram, swap(gram, "gal", bit))
                    bit *= 2
                got = swap(gram, "gal", bit)
                sparse, dual = final(1, inverse, panel, other_wide, base[1], outs)
                left = outs[2]
                right = finish(gram, got, (outs[3], wide))
        return sparse, dual, left, right

    return jax.shard_map(
        per_device,
        mesh=mesh,
        in_specs=(P("pix", "gal"), P("pix", "gal"), P("pix", "gal"), P(None, "gal")),
        out_specs=(P("pix", "gal"), P("pix", "gal"), P(None, "pix"), P(None, "gal")),
        check_vma=False,
    )
```

```python
import jax
import jax.numpy as jnp
from jax import lax
from jax.experimental import pallas as pl
from jax.experimental.pallas import tpu as pltpu
from jax.sharding import PartitionSpec as P

ITERS = 2


MU = 1.25
TAU = 0.6 / 1.25
HIGH = lax.Precision.HIGHEST
CORES = 2
LANES = 128
F32, BF16 = jnp.float32, jnp.bfloat16
MIB = 1 << 20


def split(value):
    high = value.astype(BF16)
    return high, (value - high.astype(F32)).astype(BF16)


def dot(a, b, dims, precision=None):
    return lax.dot_general(a, b, (dims, ((), ())), precision=precision, preferred_element_type=F32)


def dot_nt(a, b):
    rows = a[0].shape[0]
    both = dot(jnp.concatenate(a, axis=0), b[0], ((1,), (1,)))
    return both[:rows] + both[rows:] + dot(a[0], b[1], ((1,), (1,)))


def dot_nn(a, b):
    rows = a[0].shape[0]
    both = dot(jnp.concatenate(a, axis=0), b[0], ((1,), (0,)))
    return both[:rows] + both[rows:] + dot(a[0], b[1], ((1,), (0,)))


def call(body, name, ins, outs, scratch=(), aliases=None, cost=(0, 0), limit=16):
    return pl.pallas_call(
        body,
        name=name,
        in_specs=[pl.BlockSpec(memory_space=space) for _, space in ins],
        out_specs=[pl.BlockSpec(memory_space=space) for _, _, space in outs],
        out_shape=[jax.ShapeDtypeStruct(shape, dtype) for shape, dtype, _ in outs],
        scratch_shapes=list(scratch),
        input_output_aliases=aliases or {},
        compiler_params=pltpu.CompilerParams(vmem_limit_bytes=limit * MIB),
        cost_estimate=pl.CostEstimate(flops=cost[0], bytes_accessed=cost[1], transcendentals=0),
    )(*[pltpu.with_memory_space_constraint(a, pltpu.HBM) if m is pltpu.HBM else a for a, m in ins])


def invert(packed, out):
    gram_rows, rank = packed.shape[0], out.shape[0]
    full = (8, LANES)
    lane = lax.broadcasted_iota(jnp.int32, full, 1)
    sub = lax.broadcasted_iota(jnp.int32, full, 0)
    turned = pltpu.roll(packed, LANES // 2, 1)
    rows = []
    for j in range(rank // 8):
        source = packed if 8 * j < gram_rows else turned
        at = 8 * j % gram_rows
        eye = jnp.where(lane - rank == sub + 8 * j, 1.0, 0.0)
        rows.append(jnp.where(lane < rank, source[at : at + 8], eye))
    wide = 4
    for k in range(0, rank, wide):
        r, at = divmod(k, 8)
        after = range(r if at + wide < 8 else r + 1, rank // 8)
        lines = [jnp.broadcast_to(rows[r][at + p : at + p + 1, :], full) for p in range(wide)]
        core = {
            (p, q): jnp.broadcast_to(lines[p][:, k + q : k + q + 1], full)
            for p in range(wide)
            for q in range(p, wide)
        }
        columns = {
            (j, p): jnp.broadcast_to(rows[j][:, k + p : k + p + 1], full) for j in after for p in range(wide)
        }
        for p in range(wide):
            inverse = 1.0 / core[p, p]
            factors = [core[p, q] * inverse for q in range(p + 1, wide)]
            for q, factor in zip(range(p + 1, wide), factors):
                for t in range(q, wide):
                    core[q, t] = core[q, t] - factor * core[p, t]
            scaled = lines[p] * inverse
            for q in range(p + 1, wide):
                lines[q] = lines[q] - core[p, q] * scaled
            for j in after:
                column = columns[j, p]
                if j == r:
                    column = jnp.where(sub >= at + wide, column, 0.0)
                rows[j] = rows[j] - column * scaled
                for q, factor in zip(range(p + 1, wide), factors):
                    columns[j, q] = columns[j, q] - factor * columns[j, p]
            done = lines[p] * lax.rsqrt(core[p, p])
            out[k + p : k + p + 1, :] = done[0:1, rank:]


def pack(gram):
    rows = gram.shape[0] // 2
    return jnp.concatenate([gram[:rows], gram[rows:]], axis=1)


def unstack(ref):
    blocks = ref.shape[0] // 64
    return jnp.concatenate([ref[64 * t : 64 * (t + 1), :] for t in range(blocks)], axis=1)


def solution(mesh):
    n_gal, n_pix = mesh.shape["gal"], mesh.shape["pix"]
    levels = n_pix.bit_length() - 1

    def swap(value, axis, bit):
        n = mesh.shape[axis]
        return lax.ppermute(value, axis, [(i, i ^ bit) for i in range(n)])

    def per_device(observed, sparse_init, dual_init, right_init):
        rank = right_init.shape[0]
        n_rows, n_cols = observed.shape
        half = n_cols // 2
        tall = min(256, n_rows // 2)
        steps = n_rows // tall
        quarter = rank * (half // LANES) // 2
        gram_rows = rank * rank // LANES

        def place():
            pix = lax.axis_index("pix")
            return [lax.rem(lax.axis_index("gal"), CORES)] + [lax.rem(pix >> level, 2) for level in range(levels)]

        def gal_at(i, s):
            turn = (1 - s[0]) * (steps // 2)
            return pl.multiple_of(lax.rem(i + turn, steps) * tall, tall)

        def pix_at(p, s):
            return pl.multiple_of(lax.rem(s[1] + p, 2) * half, half)

        def chunk(i):
            return slice(tall * i, tall * (i + 1))

        def join(pair):
            return jnp.concatenate([half[...] for half in pair], axis=1)

        def small(body, name, ins, rows, scratch=()):
            outs = [((n, LANES), F32, pltpu.VMEM) for n in rows]
            return call(body, name, ins, outs, scratch, cost=(10**5, 10**6), limit=4)

        def add(*arrays):
            def body(*refs):
                *ins, out = refs
                total = ins[0][...]
                for ref in ins[1:]:
                    total = total + ref[...]
                out[...] = total

            out = (arrays[0].shape, F32, pltpu.VMEM)
            return call(body, "add", [(a, pltpu.VMEM) for a in arrays], [out], cost=(10**5, 10**6), limit=4)[0]

        def first(right):
            def body(o_in, s_in, d_in, r_in, o, d, h0, l0, h1, l1, away, mine, sp, right, r_sem, sems):
                s = place()
                right_move = pltpu.make_async_copy(r_in, right, r_sem)
                right_move.start()
                moves = {}
                for i in range(steps):
                    for a, (source, target) in enumerate(((o_in, o), (s_in, sp), (d_in, d))):
                        block = source.at[pl.ds(gal_at(i, s), tall), :]
                        move = pltpu.make_async_copy(block, target.at[chunk(i), :], sems.at[i, a])
                        move.start(priority=(i + a) % 2)
                        moves[i, a] = move
                right_move.wait()
                rights = [split(right[:, pl.ds(pix_at(p, s), half)]) for p in (0, 1)]
                for i in range(steps):
                    total = None
                    for a in range(3):
                        moves[i, a].wait()
                    for p, (h, l) in enumerate(((h0, l0), (h1, l1))):
                        at = chunk(i), pl.ds(pix_at(p, s), half)
                        pair = split(o[at] - sp[at] + d[at] * (1 / MU))
                        h[chunk(i), :], l[chunk(i), :] = pair
                        term = dot_nt(rights[p], pair)
                        total = term if total is None else total + term
                    out = away if i < steps // 2 else mine
                    out[:, chunk(i % (steps // 2))] = total

            ins = [(a, pltpu.HBM) for a in (observed, sparse_init, dual_init, right)]
            outs = [((n_rows, n_cols), F32, pltpu.VMEM)] * 2 + [((n_rows, half), BF16, pltpu.VMEM)] * 4
            outs += [((rank, n_rows // 2), F32, pltpu.VMEM)] * 2
            scratch = [pltpu.VMEM((n_rows, n_cols), F32), pltpu.VMEM((rank, n_cols), F32)]
            scratch += [pltpu.SemaphoreType.DMA(()), pltpu.SemaphoreType.DMA((steps, 3))]
            cost = (6 * rank * n_rows * n_cols, 16 * n_rows * n_cols)
            got = call(body, "first", ins, outs, scratch, cost=cost)
            return got[0], got[1], got[2:4], got[4:6], got[6:8]

        def sum_gal(part):
            away, mine = part
            mine = add(mine, swap(away, "gal", 1))
            got = [
                lax.ppermute(mine, "gal", [(i, (i + CORES * k) % n_gal) for i in range(n_gal)])
                for k in range(1, n_gal // CORES)
            ]
            mine = add(mine, *got)
            return swap(mine, "gal", 1), mine

        def multiply_other(panel, pair):
            def body(away, mine, high, low, straight, across, stack):
                s = place()
                panel = join((away, mine))
                put_stack(dot_nn(split(panel), (high[...], low[...])), stack)
                gram = pack(dot(panel, panel, ((1,), (1,)), HIGH))
                for side, out in ((s[2], straight), (1 - s[2], across)):
                    out[:quarter, :] = stack[rows_at(side), :]
                    out[quarter:, :] = gram

            ins = [(a, pltpu.VMEM) for a in (*panel, *pair)]
            outs = [((quarter + gram_rows, LANES), F32, pltpu.VMEM)] * 2
            cost = (3 * rank * n_rows * n_cols, 2 * n_rows * n_cols)
            return call(body, "multiply_other", ins, outs, [pltpu.VMEM((2 * quarter, LANES), F32)], cost=cost)

        def multiply_own(panel, pair, sent):
            def body(away, mine, high, low, sent, keep, out, stack):
                s = place()
                put_stack(dot_nn(split(join((away, mine))), (high[...], low[...])), stack)
                keep[...] = stack[rows_at(s[2]), :]
                out[:quarter, :] = stack[rows_at(1 - s[2]), :]
                out[quarter:, :] = sent[quarter:, :]

            ins = [(a, pltpu.VMEM) for a in (*panel, *pair, sent)]
            outs = [((rows, LANES), F32, pltpu.VMEM) for rows in (quarter, quarter + gram_rows)]
            cost = (3 * rank * n_rows * n_cols, 2 * n_rows * n_cols)
            return call(body, "multiply_own", ins, outs, [pltpu.VMEM((2 * quarter, LANES), F32)], cost=cost)

        def put_stack(value, stack):
            for t in range(half // LANES):
                stack[rank * t : rank * (t + 1), :] = value[:, LANES * t : LANES * (t + 1)]

        def rows_at(side):
            return pl.ds(pl.multiple_of(side * quarter, quarter), quarter)

        def eliminate(one, two):
            def body(one, two, out):
                invert(one[-gram_rows:, :] + two[-gram_rows:, :], out)

            ins = [(one, pltpu.VMEM), (two, pltpu.VMEM)]
            outs = [((rank, rank), F32, pltpu.VMEM)]
            return call(body, "eliminate", ins, outs, cost=(10**8, 8 * MIB), limit=4)[0]

        def collect(keep, sent, gots):
            rows = keep.shape[0]

            def body(keep, sent, *refs):
                *gots, out = refs
                top, low = keep[...], sent[rows:, :]
                for got in gots:
                    top, low = top + got[:rows, :], low + got[rows:, :]
                out[:rows, :] = top
                out[rows:, :] = low

            ins = [(a, pltpu.VMEM) for a in (keep, sent, *gots)]
            return small(body, "collect", ins, [rows + gram_rows])[0]

        def divide(level, total):
            rows = (total.shape[0] - gram_rows) // 2

            def body(total, keep, out):
                s = place()
                for side, ref in ((s[1 + level], keep), (1 - s[1 + level], out)):
                    ref[:rows, :] = total[pl.ds(pl.multiple_of(side * rows, rows), rows), :]
                out[rows:, :] = total[2 * rows :, :]

            return small(body, "divide", [(total, pltpu.VMEM)], [rows, rows + gram_rows])

        def unfold(level, value, got):
            rows = value.shape[0]

            def body(value, got, out):
                s = place()
                for side, ref in ((s[1 + level], value), (1 - s[1 + level], got)):
                    out[pl.ds(pl.multiple_of(side * rows, rows), rows), :] = ref[...]

            ins = [(value, pltpu.VMEM), (got, pltpu.VMEM)]
            return small(body, "unfold", ins, [2 * rows])[0]

        def top(one, two):
            rows = one.shape[0] - gram_rows

            def body(one, two, out):
                out[...] = one[:rows, :] + two[:rows, :]

            return small(body, "top", [(one, pltpu.VMEM), (two, pltpu.VMEM)], [rows])[0]

        def sum_pix(panel, own, other):
            straight, across = multiply_other(panel, other)
            gots = [swap(straight, "pix", 1), swap(across, "pix", 3)]
            keep, beside = multiply_own(panel, own, straight)
            total = collect(keep, straight, gots + [swap(beside, "pix", 2)])
            for level in range(2, levels - 1):
                keep, sent = divide(level, total)
                total = collect(keep, sent, [swap(sent, "pix", 1 << level)])
            got = swap(total, "pix", 1 << (levels - 1))
            value = top(total, got)
            inverse = eliminate(total, got)
            for level in range(levels - 2, 1, -1):
                value = unfold(level, value, swap(value, "pix", 1 << level))
            beside, straight, across = [swap(value, "pix", bit) for bit in (2, 1, 3)]
            return inverse, unfold(1, value, beside), unfold(1, straight, across)

        def halves(inverse, panel, stacked):
            left = dot(inverse[...], join(panel), ((1,), (0,)), HIGH)
            wide = dot(inverse[...], unstack(stacked), ((1,), (0,)), HIGH)
            left_high, left_low = split(left)
            wide_high, wide_low = split(wide)
            tops = jnp.concatenate([left_high, left_low, left_high], axis=0)
            return left, (wide_high, wide_low), tops, jnp.concatenate([wide_high, wide_high, wide_low], axis=0)

        def middle(p, inverse, panel, stacked, o, d, before):
            def body(inverse, away, mine, stacked, o, d, *rest):
                s = place()
                base, high, low, *after = rest[2 * p :]
                _, right, tops, wides = halves(inverse, (away, mine), stacked)
                for i in range(steps):
                    lowrank = dot(tops[:, chunk(i)], wides, ((0,), (0,)))
                    at = chunk(i), pl.ds(pix_at(p, s), half)
                    seen = o[at]
                    value = seen + d[at] * (1 / MU) - lowrank
                    scaled = jnp.clip(value, -TAU, TAU)
                    base[chunk(i), :] = seen + scaled
                    pair = split(seen + 2.0 * scaled - value)
                    high[chunk(i), :], low[chunk(i), :] = pair
                    term = dot_nt(right, pair)
                    side, block = divmod(i, steps // 2)
                    after[side][:, chunk(block)] = rest[side][:, chunk(block)] + term if p else term

            arrays = [inverse, *panel, stacked, o, d] + (list(before) if p else [])
            outs = [((n_rows, half), F32, pltpu.VMEM)] + [((n_rows, half), BF16, pltpu.VMEM)] * 2
            outs += [((rank, n_rows // 2), F32, pltpu.VMEM)] * 2
            cost = (9 * rank * n_rows * n_cols, 4 * n_rows * n_cols)
            ins = [(a, pltpu.VMEM) for a in arrays]
            base, high, low, *part = call(body, "middle", ins, outs, cost=cost)
            return base, (high, low), part

        def final(p, inverse, panel, stacked, base, before):
            def body(inverse, away, mine, stacked, base, *rest):
                s = place()
                sparse, dual, *outs, sparse_part, dual_part, left_part, sems = rest[2 * p :]
                left, _, tops, wides = halves(inverse, (away, mine), stacked)
                moves = []
                if not p:
                    for i in range(steps):
                        left_part[:, pl.ds(gal_at(i, s), tall)] = left[:, chunk(i)]
                    moves.append(pltpu.make_async_copy(left_part, outs[0], sems.at[steps, 0]))
                    moves[0].start()
                for i in range(steps):
                    value = base[chunk(i), :] - dot(tops[:, chunk(i)], wides, ((0,), (0,)))
                    scaled = jnp.clip(value, -TAU, TAU)
                    sparse_part[chunk(i), :] = value - scaled
                    dual_part[chunk(i), :] = MU * scaled
                    for a, (source, target) in enumerate(((sparse_part, sparse), (dual_part, dual))):
                        block = target.at[pl.ds(gal_at(i, s), tall), pl.ds(pix_at(p, s), half)]
                        move = pltpu.make_async_copy(source.at[chunk(i), :], block, sems.at[i, a])
                        move.start(priority=(i + a) % 2)
                        moves.append(move)
                for move in moves:
                    move.wait()

            ins = [(a, pltpu.VMEM) for a in (inverse, *panel, stacked, base)]
            outs = [((n_rows, n_cols), F32, pltpu.HBM)] * 2
            aliases = {}
            if p:
                ins += [(a, pltpu.HBM) for a in before[:2]]
                aliases = {5: 0, 6: 1}
            else:
                outs += [((rank, n_rows), F32, pltpu.HBM)]
            scratch = [pltpu.VMEM((n_rows, half), F32)] * 2 + [pltpu.VMEM((rank, n_rows), F32)]
            scratch += [pltpu.SemaphoreType.DMA((steps + 1, 2))]
            cost = (3 * rank * n_rows * n_cols, 4 * n_rows * n_cols)
            return call(body, "final", ins, outs, scratch, aliases, cost)

        def widen(inverse, own, other):
            def body(inverse, own, other, wide_own, wide_other, out):
                grams = []
                for stacked, wide in ((own, wide_own), (other, wide_other)):
                    value = dot(inverse[...], unstack(stacked), ((1,), (0,)), HIGH)
                    wide[...] = value
                    grams.append(dot(value, value, ((1,), (1,)), HIGH))
                out[...] = pack(grams[0] + grams[1])

            ins = [(a, pltpu.VMEM) for a in (inverse, own, other)]
            outs = [((rank, half), F32, pltpu.VMEM)] * 2 + [((gram_rows, LANES), F32, pltpu.VMEM)]
            return call(body, "widen", ins, outs, cost=(10**8, MIB), limit=8)

        def finish(one, two, wide):
            def body(one, two, own, other, out, inverse, right, sem):
                s = place()
                invert(one[...] + two[...], inverse)
                for p, value in enumerate((own, other)):
                    right[:, pl.ds(pix_at(p, s), half)] = dot(inverse[...], value[...], ((1,), (0,)), HIGH)
                move = pltpu.make_async_copy(right, out, sem)
                move.start()
                move.wait()

            ins = [(a, pltpu.VMEM) for a in (one, two, *wide)]
            outs = [((rank, n_cols), F32, pltpu.HBM)]
            scratch = [pltpu.VMEM((rank, rank), F32), pltpu.VMEM((rank, n_cols), F32), pltpu.SemaphoreType.DMA(())]
            return call(body, "finish", ins, outs, scratch, cost=(10**8, 8 * MIB))[0]

        seen, pulls, own, other, part = first(right_init)
        base = [None, None]
        for step in range(ITERS):
            panel = sum_gal(part)
            inverse, own_wide, other_wide = sum_pix(panel, own, other)
            if step < ITERS - 1:
                base[0], own, part = middle(0, inverse, panel, own_wide, seen, pulls, None)
                base[1], other, part = middle(1, inverse, panel, other_wide, seen, pulls, part)
            else:
                *wide, gram = widen(inverse, own_wide, other_wide)
                outs = final(0, inverse, panel, own_wide, base[0], None)
                bit = 1
                while 2 * bit < n_gal:
                    gram = add(gram, swap(gram, "gal", bit))
                    bit *= 2
                got = swap(gram, "gal", bit)
                sparse, dual = final(1, inverse, panel, other_wide, base[1], outs)
                left = outs[2]
                right = finish(gram, got, wide)
        return sparse, dual, left, right

    return jax.shard_map(
        per_device,
        mesh=mesh,
        in_specs=(P("pix", "gal"), P("pix", "gal"), P("pix", "gal"), P(None, "gal")),
        out_specs=(P("pix", "gal"), P("pix", "gal"), P(None, "pix"), P(None, "gal")),
        check_vma=False,
    )
```

```python
import jax
import jax.numpy as jnp
from jax import lax
from jax.experimental import pallas as pl
from jax.experimental.pallas import tpu as pltpu
from jax.sharding import PartitionSpec as P

ITERS = 2


MU = 1.25
TAU = 0.6 / 1.25
HIGH = lax.Precision.HIGHEST
CORES = 2
LANES = 128
F32, BF16 = jnp.float32, jnp.bfloat16
MIB = 1 << 20


def split(value):
    high = value.astype(BF16)
    return high, (value - high.astype(F32)).astype(BF16)


def dot(a, b, dims, precision=None):
    return lax.dot_general(a, b, (dims, ((), ())), precision=precision, preferred_element_type=F32)


def dot_nt(a, b):
    rows = a[0].shape[0]
    both = dot(jnp.concatenate(a, axis=0), b[0], ((1,), (1,)))
    return both[:rows] + both[rows:] + dot(a[0], b[1], ((1,), (1,)))


def dot_nn(a, b):
    rows = a[0].shape[0]
    both = dot(jnp.concatenate(a, axis=0), b[0], ((1,), (0,)))
    return both[:rows] + both[rows:] + dot(a[0], b[1], ((1,), (0,)))


def call(body, name, ins, outs, scratch=(), aliases=None, cost=(0, 0), limit=16):
    return pl.pallas_call(
        body,
        name=name,
        in_specs=[pl.BlockSpec(memory_space=space) for _, space in ins],
        out_specs=[pl.BlockSpec(memory_space=space) for _, _, space in outs],
        out_shape=[jax.ShapeDtypeStruct(shape, dtype) for shape, dtype, _ in outs],
        scratch_shapes=list(scratch),
        input_output_aliases=aliases or {},
        compiler_params=pltpu.CompilerParams(vmem_limit_bytes=limit * MIB),
        cost_estimate=pl.CostEstimate(flops=cost[0], bytes_accessed=cost[1], transcendentals=0),
    )(*[pltpu.with_memory_space_constraint(a, pltpu.HBM) if m is pltpu.HBM else a for a, m in ins])


def reciprocal(value):
    guess = pl.reciprocal(value, approx=True)
    for _ in range(2):
        guess = guess * (2.0 - value * guess)
    return guess


def invert(packed, out):
    gram_rows, rank = packed.shape[0], out.shape[0]
    full = (8, LANES)
    lane = lax.broadcasted_iota(jnp.int32, full, 1)
    sub = lax.broadcasted_iota(jnp.int32, full, 0)
    turned = pltpu.roll(packed, LANES // 2, 1)
    rows = []
    for j in range(rank // 8):
        source = packed if 8 * j < gram_rows else turned
        at = 8 * j % gram_rows
        eye = jnp.where(lane - rank == sub + 8 * j, 1.0, 0.0)
        rows.append(jnp.where(lane < rank, source[at : at + 8], eye))
    wide = 4
    for k in range(0, rank, wide):
        r, at = divmod(k, 8)
        after = range(r if at + wide < 8 else r + 1, rank // 8)
        lines = [jnp.broadcast_to(rows[r][at + p : at + p + 1, :], full) for p in range(wide)]
        core = {
            (p, q): jnp.broadcast_to(lines[p][:, k + q : k + q + 1], full)
            for p in range(wide)
            for q in range(p, wide)
        }
        columns = {
            (j, p): jnp.broadcast_to(rows[j][:, k + p : k + p + 1], full) for j in after for p in range(wide)
        }
        for p in range(wide):
            inverse = reciprocal(core[p, p])
            factors = [core[p, q] * inverse for q in range(p + 1, wide)]
            for q, factor in zip(range(p + 1, wide), factors):
                for t in range(q, wide):
                    core[q, t] = core[q, t] - factor * core[p, t]
            scaled = lines[p] * inverse
            for q in range(p + 1, wide):
                lines[q] = lines[q] - core[p, q] * scaled
            for j in after:
                column = columns[j, p]
                if j == r:
                    column = jnp.where(sub >= at + wide, column, 0.0)
                rows[j] = rows[j] - column * scaled
                for q, factor in zip(range(p + 1, wide), factors):
                    columns[j, q] = columns[j, q] - factor * columns[j, p]
            done = lines[p] * lax.rsqrt(core[p, p])
            out[k + p : k + p + 1, :] = done[0:1, rank:]


def pack(gram):
    rows = gram.shape[0] // 2
    return jnp.concatenate([gram[:rows], gram[rows:]], axis=1)


def unstack(ref):
    blocks = ref.shape[0] // 64
    return jnp.concatenate([ref[64 * t : 64 * (t + 1), :] for t in range(blocks)], axis=1)


def solution(mesh):
    n_gal, n_pix = mesh.shape["gal"], mesh.shape["pix"]
    levels = n_pix.bit_length() - 1

    def swap(value, axis, bit):
        n = mesh.shape[axis]
        return lax.ppermute(value, axis, [(i, i ^ bit) for i in range(n)])

    def per_device(observed, sparse_init, dual_init, right_init):
        rank = right_init.shape[0]
        n_rows, n_cols = observed.shape
        half = n_cols // 2
        tall = min(256, n_rows // 2)
        steps = n_rows // tall
        quarter = rank * (half // LANES) // 2
        gram_rows = rank * rank // LANES

        def place():
            pix = lax.axis_index("pix")
            return [lax.rem(lax.axis_index("gal"), CORES)] + [lax.rem(pix >> level, 2) for level in range(levels)]

        def gal_at(i, s):
            turn = (1 - s[0]) * (steps // 2)
            return pl.multiple_of(lax.rem(i + turn, steps) * tall, tall)

        def pix_at(p, s):
            return pl.multiple_of(lax.rem(s[1] + p, 2) * half, half)

        def chunk(i):
            return slice(tall * i, tall * (i + 1))

        def join(pair):
            return jnp.concatenate([half[...] for half in pair], axis=1)

        def small(body, name, ins, rows, scratch=()):
            outs = [((n, LANES), F32, pltpu.VMEM) for n in rows]
            return call(body, name, ins, outs, scratch, cost=(10**5, 10**6), limit=4)

        def add(*arrays):
            def body(*refs):
                *ins, out = refs
                total = ins[0][...]
                for ref in ins[1:]:
                    total = total + ref[...]
                out[...] = total

            out = (arrays[0].shape, F32, pltpu.VMEM)
            return call(body, "add", [(a, pltpu.VMEM) for a in arrays], [out], cost=(10**5, 10**6), limit=4)[0]

        def first(right):
            def body(o_in, s_in, d_in, r_in, o, u, h0, l0, h1, l1, away, mine, sp, d, right, r_sem, sems):
                s = place()
                right_move = pltpu.make_async_copy(r_in, right, r_sem)
                right_move.start()
                moves = {}
                for i in range(steps):
                    for a, (source, target) in enumerate(((o_in, o), (s_in, sp), (d_in, d))):
                        block = source.at[pl.ds(gal_at(i, s), tall), :]
                        move = pltpu.make_async_copy(block, target.at[chunk(i), :], sems.at[i, a])
                        move.start(priority=(i + a) % 2)
                        moves[i, a] = move
                right_move.wait()
                rights = [split(right[:, pl.ds(pix_at(p, s), half)]) for p in (0, 1)]
                for i in range(steps):
                    total = None
                    for a in range(3):
                        moves[i, a].wait()
                    for p, (h, l) in enumerate(((h0, l0), (h1, l1))):
                        at = chunk(i), pl.ds(pix_at(p, s), half)
                        pulled = o[at] + d[at] * (1 / MU)
                        u[at] = pulled
                        pair = split(pulled - sp[at])
                        h[chunk(i), :], l[chunk(i), :] = pair
                        term = dot_nt(rights[p], pair)
                        total = term if total is None else total + term
                    out = away if i < steps // 2 else mine
                    out[:, chunk(i % (steps // 2))] = total

            ins = [(a, pltpu.HBM) for a in (observed, sparse_init, dual_init, right)]
            outs = [((n_rows, n_cols), F32, pltpu.VMEM)] * 2 + [((n_rows, half), BF16, pltpu.VMEM)] * 4
            outs += [((rank, n_rows // 2), F32, pltpu.VMEM)] * 2
            scratch = [pltpu.VMEM((n_rows, n_cols), F32)] * 2 + [pltpu.VMEM((rank, n_cols), F32)]
            scratch += [pltpu.SemaphoreType.DMA(()), pltpu.SemaphoreType.DMA((steps, 3))]
            cost = (6 * rank * n_rows * n_cols, 16 * n_rows * n_cols)
            got = call(body, "first", ins, outs, scratch, cost=cost)
            return got[0], got[1], got[2:4], got[4:6], got[6:8]

        def sum_gal(part):
            away, mine = part
            mine = add(mine, swap(away, "gal", 1))
            got = [
                lax.ppermute(mine, "gal", [(i, (i + CORES * k) % n_gal) for i in range(n_gal)])
                for k in range(1, n_gal // CORES)
            ]
            mine = add(mine, *got)
            return swap(mine, "gal", 1), mine

        def multiply_other(panel, pair):
            def body(away, mine, high, low, straight, across, stack):
                s = place()
                panel = join((away, mine))
                put_stack(dot_nn(split(panel), (high[...], low[...])), stack)
                gram = pack(dot(panel, panel, ((1,), (1,)), HIGH))
                for side, out in ((s[2], straight), (1 - s[2], across)):
                    out[:quarter, :] = stack[rows_at(side), :]
                    out[quarter:, :] = gram

            ins = [(a, pltpu.VMEM) for a in (*panel, *pair)]
            outs = [((quarter + gram_rows, LANES), F32, pltpu.VMEM)] * 2
            cost = (3 * rank * n_rows * n_cols, 2 * n_rows * n_cols)
            return call(body, "multiply_other", ins, outs, [pltpu.VMEM((2 * quarter, LANES), F32)], cost=cost)

        def multiply_own(panel, pair, sent):
            def body(away, mine, high, low, sent, keep, out, stack):
                s = place()
                put_stack(dot_nn(split(join((away, mine))), (high[...], low[...])), stack)
                keep[...] = stack[rows_at(s[2]), :]
                out[:quarter, :] = stack[rows_at(1 - s[2]), :]
                out[quarter:, :] = sent[quarter:, :]

            ins = [(a, pltpu.VMEM) for a in (*panel, *pair, sent)]
            outs = [((rows, LANES), F32, pltpu.VMEM) for rows in (quarter, quarter + gram_rows)]
            cost = (3 * rank * n_rows * n_cols, 2 * n_rows * n_cols)
            return call(body, "multiply_own", ins, outs, [pltpu.VMEM((2 * quarter, LANES), F32)], cost=cost)

        def put_stack(value, stack):
            for t in range(half // LANES):
                stack[rank * t : rank * (t + 1), :] = value[:, LANES * t : LANES * (t + 1)]

        def rows_at(side):
            return pl.ds(pl.multiple_of(side * quarter, quarter), quarter)

        def eliminate(one, two):
            def body(one, two, out):
                invert(one[-gram_rows:, :] + two[-gram_rows:, :], out)

            ins = [(one, pltpu.VMEM), (two, pltpu.VMEM)]
            outs = [((rank, rank), F32, pltpu.VMEM)]
            return call(body, "eliminate", ins, outs, cost=(10**8, 8 * MIB), limit=4)[0]

        def collect(keep, sent, gots):
            rows = keep.shape[0]

            def body(keep, sent, *refs):
                *gots, out = refs
                top, low = keep[...], sent[rows:, :]
                for got in gots:
                    top, low = top + got[:rows, :], low + got[rows:, :]
                out[:rows, :] = top
                out[rows:, :] = low

            ins = [(a, pltpu.VMEM) for a in (keep, sent, *gots)]
            return small(body, "collect", ins, [rows + gram_rows])[0]

        def divide(level, total):
            rows = (total.shape[0] - gram_rows) // 2

            def body(total, keep, out):
                s = place()
                for side, ref in ((s[1 + level], keep), (1 - s[1 + level], out)):
                    ref[:rows, :] = total[pl.ds(pl.multiple_of(side * rows, rows), rows), :]
                out[rows:, :] = total[2 * rows :, :]

            return small(body, "divide", [(total, pltpu.VMEM)], [rows, rows + gram_rows])

        def unfold(level, value, got):
            rows = value.shape[0]

            def body(value, got, out):
                s = place()
                for side, ref in ((s[1 + level], value), (1 - s[1 + level], got)):
                    out[pl.ds(pl.multiple_of(side * rows, rows), rows), :] = ref[...]

            ins = [(value, pltpu.VMEM), (got, pltpu.VMEM)]
            return small(body, "unfold", ins, [2 * rows])[0]

        def top(one, two):
            rows = one.shape[0] - gram_rows

            def body(one, two, out):
                out[...] = one[:rows, :] + two[:rows, :]

            return small(body, "top", [(one, pltpu.VMEM), (two, pltpu.VMEM)], [rows])[0]

        def sum_pix(panel, own, other):
            straight, across = multiply_other(panel, other)
            gots = [swap(straight, "pix", 1), swap(across, "pix", 3)]
            keep, beside = multiply_own(panel, own, straight)
            total = collect(keep, straight, gots + [swap(beside, "pix", 2)])
            for level in range(2, levels - 1):
                keep, sent = divide(level, total)
                total = collect(keep, sent, [swap(sent, "pix", 1 << level)])
            got = swap(total, "pix", 1 << (levels - 1))
            value = top(total, got)
            inverse = eliminate(total, got)
            for level in range(levels - 2, 1, -1):
                value = unfold(level, value, swap(value, "pix", 1 << level))
            beside, straight, across = [swap(value, "pix", bit) for bit in (2, 1, 3)]
            return inverse, unfold(1, value, beside), unfold(1, straight, across)

        def halves(inverse, panel, stacked):
            left = dot(inverse[...], join(panel), ((1,), (0,)), HIGH)
            wide = dot(inverse[...], unstack(stacked), ((1,), (0,)), HIGH)
            left_high, left_low = split(left)
            wide_high, wide_low = split(wide)
            tops = jnp.concatenate([left_high, left_low, left_high], axis=0)
            return left, (wide_high, wide_low), tops, jnp.concatenate([wide_high, wide_high, wide_low], axis=0)

        def middle(p, inverse, panel, stacked, o, u, before):
            def body(inverse, away, mine, stacked, o, u, *rest):
                s = place()
                base, high, low, *after = rest[2 * p :]
                _, right, tops, wides = halves(inverse, (away, mine), stacked)
                for i in range(steps):
                    lowrank = dot(tops[:, chunk(i)], wides, ((0,), (0,)))
                    at = chunk(i), pl.ds(pix_at(p, s), half)
                    value = u[at] - lowrank
                    scaled = jnp.clip(value, -TAU, TAU)
                    moved = o[at] + scaled
                    base[chunk(i), :] = moved
                    pair = split(moved + (scaled - value))
                    high[chunk(i), :], low[chunk(i), :] = pair
                    term = dot_nt(right, pair)
                    side, block = divmod(i, steps // 2)
                    after[side][:, chunk(block)] = rest[side][:, chunk(block)] + term if p else term

            arrays = [inverse, *panel, stacked, o, u] + (list(before) if p else [])
            outs = [((n_rows, half), F32, pltpu.VMEM)] + [((n_rows, half), BF16, pltpu.VMEM)] * 2
            outs += [((rank, n_rows // 2), F32, pltpu.VMEM)] * 2
            cost = (9 * rank * n_rows * n_cols, 4 * n_rows * n_cols)
            ins = [(a, pltpu.VMEM) for a in arrays]
            base, high, low, *part = call(body, "middle", ins, outs, cost=cost)
            return base, (high, low), part

        def put(sources, targets, p, s, sems):
            moves = []
            for i in range(steps):
                for a, (source, target) in enumerate(zip(sources, targets)):
                    block = target.at[pl.ds(gal_at(i, s), tall), pl.ds(pix_at(p, s), half)]
                    move = pltpu.make_async_copy(source.at[chunk(i), :], block, sems.at[i, a])
                    move.start(priority=(i + a) % 2)
                    moves.append(move)
            return moves

        def final(p, inverse, panel, stacked, base, before=()):
            def body(inverse, away, mine, stacked, base, *rest):
                s = place()
                sparse, dual, *outs = rest[len(before) :]
                *outs, left_part, sems = outs
                left, _, tops, wides = halves(inverse, (away, mine), stacked)
                if p:
                    moves = put(rest[:2], outs, 0, s, sems)
                else:
                    for i in range(steps):
                        left_part[:, pl.ds(gal_at(i, s), tall)] = left[:, chunk(i)]
                    moves = [pltpu.make_async_copy(left_part, outs[0], sems.at[0, 0])]
                    moves[0].start()
                for i in range(steps):
                    value = base[chunk(i), :] - dot(tops[:, chunk(i)], wides, ((0,), (0,)))
                    scaled = jnp.clip(value, -TAU, TAU)
                    sparse[chunk(i), :] = value - scaled
                    dual[chunk(i), :] = MU * scaled
                for move in moves:
                    move.wait()

            ins = [(a, pltpu.VMEM) for a in (inverse, *panel, stacked, base, *before)]
            outs = [((n_rows, half), F32, pltpu.VMEM)] * 2
            if p:
                outs += [((n_rows, n_cols), F32, pltpu.HBM)] * 2
            else:
                outs += [((rank, n_rows), F32, pltpu.HBM)]
            scratch = [pltpu.VMEM((rank, n_rows), F32), pltpu.SemaphoreType.DMA((steps, 2))]
            cost = (3 * rank * n_rows * n_cols, 4 * n_rows * n_cols)
            return call(body, "final", ins, outs, scratch, cost=cost)

        def widen(inverse, own, other):
            def body(inverse, own, other, wide_own, wide_other, out):
                grams = []
                for stacked, wide in ((own, wide_own), (other, wide_other)):
                    value = dot(inverse[...], unstack(stacked), ((1,), (0,)), HIGH)
                    wide[...] = value
                    grams.append(dot(value, value, ((1,), (1,)), HIGH))
                out[...] = pack(grams[0] + grams[1])

            ins = [(a, pltpu.VMEM) for a in (inverse, own, other)]
            outs = [((rank, half), F32, pltpu.VMEM)] * 2 + [((gram_rows, LANES), F32, pltpu.VMEM)]
            return call(body, "widen", ins, outs, cost=(10**8, MIB), limit=8)

        def finish(one, two, wide, made, outs):
            def body(one, two, own, other, sparse, dual, _, __, out, sparse_out, dual_out, inverse, right, sem, sems):
                s = place()
                moves = put((sparse, dual), (sparse_out, dual_out), 1, s, sems)
                invert(one[...] + two[...], inverse)
                for p, value in enumerate((own, other)):
                    at = pl.ds(pix_at(p, s), half)
                    right[:, at] = dot(inverse[...], value[...], ((1,), (0,)), HIGH)
                    move = pltpu.make_async_copy(right.at[:, at], out.at[:, at], sem.at[p])
                    move.start()
                    moves.append(move)
                for move in moves:
                    move.wait()

            ins = [(a, pltpu.VMEM) for a in (one, two, *wide, *made)] + [(a, pltpu.HBM) for a in outs]
            results = [((rank, n_cols), F32, pltpu.HBM)] + [((n_rows, n_cols), F32, pltpu.HBM)] * 2
            scratch = [pltpu.VMEM((rank, rank), F32), pltpu.VMEM((rank, n_cols), F32)]
            scratch += [pltpu.SemaphoreType.DMA((2,)), pltpu.SemaphoreType.DMA((steps, 2))]
            return call(body, "finish", ins, results, scratch, {6: 1, 7: 2}, cost=(10**8, 8 * MIB))

        seen, pulls, own, other, part = first(right_init)
        base = [None, None]
        for step in range(ITERS):
            panel = sum_gal(part)
            inverse, own_wide, other_wide = sum_pix(panel, own, other)
            if step < ITERS - 1:
                base[0], own, part = middle(0, inverse, panel, own_wide, seen, pulls, None)
                base[1], other, part = middle(1, inverse, panel, other_wide, seen, pulls, part)
            else:
                *wide, gram = widen(inverse, own_wide, other_wide)
                *made, left = final(0, inverse, panel, own_wide, base[0])
                bit = 1
                while 2 * bit < n_gal:
                    gram = add(gram, swap(gram, "gal", bit))
                    bit *= 2
                got = swap(gram, "gal", bit)
                *made, sparse, dual = final(1, inverse, panel, other_wide, base[1], made)
                right, sparse, dual = finish(gram, got, wide, made, (sparse, dual))
        return sparse, dual, left, right

    return jax.shard_map(
        per_device,
        mesh=mesh,
        in_specs=(P("pix", "gal"), P("pix", "gal"), P("pix", "gal"), P(None, "gal")),
        out_specs=(P("pix", "gal"), P("pix", "gal"), P(None, "pix"), P(None, "gal")),
        check_vma=False,
    )
```

```python
import jax
import jax.numpy as jnp
from jax import lax
from jax.experimental import pallas as pl
from jax.experimental.pallas import tpu as pltpu
from jax.sharding import PartitionSpec as P

ITERS = 2


MU = 1.25
TAU = 0.6 / 1.25
HIGH = lax.Precision.HIGHEST
CORES = 2
LANES = 128
F32, BF16 = jnp.float32, jnp.bfloat16
MIB = 1 << 20


def split(value):
    high = value.astype(BF16)
    return high, (value - high.astype(F32)).astype(BF16)


def dot(a, b, dims, precision=None):
    return lax.dot_general(a, b, (dims, ((), ())), precision=precision, preferred_element_type=F32)


def dot_nt(a, b):
    rows = a[0].shape[0]
    both = dot(jnp.concatenate(a, axis=0), b[0], ((1,), (1,)))
    return both[:rows] + both[rows:] + dot(a[0], b[1], ((1,), (1,)))


def dot_nn(a, b):
    rows = a[0].shape[0]
    both = dot(jnp.concatenate(a, axis=0), b[0], ((1,), (0,)))
    return both[:rows] + both[rows:] + dot(a[0], b[1], ((1,), (0,)))


def call(body, name, ins, outs, scratch=(), aliases=None, cost=(0, 0), limit=16):
    return pl.pallas_call(
        body,
        name=name,
        in_specs=[pl.BlockSpec(memory_space=space) for _, space in ins],
        out_specs=[pl.BlockSpec(memory_space=space) for _, _, space in outs],
        out_shape=[jax.ShapeDtypeStruct(shape, dtype) for shape, dtype, _ in outs],
        scratch_shapes=list(scratch),
        input_output_aliases=aliases or {},
        compiler_params=pltpu.CompilerParams(vmem_limit_bytes=limit * MIB),
        cost_estimate=pl.CostEstimate(flops=cost[0], bytes_accessed=cost[1], transcendentals=0),
    )(*[pltpu.with_memory_space_constraint(a, pltpu.HBM) if m is pltpu.HBM else a for a, m in ins])


def invert(packed, out):
    gram_rows, rank = packed.shape[0], out.shape[0]
    full = (8, LANES)
    lane = lax.broadcasted_iota(jnp.int32, full, 1)
    sub = lax.broadcasted_iota(jnp.int32, full, 0)
    turned = pltpu.roll(packed, LANES // 2, 1)
    rows = []
    for j in range(rank // 8):
        source = packed if 8 * j < gram_rows else turned
        at = 8 * j % gram_rows
        eye = jnp.where(lane - rank == sub + 8 * j, 1.0, 0.0)
        rows.append(jnp.where(lane < rank, source[at : at + 8], eye))
    wide = 4
    for k in range(0, rank, wide):
        r, at = divmod(k, 8)
        after = range(r if at + wide < 8 else r + 1, rank // 8)
        lines = [jnp.broadcast_to(rows[r][at + p : at + p + 1, :], full) for p in range(wide)]
        core = {
            (p, q): jnp.broadcast_to(lines[p][:, k + q : k + q + 1], full)
            for p in range(wide)
            for q in range(p, wide)
        }
        columns = {
            (j, p): jnp.broadcast_to(rows[j][:, k + p : k + p + 1], full) for j in after for p in range(wide)
        }
        for p in range(wide):
            inverse = 1.0 / core[p, p]
            factors = [core[p, q] * inverse for q in range(p + 1, wide)]
            for q, factor in zip(range(p + 1, wide), factors):
                for t in range(q, wide):
                    core[q, t] = core[q, t] - factor * core[p, t]
            scaled = lines[p] * inverse
            for q in range(p + 1, wide):
                lines[q] = lines[q] - core[p, q] * scaled
            for j in after:
                column = columns[j, p]
                if j == r:
                    column = jnp.where(sub >= at + wide, column, 0.0)
                rows[j] = rows[j] - column * scaled
                for q, factor in zip(range(p + 1, wide), factors):
                    columns[j, q] = columns[j, q] - factor * columns[j, p]
            done = lines[p] * lax.rsqrt(core[p, p])
            out[k + p : k + p + 1, :] = done[0:1, rank:]


def pack(gram):
    rows = gram.shape[0] // 2
    return jnp.concatenate([gram[:rows], gram[rows:]], axis=1)


def unstack(ref):
    blocks = ref.shape[0] // 64
    return jnp.concatenate([ref[64 * t : 64 * (t + 1), :] for t in range(blocks)], axis=1)


def solution(mesh):
    n_gal, n_pix = mesh.shape["gal"], mesh.shape["pix"]
    levels = n_pix.bit_length() - 1

    def swap(value, axis, bit):
        n = mesh.shape[axis]
        return lax.ppermute(value, axis, [(i, i ^ bit) for i in range(n)])

    def per_device(observed, sparse_init, dual_init, right_init):
        rank = right_init.shape[0]
        n_rows, n_cols = observed.shape
        half = n_cols // 2
        tall = min(256, n_rows // 2)
        steps = n_rows // tall
        quarter = rank * (half // LANES) // 2
        gram_rows = rank * rank // LANES
        share = gram_rows // CORES

        def place():
            pix = lax.axis_index("pix")
            return [lax.rem(lax.axis_index("gal"), CORES)] + [lax.rem(pix >> level, 2) for level in range(levels)]

        def gal_at(i, s):
            turn = (1 - s[0]) * (steps // 2)
            return pl.multiple_of(lax.rem(i + turn, steps) * tall, tall)

        def pix_at(p, s):
            return pl.multiple_of(lax.rem(s[1] + p, 2) * half, half)

        def chunk(i):
            return slice(tall * i, tall * (i + 1))

        def join(pair):
            return jnp.concatenate([half[...] for half in pair], axis=1)

        def small(body, name, ins, rows, scratch=()):
            outs = [((n, LANES), F32, pltpu.VMEM) for n in rows]
            return call(body, name, ins, outs, scratch, cost=(10**5, 10**6), limit=4)

        def add(*arrays):
            def body(*refs):
                *ins, out = refs
                total = ins[0][...]
                for ref in ins[1:]:
                    total = total + ref[...]
                out[...] = total

            out = (arrays[0].shape, F32, pltpu.VMEM)
            return call(body, "add", [(a, pltpu.VMEM) for a in arrays], [out], cost=(10**5, 10**6), limit=4)[0]

        def first(right):
            def body(o_in, s_in, d_in, r_in, o, u, h0, l0, h1, l1, away, mine, sp, d, right, r_sem, sems):
                s = place()
                right_move = pltpu.make_async_copy(r_in, right, r_sem)
                right_move.start()
                moves = {}
                for i in range(steps):
                    for a, (source, target) in enumerate(((o_in, o), (s_in, sp), (d_in, d))):
                        block = source.at[pl.ds(gal_at(i, s), tall), :]
                        move = pltpu.make_async_copy(block, target.at[chunk(i), :], sems.at[i, a])
                        move.start(priority=(i + a) % 2)
                        moves[i, a] = move
                right_move.wait()
                rights = [split(right[:, pl.ds(pix_at(p, s), half)]) for p in (0, 1)]
                for i in range(steps):
                    total = None
                    for a in range(3):
                        moves[i, a].wait()
                    for p, (h, l) in enumerate(((h0, l0), (h1, l1))):
                        at = chunk(i), pl.ds(pix_at(p, s), half)
                        pulled = o[at] + d[at] * (1 / MU)
                        u[at] = pulled
                        pair = split(pulled - sp[at])
                        h[chunk(i), :], l[chunk(i), :] = pair
                        term = dot_nt(rights[p], pair)
                        total = term if total is None else total + term
                    out = away if i < steps // 2 else mine
                    out[:, chunk(i % (steps // 2))] = total

            ins = [(a, pltpu.HBM) for a in (observed, sparse_init, dual_init, right)]
            outs = [((n_rows, n_cols), F32, pltpu.VMEM)] * 2 + [((n_rows, half), BF16, pltpu.VMEM)] * 4
            outs += [((rank, n_rows // 2), F32, pltpu.VMEM)] * 2
            scratch = [pltpu.VMEM((n_rows, n_cols), F32)] * 2 + [pltpu.VMEM((rank, n_cols), F32)]
            scratch += [pltpu.SemaphoreType.DMA(()), pltpu.SemaphoreType.DMA((steps, 3))]
            cost = (6 * rank * n_rows * n_cols, 16 * n_rows * n_cols)
            got = call(body, "first", ins, outs, scratch, cost=cost)
            return got[0], got[1], got[2:4], got[4:6], got[6:8]

        def sum_gal(part):
            away, mine = part
            mine = add(mine, swap(away, "gal", 1))
            got = [
                lax.ppermute(mine, "gal", [(i, (i + CORES * k) % n_gal) for i in range(n_gal)])
                for k in range(1, n_gal // CORES)
            ]
            mine = add(mine, *got)
            return swap(mine, "gal", 1), mine

        def multiply_other(panel, pair):
            def body(away, mine, high, low, straight, across, stack, gram):
                s = place()
                panel = join((away, mine))
                put_stack(dot_nn(split(panel), (high[...], low[...])), stack)
                gram[...] = pack(dot(panel, panel, ((1,), (1,)), HIGH))
                mine_rows = pl.ds(pl.multiple_of(s[0] * share, share), share)
                for side, out in ((s[2], straight), (1 - s[2], across)):
                    out[:quarter, :] = stack[rows_at(side), :]
                    out[quarter:, :] = gram[mine_rows, :]

            ins = [(a, pltpu.VMEM) for a in (*panel, *pair)]
            outs = [((quarter + share, LANES), F32, pltpu.VMEM)] * 2
            cost = (3 * rank * n_rows * n_cols, 2 * n_rows * n_cols)
            scratch = [pltpu.VMEM((rows, LANES), F32) for rows in (2 * quarter, gram_rows)]
            return call(body, "multiply_other", ins, outs, scratch, cost=cost)

        def multiply_own(panel, pair, sent):
            def body(away, mine, high, low, sent, keep, out, stack):
                s = place()
                put_stack(dot_nn(split(join((away, mine))), (high[...], low[...])), stack)
                keep[...] = stack[rows_at(s[2]), :]
                out[:quarter, :] = stack[rows_at(1 - s[2]), :]
                out[quarter:, :] = sent[quarter:, :]

            ins = [(a, pltpu.VMEM) for a in (*panel, *pair, sent)]
            outs = [((rows, LANES), F32, pltpu.VMEM) for rows in (quarter, quarter + share)]
            cost = (3 * rank * n_rows * n_cols, 2 * n_rows * n_cols)
            return call(body, "multiply_own", ins, outs, [pltpu.VMEM((2 * quarter, LANES), F32)], cost=cost)

        def put_stack(value, stack):
            for t in range(half // LANES):
                stack[rank * t : rank * (t + 1), :] = value[:, LANES * t : LANES * (t + 1)]

        def rows_at(side):
            return pl.ds(pl.multiple_of(side * quarter, quarter), quarter)

        def eliminate(mine, twin):
            def body(mine, twin, out):
                pair = jnp.concatenate([mine[...], twin[...]], axis=0)
                turned = jnp.concatenate([twin[...], mine[...]], axis=0)
                invert(jnp.where(place()[0] == 0, pair, turned), out)

            ins = [(mine, pltpu.VMEM), (twin, pltpu.VMEM)]
            outs = [((rank, rank), F32, pltpu.VMEM)]
            return call(body, "eliminate", ins, outs, cost=(10**8, 8 * MIB), limit=4)[0]

        def collect(keep, sent, gots):
            rows = keep.shape[0]

            def body(keep, sent, *refs):
                *gots, out = refs
                top, low = keep[...], sent[rows:, :]
                for got in gots:
                    top, low = top + got[:rows, :], low + got[rows:, :]
                out[:rows, :] = top
                out[rows:, :] = low

            ins = [(a, pltpu.VMEM) for a in (keep, sent, *gots)]
            return small(body, "collect", ins, [rows + share])[0]

        def divide(level, total):
            rows = (total.shape[0] - share) // 2

            def body(total, keep, out):
                s = place()
                for side, ref in ((s[1 + level], keep), (1 - s[1 + level], out)):
                    ref[:rows, :] = total[pl.ds(pl.multiple_of(side * rows, rows), rows), :]
                out[rows:, :] = total[2 * rows :, :]

            return small(body, "divide", [(total, pltpu.VMEM)], [rows, rows + share])

        def unfold(level, value, got):
            rows = value.shape[0]

            def body(value, got, out):
                s = place()
                for side, ref in ((s[1 + level], value), (1 - s[1 + level], got)):
                    out[pl.ds(pl.multiple_of(side * rows, rows), rows), :] = ref[...]

            ins = [(value, pltpu.VMEM), (got, pltpu.VMEM)]
            return small(body, "unfold", ins, [2 * rows])[0]

        def top(one, two, after):
            rows = one.shape[0] - share

            def body(one, two, _, out):
                out[...] = one[:rows, :] + two[:rows, :]

            ins = [(a, pltpu.VMEM) for a in (one, two, after)]
            return call(body, "top", ins, [((rows, LANES), F32, pltpu.VMEM)], cost=(10**8, 8 * MIB), limit=4)[0]

        def tail(one, two):
            rows = one.shape[0] - share

            def body(one, two, out):
                out[...] = one[rows:, :] + two[rows:, :]

            return small(body, "tail", [(one, pltpu.VMEM), (two, pltpu.VMEM)], [share])[0]

        def sum_pix(panel, own, other):
            straight, across = multiply_other(panel, other)
            gots = [swap(straight, "pix", 1), swap(across, "pix", 3)]
            keep, beside = multiply_own(panel, own, straight)
            total = collect(keep, straight, gots + [swap(beside, "pix", 2)])
            for level in range(2, levels - 1):
                keep, sent = divide(level, total)
                total = collect(keep, sent, [swap(sent, "pix", 1 << level)])
            got = swap(total, "pix", 1 << (levels - 1))
            gram = tail(total, got)
            value = top(total, got, gram)
            twin = swap(gram, "gal", 1)
            inverse = eliminate(gram, twin)
            for level in range(levels - 2, 1, -1):
                value = unfold(level, value, swap(value, "pix", 1 << level))
            beside = swap(value, "pix", 2)
            later, _ = lax.optimization_barrier((value, twin))
            straight, across = swap(later, "pix", 1), swap(later, "pix", 3)
            return inverse, unfold(1, value, beside), unfold(1, straight, across)

        def halves(inverse, panel, stacked):
            left = dot(inverse[...], join(panel), ((1,), (0,)), HIGH)
            wide = dot(inverse[...], unstack(stacked), ((1,), (0,)), HIGH)
            left_high, left_low = split(left)
            wide_high, wide_low = split(wide)
            tops = jnp.concatenate([left_high, left_low, left_high], axis=0)
            return left, (wide_high, wide_low), tops, jnp.concatenate([wide_high, wide_high, wide_low], axis=0)

        def middle(p, inverse, panel, stacked, o, u, before):
            def body(inverse, away, mine, stacked, o, u, *rest):
                s = place()
                base, high, low, *after = rest[2 * p :]
                _, right, tops, wides = halves(inverse, (away, mine), stacked)
                for i in range(steps):
                    lowrank = dot(tops[:, chunk(i)], wides, ((0,), (0,)))
                    at = chunk(i), pl.ds(pix_at(p, s), half)
                    value = u[at] - lowrank
                    scaled = jnp.clip(value, -TAU, TAU)
                    moved = o[at] + scaled
                    base[chunk(i), :] = moved
                    pair = split(moved + (scaled - value))
                    high[chunk(i), :], low[chunk(i), :] = pair
                    term = dot_nt(right, pair)
                    side, block = divmod(i, steps // 2)
                    after[side][:, chunk(block)] = rest[side][:, chunk(block)] + term if p else term

            arrays = [inverse, *panel, stacked, o, u] + (list(before) if p else [])
            outs = [((n_rows, half), F32, pltpu.VMEM)] + [((n_rows, half), BF16, pltpu.VMEM)] * 2
            outs += [((rank, n_rows // 2), F32, pltpu.VMEM)] * 2
            cost = (9 * rank * n_rows * n_cols, 4 * n_rows * n_cols)
            ins = [(a, pltpu.VMEM) for a in arrays]
            base, high, low, *part = call(body, "middle", ins, outs, cost=cost)
            return base, (high, low), part

        def put(sources, targets, p, s, sems):
            def moves(i):
                for a, (source, target) in enumerate(zip(sources, targets)):
                    block = target.at[pl.ds(gal_at(i, s), tall), pl.ds(pix_at(p, s), half)]
                    rows = pl.ds(pl.multiple_of(i * tall, tall), tall)
                    yield pltpu.make_async_copy(source.at[rows, :], block, sems.at[i, a])

            def start(i, carry):
                for a, move in enumerate(moves(i)):
                    move.start(priority=a)
                return carry

            lax.fori_loop(0, steps, start, 0)
            return [move for i in range(steps) for move in moves(i)]

        def final(p, inverse, panel, stacked, base, before=()):
            def body(inverse, away, mine, stacked, base, *rest):
                s = place()
                sparse, dual, *outs = rest[len(before) :]
                *outs, left_part, sems = outs
                left, _, tops, wides = halves(inverse, (away, mine), stacked)
                if p:
                    moves = put(rest[:2], outs, 0, s, sems)
                else:
                    for i in range(steps):
                        left_part[:, pl.ds(gal_at(i, s), tall)] = left[:, chunk(i)]
                    moves = [pltpu.make_async_copy(left_part, outs[0], sems.at[0, 0])]
                    moves[0].start()
                for i in range(steps):
                    value = base[chunk(i), :] - dot(tops[:, chunk(i)], wides, ((0,), (0,)))
                    scaled = jnp.clip(value, -TAU, TAU)
                    sparse[chunk(i), :] = value - scaled
                    dual[chunk(i), :] = MU * scaled
                for move in moves:
                    move.wait()

            ins = [(a, pltpu.VMEM) for a in (inverse, *panel, stacked, base, *before)]
            outs = [((n_rows, half), F32, pltpu.VMEM)] * 2
            if p:
                outs += [((n_rows, n_cols), F32, pltpu.HBM)] * 2
            else:
                outs += [((rank, n_rows), F32, pltpu.HBM)]
            scratch = [pltpu.VMEM((rank, n_rows), F32), pltpu.SemaphoreType.DMA((steps, 2))]
            cost = (3 * rank * n_rows * n_cols, 4 * n_rows * n_cols)
            return call(body, "final", ins, outs, scratch, cost=cost)

        def widen(inverse, own, other):
            def body(inverse, own, other, wide_own, wide_other, out):
                grams = []
                for stacked, wide in ((own, wide_own), (other, wide_other)):
                    value = dot(inverse[...], unstack(stacked), ((1,), (0,)), HIGH)
                    wide[...] = value
                    grams.append(dot(value, value, ((1,), (1,)), HIGH))
                out[...] = pack(grams[0] + grams[1])

            ins = [(a, pltpu.VMEM) for a in (inverse, own, other)]
            outs = [((rank, half), F32, pltpu.VMEM)] * 2 + [((gram_rows, LANES), F32, pltpu.VMEM)]
            return call(body, "widen", ins, outs, cost=(10**8, MIB), limit=8)

        def finish(one, two, wide, made, outs):
            def body(one, two, own, other, sparse, dual, _, __, out, sparse_out, dual_out, inverse, right, sem, sems):
                s = place()
                moves = put((sparse, dual), (sparse_out, dual_out), 1, s, sems)
                invert(one[...] + two[...], inverse)
                for p, value in enumerate((own, other)):
                    at = pl.ds(pix_at(p, s), half)
                    right[:, at] = dot(inverse[...], value[...], ((1,), (0,)), HIGH)
                    move = pltpu.make_async_copy(right.at[:, at], out.at[:, at], sem.at[p])
                    move.start()
                    moves.append(move)
                for move in moves:
                    move.wait()

            ins = [(a, pltpu.VMEM) for a in (one, two, *wide, *made)] + [(a, pltpu.HBM) for a in outs]
            results = [((rank, n_cols), F32, pltpu.HBM)] + [((n_rows, n_cols), F32, pltpu.HBM)] * 2
            scratch = [pltpu.VMEM((rank, rank), F32), pltpu.VMEM((rank, n_cols), F32)]
            scratch += [pltpu.SemaphoreType.DMA((2,)), pltpu.SemaphoreType.DMA((steps, 2))]
            return call(body, "finish", ins, results, scratch, {6: 1, 7: 2}, cost=(10**8, 8 * MIB))

        seen, pulls, own, other, part = first(right_init)
        base = [None, None]
        for step in range(ITERS):
            panel = sum_gal(part)
            inverse, own_wide, other_wide = sum_pix(panel, own, other)
            if step < ITERS - 1:
                base[0], own, part = middle(0, inverse, panel, own_wide, seen, pulls, None)
                base[1], other, part = middle(1, inverse, panel, other_wide, seen, pulls, part)
            else:
                *wide, gram = widen(inverse, own_wide, other_wide)
                *made, left = final(0, inverse, panel, own_wide, base[0])
                bit = 1
                while 2 * bit < n_gal:
                    gram = add(gram, swap(gram, "gal", bit))
                    bit *= 2
                got = swap(gram, "gal", bit)
                *made, sparse, dual = final(1, inverse, panel, other_wide, base[1], made)
                right, sparse, dual = finish(gram, got, wide, made, (sparse, dual))
        return sparse, dual, left, right

    return jax.shard_map(
        per_device,
        mesh=mesh,
        in_specs=(P("pix", "gal"), P("pix", "gal"), P("pix", "gal"), P(None, "gal")),
        out_specs=(P("pix", "gal"), P("pix", "gal"), P(None, "pix"), P(None, "gal")),
        check_vma=False,
    )
```

```python
import jax
import jax.numpy as jnp
from jax import lax
from jax.experimental import pallas as pl
from jax.experimental.pallas import tpu as pltpu
from jax.sharding import PartitionSpec as P

ITERS = 2


MU = 1.25
TAU = 0.6 / 1.25
HIGH = lax.Precision.HIGHEST
CORES = 2
LANES = 128
F32, BF16 = jnp.float32, jnp.bfloat16
MIB = 1 << 20


def split(value):
    high = value.astype(BF16)
    return high, (value - high.astype(F32)).astype(BF16)


def dot(a, b, dims, precision=None):
    return lax.dot_general(a, b, (dims, ((), ())), precision=precision, preferred_element_type=F32)


def dot_nt(a, b):
    rows = a[0].shape[0]
    both = dot(jnp.concatenate(a, axis=0), b[0], ((1,), (1,)))
    return both[:rows] + both[rows:] + dot(a[0], b[1], ((1,), (1,)))


def dot_nn(a, b):
    rows = a[0].shape[0]
    both = dot(jnp.concatenate(a, axis=0), b[0], ((1,), (0,)))
    return both[:rows] + both[rows:] + dot(a[0], b[1], ((1,), (0,)))


def call(body, name, ins, outs, scratch=(), aliases=None, cost=(0, 0), limit=16):
    return pl.pallas_call(
        body,
        name=name,
        in_specs=[pl.BlockSpec(memory_space=space) for _, space in ins],
        out_specs=[pl.BlockSpec(memory_space=space) for _, _, space in outs],
        out_shape=[jax.ShapeDtypeStruct(shape, dtype) for shape, dtype, _ in outs],
        scratch_shapes=list(scratch),
        input_output_aliases=aliases or {},
        compiler_params=pltpu.CompilerParams(vmem_limit_bytes=limit * MIB),
        cost_estimate=pl.CostEstimate(flops=cost[0], bytes_accessed=cost[1], transcendentals=0),
    )(*[pltpu.with_memory_space_constraint(a, pltpu.HBM) if m is pltpu.HBM else a for a, m in ins])


def invert(packed, out):
    gram_rows, rank = packed.shape[0], out.shape[0]
    full = (8, LANES)
    lane = lax.broadcasted_iota(jnp.int32, full, 1)
    sub = lax.broadcasted_iota(jnp.int32, full, 0)
    turned = pltpu.roll(packed, LANES // 2, 1)
    rows = []
    for j in range(rank // 8):
        source = packed if 8 * j < gram_rows else turned
        at = 8 * j % gram_rows
        eye = jnp.where(lane - rank == sub + 8 * j, 1.0, 0.0)
        rows.append(jnp.where(lane < rank, source[at : at + 8], eye))
    wide = 4
    for k in range(0, rank, wide):
        r, at = divmod(k, 8)
        after = range(r if at + wide < 8 else r + 1, rank // 8)
        lines = [jnp.broadcast_to(rows[r][at + p : at + p + 1, :], full) for p in range(wide)]
        core = {
            (p, q): jnp.broadcast_to(lines[p][:, k + q : k + q + 1], full)
            for p in range(wide)
            for q in range(p, wide)
        }
        columns = {
            (j, p): jnp.broadcast_to(rows[j][:, k + p : k + p + 1], full) for j in after for p in range(wide)
        }
        for p in range(wide):
            inverse = 1.0 / core[p, p]
            factors = [core[p, q] * inverse for q in range(p + 1, wide)]
            for q, factor in zip(range(p + 1, wide), factors):
                for t in range(q, wide):
                    core[q, t] = core[q, t] - factor * core[p, t]
            scaled = lines[p] * inverse
            for q in range(p + 1, wide):
                lines[q] = lines[q] - core[p, q] * scaled
            for j in after:
                column = columns[j, p]
                if j == r:
                    column = jnp.where(sub >= at + wide, column, 0.0)
                rows[j] = rows[j] - column * scaled
                for q, factor in zip(range(p + 1, wide), factors):
                    columns[j, q] = columns[j, q] - factor * columns[j, p]
            done = lines[p] * lax.rsqrt(core[p, p])
            out[k + p : k + p + 1, :] = done[0:1, rank:]


def pack(gram):
    rows = gram.shape[0] // 2
    return jnp.concatenate([gram[:rows], gram[rows:]], axis=1)


def unstack(ref):
    blocks = ref.shape[0] // 64
    return jnp.concatenate([ref[64 * t : 64 * (t + 1), :] for t in range(blocks)], axis=1)


def solution(mesh):
    n_gal, n_pix = mesh.shape["gal"], mesh.shape["pix"]
    levels = n_pix.bit_length() - 1

    def swap(value, axis, bit):
        n = mesh.shape[axis]
        return lax.ppermute(value, axis, [(i, i ^ bit) for i in range(n)])

    def per_device(observed, sparse_init, dual_init, right_init):
        rank = right_init.shape[0]
        n_rows, n_cols = observed.shape
        half = n_cols // 2
        tall = min(256, n_rows // 2)
        steps = n_rows // tall
        quarter = rank * (half // LANES) // 2
        gram_rows = rank * rank // LANES

        def place():
            pix = lax.axis_index("pix")
            return [lax.rem(lax.axis_index("gal"), CORES)] + [lax.rem(pix >> level, 2) for level in range(levels)]

        def gal_at(i, s):
            turn = (1 - s[0]) * (steps // 2)
            return pl.multiple_of(lax.rem(i + turn, steps) * tall, tall)

        def pix_at(p, s):
            return pl.multiple_of(lax.rem(s[1] + p, 2) * half, half)

        def chunk(i):
            return slice(tall * i, tall * (i + 1))

        def join(pair):
            return jnp.concatenate([half[...] for half in pair], axis=1)

        def small(body, name, ins, rows, scratch=()):
            outs = [((n, LANES), F32, pltpu.VMEM) for n in rows]
            return call(body, name, ins, outs, scratch, cost=(10**5, 10**6), limit=4)

        def add(*arrays):
            def body(*refs):
                *ins, out = refs
                total = ins[0][...]
                for ref in ins[1:]:
                    total = total + ref[...]
                out[...] = total

            out = (arrays[0].shape, F32, pltpu.VMEM)
            return call(body, "add", [(a, pltpu.VMEM) for a in arrays], [out], cost=(10**5, 10**6), limit=4)[0]

        def first(right):
            def body(o_in, s_in, d_in, r_in, o, u, h0, l0, h1, l1, away, mine, sp, d, right, r_sem, sems):
                s = place()
                right_move = pltpu.make_async_copy(r_in, right, r_sem)
                right_move.start()
                moves = {}
                for i in range(steps):
                    for a, (source, target) in enumerate(((o_in, o), (s_in, sp), (d_in, d))):
                        block = source.at[pl.ds(gal_at(i, s), tall), :]
                        move = pltpu.make_async_copy(block, target.at[chunk(i), :], sems.at[i, a])
                        move.start(priority=(i + a) % 2)
                        moves[i, a] = move
                right_move.wait()
                rights = [split(right[:, pl.ds(pix_at(p, s), half)]) for p in (0, 1)]
                for i in range(steps):
                    total = None
                    for a in range(3):
                        moves[i, a].wait()
                    for p, (h, l) in enumerate(((h0, l0), (h1, l1))):
                        at = chunk(i), pl.ds(pix_at(p, s), half)
                        pulled = o[at] + d[at] * (1 / MU)
                        u[at] = pulled
                        pair = split(pulled - sp[at])
                        h[chunk(i), :], l[chunk(i), :] = pair
                        term = dot_nt(rights[p], pair)
                        total = term if total is None else total + term
                    out = away if i < steps // 2 else mine
                    out[:, chunk(i % (steps // 2))] = total

            ins = [(a, pltpu.HBM) for a in (observed, sparse_init, dual_init, right)]
            outs = [((n_rows, n_cols), F32, pltpu.VMEM)] * 2 + [((n_rows, half), BF16, pltpu.VMEM)] * 4
            outs += [((rank, n_rows // 2), F32, pltpu.VMEM)] * 2
            scratch = [pltpu.VMEM((n_rows, n_cols), F32)] * 2 + [pltpu.VMEM((rank, n_cols), F32)]
            scratch += [pltpu.SemaphoreType.DMA(()), pltpu.SemaphoreType.DMA((steps, 3))]
            cost = (6 * rank * n_rows * n_cols, 16 * n_rows * n_cols)
            got = call(body, "first", ins, outs, scratch, cost=cost)
            return got[0], got[1], got[2:4], got[4:6], got[6:8]

        def sum_gal(part):
            away, mine = part
            mine = add(mine, swap(away, "gal", 1))
            got = [
                lax.ppermute(mine, "gal", [(i, (i + CORES * k) % n_gal) for i in range(n_gal)])
                for k in range(1, n_gal // CORES)
            ]
            mine = add(mine, *got)
            return swap(mine, "gal", 1), mine

        def multiply_mine(mine, pair, other_pair):
            def body(mine, high, low, high_other, low_other, own, other, gram):
                panel = split(mine[...])
                for at, out in (((high, low), own), ((high_other, low_other), other)):
                    put_stack(dot_nn(panel, [ref[n_rows // 2 :, :] for ref in at]), out)
                gram[...] = pack(dot(mine[...], mine[...], ((1,), (1,)), HIGH))

            ins = [(a, pltpu.VMEM) for a in (mine, *pair, *other_pair)]
            outs = [((rows, LANES), F32, pltpu.VMEM) for rows in (2 * quarter, 2 * quarter, gram_rows)]
            cost = (3 * rank * n_rows * n_cols, 2 * n_rows * n_cols)
            return call(body, "multiply_mine", ins, outs, cost=cost)

        def multiply_other(away, pair, before, gram):
            def body(away, high, low, before, gram, straight, across, stack):
                s = place()
                pairs = [ref[: n_rows // 2, :] for ref in (high, low)]
                put_stack(dot_nn(split(away[...]), pairs), stack)
                total = gram[...] + pack(dot(away[...], away[...], ((1,), (1,)), HIGH))
                for side, out in ((s[2], straight), (1 - s[2], across)):
                    out[:quarter, :] = stack[rows_at(side), :] + before[rows_at(side), :]
                    out[quarter:, :] = total

            ins = [(a, pltpu.VMEM) for a in (away, *pair, before, gram)]
            outs = [((quarter + gram_rows, LANES), F32, pltpu.VMEM)] * 2
            cost = (2 * rank * n_rows * n_cols, n_rows * n_cols)
            return call(body, "multiply_other", ins, outs, [pltpu.VMEM((2 * quarter, LANES), F32)], cost=cost)

        def multiply_own(away, pair, before, sent):
            def body(away, high, low, before, sent, keep, out, stack):
                s = place()
                pairs = [ref[: n_rows // 2, :] for ref in (high, low)]
                put_stack(dot_nn(split(away[...]), pairs), stack)
                for side, ref in ((s[2], keep), (1 - s[2], out)):
                    ref[:quarter, :] = stack[rows_at(side), :] + before[rows_at(side), :]
                out[quarter:, :] = sent[quarter:, :]

            ins = [(a, pltpu.VMEM) for a in (away, *pair, before, sent)]
            outs = [((rows, LANES), F32, pltpu.VMEM) for rows in (quarter, quarter + gram_rows)]
            cost = (10**9, 8 * MIB)
            return call(body, "multiply_own", ins, outs, [pltpu.VMEM((2 * quarter, LANES), F32)], cost=cost)

        def put_stack(value, stack):
            for t in range(half // LANES):
                stack[rank * t : rank * (t + 1), :] = value[:, LANES * t : LANES * (t + 1)]

        def rows_at(side):
            return pl.ds(pl.multiple_of(side * quarter, quarter), quarter)

        def eliminate(one, two):
            def body(one, two, out):
                invert(one[-gram_rows:, :] + two[-gram_rows:, :], out)

            ins = [(one, pltpu.VMEM), (two, pltpu.VMEM)]
            outs = [((rank, rank), F32, pltpu.VMEM)]
            return call(body, "eliminate", ins, outs, cost=(10**8, 8 * MIB), limit=4)[0]

        def collect(keep, sent, gots):
            rows = keep.shape[0]

            def body(keep, sent, *refs):
                *gots, out = refs
                top, low = keep[...], sent[rows:, :]
                for got in gots:
                    top, low = top + got[:rows, :], low + got[rows:, :]
                out[:rows, :] = top
                out[rows:, :] = low

            ins = [(a, pltpu.VMEM) for a in (keep, sent, *gots)]
            return small(body, "collect", ins, [rows + gram_rows])[0]

        def divide(level, total):
            rows = (total.shape[0] - gram_rows) // 2

            def body(total, keep, out):
                s = place()
                for side, ref in ((s[1 + level], keep), (1 - s[1 + level], out)):
                    ref[:rows, :] = total[pl.ds(pl.multiple_of(side * rows, rows), rows), :]
                out[rows:, :] = total[2 * rows :, :]

            return small(body, "divide", [(total, pltpu.VMEM)], [rows, rows + gram_rows])

        def unfold(level, value, got):
            rows = value.shape[0]

            def body(value, got, out):
                s = place()
                for side, ref in ((s[1 + level], value), (1 - s[1 + level], got)):
                    out[pl.ds(pl.multiple_of(side * rows, rows), rows), :] = ref[...]

            ins = [(value, pltpu.VMEM), (got, pltpu.VMEM)]
            return small(body, "unfold", ins, [2 * rows])[0]

        def top(one, two):
            rows = one.shape[0] - gram_rows

            def body(one, two, out):
                out[...] = one[:rows, :] + two[:rows, :]

            return small(body, "top", [(one, pltpu.VMEM), (two, pltpu.VMEM)], [rows])[0]

        def sum_pix(panel, own, other):
            away, mine = panel
            own_before, other_before, gram = multiply_mine(mine, own, other)
            straight, across = multiply_other(away, other, other_before, gram)
            gots = [swap(straight, "pix", 1), swap(across, "pix", 3)]
            keep, beside = multiply_own(away, own, own_before, straight)
            total = collect(keep, straight, gots + [swap(beside, "pix", 2)])
            for level in range(2, levels - 1):
                keep, sent = divide(level, total)
                total = collect(keep, sent, [swap(sent, "pix", 1 << level)])
            got = swap(total, "pix", 1 << (levels - 1))
            value = top(total, got)
            inverse = eliminate(total, got)
            for level in range(levels - 2, 1, -1):
                value = unfold(level, value, swap(value, "pix", 1 << level))
            beside, straight, across = [swap(value, "pix", bit) for bit in (2, 1, 3)]
            return inverse, unfold(1, value, beside), unfold(1, straight, across)

        def halves(inverse, panel, stacked):
            left = dot(inverse[...], join(panel), ((1,), (0,)), HIGH)
            wide = dot(inverse[...], unstack(stacked), ((1,), (0,)), HIGH)
            left_high, left_low = split(left)
            wide_high, wide_low = split(wide)
            tops = jnp.concatenate([left_high, left_low, left_high], axis=0)
            return left, (wide_high, wide_low), tops, jnp.concatenate([wide_high, wide_high, wide_low], axis=0)

        def middle(p, sides, inverse, panel, stacked, o, u, before, arrays=()):
            n = len(sides)
            blocks = [i for i in range(steps) if i // (steps // 2) in sides]

            def body(inverse, *rest):
                s = place()
                panel, (stacked, o, u, *rest) = rest[:n], rest[n:]
                base, high, low, *after = rest[n * p + len(arrays) :]
                _, right, tops, wides = halves(inverse, panel, stacked)
                for k, i in enumerate(blocks):
                    lowrank = dot(tops[:, chunk(k)], wides, ((0,), (0,)))
                    at = chunk(i), pl.ds(pix_at(p, s), half)
                    value = u[at] - lowrank
                    scaled = jnp.clip(value, -TAU, TAU)
                    moved = o[at] + scaled
                    base[chunk(i), :] = moved
                    pair = split(moved + (scaled - value))
                    high[chunk(i), :], low[chunk(i), :] = pair
                    term = dot_nt(right, pair)
                    side, block = divmod(k, steps // 2)
                    after[side][:, chunk(block)] = rest[side][:, chunk(block)] + term if p else term

            ins = [inverse, *[panel[side] for side in sides], stacked, o, u]
            ins += [before[side] for side in sides] if p else []
            aliases = {len(ins) + k: k for k in range(len(arrays))}
            outs = [((n_rows, half), F32, pltpu.VMEM)] + [((n_rows, half), BF16, pltpu.VMEM)] * 2
            outs += [((rank, n_rows // 2), F32, pltpu.VMEM)] * n
            cost = (9 * rank * n_rows * n_cols // (3 - n), 4 * n_rows * n_cols // (3 - n))
            ins = [(a, pltpu.VMEM) for a in (*ins, *arrays)]
            base, high, low, *part = call(body, "middle", ins, outs, aliases=aliases, cost=cost)
            return base, (high, low), part

        def put(sources, targets, p, s, sems):
            def moves(i):
                for a, (source, target) in enumerate(zip(sources, targets)):
                    block = target.at[pl.ds(gal_at(i, s), tall), pl.ds(pix_at(p, s), half)]
                    rows = pl.ds(pl.multiple_of(i * tall, tall), tall)
                    yield pltpu.make_async_copy(source.at[rows, :], block, sems.at[i, a])

            def start(i, carry):
                for a, move in enumerate(moves(i)):
                    move.start(priority=a)
                return carry

            lax.fori_loop(0, steps, start, 0)
            return [move for i in range(steps) for move in moves(i)]

        def final(p, inverse, panel, stacked, base, before=()):
            def body(inverse, away, mine, stacked, base, *rest):
                s = place()
                sparse, dual, *outs = rest[len(before) :]
                *outs, left_part, sems = outs
                left, _, tops, wides = halves(inverse, (away, mine), stacked)
                if p:
                    moves = put(rest[:2], outs, 0, s, sems)
                else:
                    for i in range(steps):
                        left_part[:, pl.ds(gal_at(i, s), tall)] = left[:, chunk(i)]
                    moves = [pltpu.make_async_copy(left_part, outs[0], sems.at[0, 0])]
                    moves[0].start()
                for i in range(steps):
                    value = base[chunk(i), :] - dot(tops[:, chunk(i)], wides, ((0,), (0,)))
                    scaled = jnp.clip(value, -TAU, TAU)
                    sparse[chunk(i), :] = value - scaled
                    dual[chunk(i), :] = MU * scaled
                for move in moves:
                    move.wait()

            ins = [(a, pltpu.VMEM) for a in (inverse, *panel, stacked, base, *before)]
            outs = [((n_rows, half), F32, pltpu.VMEM)] * 2
            if p:
                outs += [((n_rows, n_cols), F32, pltpu.HBM)] * 2
            else:
                outs += [((rank, n_rows), F32, pltpu.HBM)]
            scratch = [pltpu.VMEM((rank, n_rows), F32), pltpu.SemaphoreType.DMA((steps, 2))]
            cost = (3 * rank * n_rows * n_cols, 4 * n_rows * n_cols)
            return call(body, "final", ins, outs, scratch, cost=cost)

        def widen(inverse, own, other):
            def body(inverse, own, other, wide_own, wide_other, out):
                grams = []
                for stacked, wide in ((own, wide_own), (other, wide_other)):
                    value = dot(inverse[...], unstack(stacked), ((1,), (0,)), HIGH)
                    wide[...] = value
                    grams.append(dot(value, value, ((1,), (1,)), HIGH))
                out[...] = pack(grams[0] + grams[1])

            ins = [(a, pltpu.VMEM) for a in (inverse, own, other)]
            outs = [((rank, half), F32, pltpu.VMEM)] * 2 + [((gram_rows, LANES), F32, pltpu.VMEM)]
            return call(body, "widen", ins, outs, cost=(10**8, MIB), limit=8)

        def finish(one, two, wide, made, outs):
            def body(one, two, own, other, sparse, dual, _, __, out, sparse_out, dual_out, inverse, right, sem, sems):
                s = place()
                moves = put((sparse, dual), (sparse_out, dual_out), 1, s, sems)
                invert(one[...] + two[...], inverse)
                for p, value in enumerate((own, other)):
                    at = pl.ds(pix_at(p, s), half)
                    right[:, at] = dot(inverse[...], value[...], ((1,), (0,)), HIGH)
                    move = pltpu.make_async_copy(right.at[:, at], out.at[:, at], sem.at[p])
                    move.start()
                    moves.append(move)
                for move in moves:
                    move.wait()

            ins = [(a, pltpu.VMEM) for a in (one, two, *wide, *made)] + [(a, pltpu.HBM) for a in outs]
            results = [((rank, n_cols), F32, pltpu.HBM)] + [((n_rows, n_cols), F32, pltpu.HBM)] * 2
            scratch = [pltpu.VMEM((rank, rank), F32), pltpu.VMEM((rank, n_cols), F32)]
            scratch += [pltpu.SemaphoreType.DMA((2,)), pltpu.SemaphoreType.DMA((steps, 2))]
            return call(body, "finish", ins, results, scratch, {6: 1, 7: 2}, cost=(10**8, 8 * MIB))

        seen, pulls, own, other, part = first(right_init)
        base = [None, None]
        for step in range(ITERS):
            panel = sum_gal(part)
            inverse, own_wide, other_wide = sum_pix(panel, own, other)
            if step < ITERS - 1:
                given = inverse, panel, own_wide, seen, pulls
                base[0], own, part = middle(0, (0, 1), *given, None)
                given = inverse, panel, other_wide, seen, pulls, part
                base[1], other, away = middle(1, (0,), *given)
                base[1], other, mine = middle(1, (1,), *given, (base[1], *other))
                part = away + mine
            else:
                *wide, gram = widen(inverse, own_wide, other_wide)
                *made, left = final(0, inverse, panel, own_wide, base[0])
                bit = 1
                while 2 * bit < n_gal:
                    gram = add(gram, swap(gram, "gal", bit))
                    bit *= 2
                got = swap(gram, "gal", bit)
                *made, sparse, dual = final(1, inverse, panel, other_wide, base[1], made)
                right, sparse, dual = finish(gram, got, wide, made, (sparse, dual))
        return sparse, dual, left, right

    return jax.shard_map(
        per_device,
        mesh=mesh,
        in_specs=(P("pix", "gal"), P("pix", "gal"), P("pix", "gal"), P(None, "gal")),
        out_specs=(P("pix", "gal"), P("pix", "gal"), P(None, "pix"), P(None, "gal")),
        check_vma=False,
    )
```

```python
import jax
import jax.numpy as jnp
from jax import lax
from jax.experimental import pallas as pl
from jax.experimental.pallas import tpu as pltpu
from jax.sharding import PartitionSpec as P

ITERS = 2


MU = 1.25
TAU = 0.6 / 1.25
HIGH = lax.Precision.HIGHEST
CORES = 2
LANES = 128
F32, BF16 = jnp.float32, jnp.bfloat16
MIB = 1 << 20


def split(value):
    high = value.astype(BF16)
    return high, (value - high.astype(F32)).astype(BF16)


def dot(a, b, dims, precision=None):
    return lax.dot_general(a, b, (dims, ((), ())), precision=precision, preferred_element_type=F32)


def dot_nt(a, b):
    rows = a[0].shape[0]
    both = dot(jnp.concatenate(a, axis=0), b[0], ((1,), (1,)))
    return both[:rows] + both[rows:] + dot(a[0], b[1], ((1,), (1,)))


def dot_nn(a, b):
    rows = a[0].shape[0]
    both = dot(jnp.concatenate(a, axis=0), b[0], ((1,), (0,)))
    return both[:rows] + both[rows:] + dot(a[0], b[1], ((1,), (0,)))


def call(body, name, ins, outs, scratch=(), aliases=None, cost=(0, 0), limit=16):
    return pl.pallas_call(
        body,
        name=name,
        in_specs=[pl.BlockSpec(memory_space=space) for _, space in ins],
        out_specs=[pl.BlockSpec(memory_space=space) for _, _, space in outs],
        out_shape=[jax.ShapeDtypeStruct(shape, dtype) for shape, dtype, _ in outs],
        scratch_shapes=list(scratch),
        input_output_aliases=aliases or {},
        compiler_params=pltpu.CompilerParams(vmem_limit_bytes=limit * MIB),
        cost_estimate=pl.CostEstimate(flops=cost[0], bytes_accessed=cost[1], transcendentals=0),
    )(*[pltpu.with_memory_space_constraint(a, pltpu.HBM) if m is pltpu.HBM else a for a, m in ins])


def invert(packed, out):
    gram_rows, rank = packed.shape[0], out.shape[0]
    full = (8, LANES)
    lane = lax.broadcasted_iota(jnp.int32, full, 1)
    sub = lax.broadcasted_iota(jnp.int32, full, 0)
    turned = pltpu.roll(packed, LANES // 2, 1)
    rows = []
    for j in range(rank // 8):
        source = packed if 8 * j < gram_rows else turned
        at = 8 * j % gram_rows
        eye = jnp.where(lane - rank == sub + 8 * j, 1.0, 0.0)
        rows.append(jnp.where(lane < rank, source[at : at + 8], eye))
    wide = 8
    for k in range(0, rank, wide):
        r, at = divmod(k, 8)
        after = range(r if at + wide < 8 else r + 1, rank // 8)
        lines = [jnp.broadcast_to(rows[r][at + p : at + p + 1, :], full) for p in range(wide)]
        core = {
            (p, q): jnp.broadcast_to(lines[p][:, k + q : k + q + 1], full)
            for p in range(wide)
            for q in range(p, wide)
        }
        columns = {
            (j, p): jnp.broadcast_to(rows[j][:, k + p : k + p + 1], full) for j in after for p in range(wide)
        }
        for p in range(wide):
            inverse = 1.0 / core[p, p]
            factors = [core[p, q] * inverse for q in range(p + 1, wide)]
            for q, factor in zip(range(p + 1, wide), factors):
                for t in range(q, wide):
                    core[q, t] = core[q, t] - factor * core[p, t]
            scaled = lines[p] * inverse
            for q in range(p + 1, wide):
                lines[q] = lines[q] - core[p, q] * scaled
            for j in after:
                column = columns[j, p]
                if j == r:
                    column = jnp.where(sub >= at + wide, column, 0.0)
                rows[j] = rows[j] - column * scaled
                for q, factor in zip(range(p + 1, wide), factors):
                    columns[j, q] = columns[j, q] - factor * columns[j, p]
            done = lines[p] * lax.rsqrt(core[p, p])
            out[k + p : k + p + 1, :] = done[0:1, rank:]


def pack(gram):
    rows = gram.shape[0] // 2
    return jnp.concatenate([gram[:rows], gram[rows:]], axis=1)


def unstack(ref):
    blocks = ref.shape[0] // 64
    return jnp.concatenate([ref[64 * t : 64 * (t + 1), :] for t in range(blocks)], axis=1)


def solution(mesh):
    n_gal, n_pix = mesh.shape["gal"], mesh.shape["pix"]
    levels = n_pix.bit_length() - 1

    def swap(value, axis, bit):
        n = mesh.shape[axis]
        return lax.ppermute(value, axis, [(i, i ^ bit) for i in range(n)])

    def per_device(observed, sparse_init, dual_init, right_init):
        rank = right_init.shape[0]
        n_rows, n_cols = observed.shape
        half = n_cols // 2
        tall = min(256, n_rows // 2)
        steps = n_rows // tall
        quarter = rank * (half // LANES) // 2
        gram_rows = rank * rank // LANES

        def place():
            pix = lax.axis_index("pix")
            return [lax.rem(lax.axis_index("gal"), CORES)] + [lax.rem(pix >> level, 2) for level in range(levels)]

        def gal_at(i, s):
            turn = (1 - s[0]) * (steps // 2)
            return pl.multiple_of(lax.rem(i + turn, steps) * tall, tall)

        def pix_at(p, s):
            return pl.multiple_of(lax.rem(s[1] + p, 2) * half, half)

        def chunk(i):
            return slice(tall * i, tall * (i + 1))

        def join(pair):
            return jnp.concatenate([half[...] for half in pair], axis=1)

        def small(body, name, ins, rows, scratch=()):
            outs = [((n, LANES), F32, pltpu.VMEM) for n in rows]
            return call(body, name, ins, outs, scratch, cost=(10**5, 10**6), limit=4)

        def add(*arrays):
            def body(*refs):
                *ins, out = refs
                total = ins[0][...]
                for ref in ins[1:]:
                    total = total + ref[...]
                out[...] = total

            out = (arrays[0].shape, F32, pltpu.VMEM)
            return call(body, "add", [(a, pltpu.VMEM) for a in arrays], [out], cost=(10**5, 10**6), limit=4)[0]

        def first(right):
            def body(o_in, s_in, d_in, r_in, o, u, h0, l0, h1, l1, away, mine, sp, d, right, r_sem, sems):
                s = place()
                right_move = pltpu.make_async_copy(r_in, right, r_sem)
                right_move.start()
                moves = {}
                for i in range(steps):
                    for a, (source, target) in enumerate(((o_in, o), (s_in, sp), (d_in, d))):
                        block = source.at[pl.ds(gal_at(i, s), tall), :]
                        move = pltpu.make_async_copy(block, target.at[chunk(i), :], sems.at[i, a])
                        move.start(priority=(i + a) % 2)
                        moves[i, a] = move
                right_move.wait()
                rights = [split(right[:, pl.ds(pix_at(p, s), half)]) for p in (0, 1)]
                for i in range(steps):
                    total = None
                    for a in range(3):
                        moves[i, a].wait()
                    for p, (h, l) in enumerate(((h0, l0), (h1, l1))):
                        at = chunk(i), pl.ds(pix_at(p, s), half)
                        pulled = o[at] + d[at] * (1 / MU)
                        u[at] = pulled
                        pair = split(pulled - sp[at])
                        h[chunk(i), :], l[chunk(i), :] = pair
                        term = dot_nt(rights[p], pair)
                        total = term if total is None else total + term
                    out = away if i < steps // 2 else mine
                    out[:, chunk(i % (steps // 2))] = total

            ins = [(a, pltpu.HBM) for a in (observed, sparse_init, dual_init, right)]
            outs = [((n_rows, n_cols), F32, pltpu.VMEM)] * 2 + [((n_rows, half), BF16, pltpu.VMEM)] * 4
            outs += [((rank, n_rows // 2), F32, pltpu.VMEM)] * 2
            scratch = [pltpu.VMEM((n_rows, n_cols), F32)] * 2 + [pltpu.VMEM((rank, n_cols), F32)]
            scratch += [pltpu.SemaphoreType.DMA(()), pltpu.SemaphoreType.DMA((steps, 3))]
            cost = (6 * rank * n_rows * n_cols, 16 * n_rows * n_cols)
            got = call(body, "first", ins, outs, scratch, cost=cost)
            return got[0], got[1], got[2:4], got[4:6], got[6:8]

        def sum_gal(part):
            away, mine = part
            mine = add(mine, swap(away, "gal", 1))
            got = [
                lax.ppermute(mine, "gal", [(i, (i + CORES * k) % n_gal) for i in range(n_gal)])
                for k in range(1, n_gal // CORES)
            ]
            mine = add(mine, *got)
            return swap(mine, "gal", 1), mine

        def multiply_mine(mine, pair, other_pair):
            def body(mine, high, low, high_other, low_other, own, other, gram):
                panel = split(mine[...])
                for at, out in (((high, low), own), ((high_other, low_other), other)):
                    put_stack(dot_nn(panel, [ref[n_rows // 2 :, :] for ref in at]), out)
                gram[...] = pack(dot(mine[...], mine[...], ((1,), (1,)), HIGH))

            ins = [(a, pltpu.VMEM) for a in (mine, *pair, *other_pair)]
            outs = [((rows, LANES), F32, pltpu.VMEM) for rows in (2 * quarter, 2 * quarter, gram_rows)]
            cost = (3 * rank * n_rows * n_cols, 2 * n_rows * n_cols)
            return call(body, "multiply_mine", ins, outs, cost=cost)

        def multiply_other(away, pair, before, gram):
            def body(away, high, low, before, gram, straight, across, stack):
                s = place()
                pairs = [ref[: n_rows // 2, :] for ref in (high, low)]
                put_stack(dot_nn(split(away[...]), pairs), stack)
                total = gram[...] + pack(dot(away[...], away[...], ((1,), (1,)), HIGH))
                for side, out in ((s[2], straight), (1 - s[2], across)):
                    out[:quarter, :] = stack[rows_at(side), :] + before[rows_at(side), :]
                    out[quarter:, :] = total

            ins = [(a, pltpu.VMEM) for a in (away, *pair, before, gram)]
            outs = [((quarter + gram_rows, LANES), F32, pltpu.VMEM)] * 2
            cost = (2 * rank * n_rows * n_cols, n_rows * n_cols)
            return call(body, "multiply_other", ins, outs, [pltpu.VMEM((2 * quarter, LANES), F32)], cost=cost)

        def multiply_own(away, pair, before, sent):
            def body(away, high, low, before, sent, keep, out, stack):
                s = place()
                pairs = [ref[: n_rows // 2, :] for ref in (high, low)]
                put_stack(dot_nn(split(away[...]), pairs), stack)
                for side, ref in ((s[2], keep), (1 - s[2], out)):
                    ref[:quarter, :] = stack[rows_at(side), :] + before[rows_at(side), :]
                out[quarter:, :] = sent[quarter:, :]

            ins = [(a, pltpu.VMEM) for a in (away, *pair, before, sent)]
            outs = [((rows, LANES), F32, pltpu.VMEM) for rows in (quarter, quarter + gram_rows)]
            cost = (10**9, 8 * MIB)
            return call(body, "multiply_own", ins, outs, [pltpu.VMEM((2 * quarter, LANES), F32)], cost=cost)

        def put_stack(value, stack):
            for t in range(half // LANES):
                stack[rank * t : rank * (t + 1), :] = value[:, LANES * t : LANES * (t + 1)]

        def rows_at(side):
            return pl.ds(pl.multiple_of(side * quarter, quarter), quarter)

        def eliminate(one, two):
            def body(one, two, out):
                invert(one[-gram_rows:, :] + two[-gram_rows:, :], out)

            ins = [(one, pltpu.VMEM), (two, pltpu.VMEM)]
            outs = [((rank, rank), F32, pltpu.VMEM)]
            return call(body, "eliminate", ins, outs, cost=(10**8, 8 * MIB), limit=4)[0]

        def collect(keep, sent, gots):
            rows = keep.shape[0]

            def body(keep, sent, *refs):
                *gots, out = refs
                top, low = keep[...], sent[rows:, :]
                for got in gots:
                    top, low = top + got[:rows, :], low + got[rows:, :]
                out[:rows, :] = top
                out[rows:, :] = low

            ins = [(a, pltpu.VMEM) for a in (keep, sent, *gots)]
            return small(body, "collect", ins, [rows + gram_rows])[0]

        def divide(level, total):
            rows = (total.shape[0] - gram_rows) // 2

            def body(total, keep, out):
                s = place()
                for side, ref in ((s[1 + level], keep), (1 - s[1 + level], out)):
                    ref[:rows, :] = total[pl.ds(pl.multiple_of(side * rows, rows), rows), :]
                out[rows:, :] = total[2 * rows :, :]

            return small(body, "divide", [(total, pltpu.VMEM)], [rows, rows + gram_rows])

        def unfold(level, value, got):
            rows = value.shape[0]

            def body(value, got, out):
                s = place()
                for side, ref in ((s[1 + level], value), (1 - s[1 + level], got)):
                    out[pl.ds(pl.multiple_of(side * rows, rows), rows), :] = ref[...]

            ins = [(value, pltpu.VMEM), (got, pltpu.VMEM)]
            return small(body, "unfold", ins, [2 * rows])[0]

        def top(one, two):
            rows = one.shape[0] - gram_rows

            def body(one, two, out):
                out[...] = one[:rows, :] + two[:rows, :]

            return small(body, "top", [(one, pltpu.VMEM), (two, pltpu.VMEM)], [rows])[0]

        def sum_pix(panel, own, other):
            away, mine = panel
            own_before, other_before, gram = multiply_mine(mine, own, other)
            straight, across = multiply_other(away, other, other_before, gram)
            gots = [swap(straight, "pix", 1), swap(across, "pix", 3)]
            keep, beside = multiply_own(away, own, own_before, straight)
            total = collect(keep, straight, gots + [swap(beside, "pix", 2)])
            for level in range(2, levels - 1):
                keep, sent = divide(level, total)
                total = collect(keep, sent, [swap(sent, "pix", 1 << level)])
            got = swap(total, "pix", 1 << (levels - 1))
            value = top(total, got)
            inverse = eliminate(total, got)
            for level in range(levels - 2, 1, -1):
                value = unfold(level, value, swap(value, "pix", 1 << level))
            beside, straight, across = [swap(value, "pix", bit) for bit in (2, 1, 3)]
            return inverse, unfold(1, value, beside), unfold(1, straight, across)

        def tops_of(inverse, panel):
            left = dot(inverse[...], join(panel), ((1,), (0,)), HIGH)
            high, low = split(left)
            return left, jnp.concatenate([high, low, high], axis=0)

        def wides_of(inverse, stacked):
            high, low = split(dot(inverse[...], unstack(stacked), ((1,), (0,)), HIGH))
            return (high, low), jnp.concatenate([high, high, low], axis=0)

        tops_out = (3 * rank, n_rows), BF16, pltpu.VMEM

        def middle(p, sides, inverse, left, stacked, o, u, before, arrays=()):
            n = len(sides)
            blocks = [i for i in range(steps) if i // (steps // 2) in sides]
            lefts = [left] if p else list(left)

            def body(inverse, *rest):
                s = place()
                panel, (stacked, o, u, *rest) = rest[: len(lefts)], rest[len(lefts) :]
                base, high, low, *after = rest[n * p + len(arrays) :]
                if p:
                    tops = panel[0]
                else:
                    tops = after[n]
                    tops[...] = tops_of(inverse, panel)[1]
                right, wides = wides_of(inverse, stacked)
                for k, i in enumerate(blocks):
                    lowrank = dot(tops[:, chunk(i)], wides, ((0,), (0,)))
                    at = chunk(i), pl.ds(pix_at(p, s), half)
                    value = u[at] - lowrank
                    scaled = jnp.clip(value, -TAU, TAU)
                    moved = o[at] + scaled
                    base[chunk(i), :] = moved
                    pair = split(moved + (scaled - value))
                    high[chunk(i), :], low[chunk(i), :] = pair
                    term = dot_nt(right, pair)
                    side, block = divmod(k, steps // 2)
                    after[side][:, chunk(block)] = rest[side][:, chunk(block)] + term if p else term

            ins = [inverse, *lefts, stacked, o, u]
            ins += [before[side] for side in sides] if p else []
            aliases = {len(ins) + k: k for k in range(len(arrays))}
            outs = [((n_rows, half), F32, pltpu.VMEM)] + [((n_rows, half), BF16, pltpu.VMEM)] * 2
            outs += [((rank, n_rows // 2), F32, pltpu.VMEM)] * n + [tops_out] * (1 - p)
            cost = (9 * rank * n_rows * n_cols // (3 - n), 4 * n_rows * n_cols // (3 - n))
            ins = [(a, pltpu.VMEM) for a in (*ins, *arrays)]
            base, high, low, *rest = call(body, "middle", ins, outs, aliases=aliases, cost=cost)
            return base, (high, low), *((rest,) if p else (rest[:n], rest[n]))

        def put(sources, targets, p, s, sems):
            def moves(i):
                for a, (source, target) in enumerate(zip(sources, targets)):
                    block = target.at[pl.ds(gal_at(i, s), tall), pl.ds(pix_at(p, s), half)]
                    rows = pl.ds(pl.multiple_of(i * tall, tall), tall)
                    yield pltpu.make_async_copy(source.at[rows, :], block, sems.at[i, a])

            def start(i, carry):
                for a, move in enumerate(moves(i)):
                    move.start(priority=a)
                return carry

            lax.fori_loop(0, steps, start, 0)
            return [move for i in range(steps) for move in moves(i)]

        def final(p, inverse, left, stacked, base, before=()):
            lefts = [left] if p else list(left)

            def body(inverse, *rest):
                s = place()
                panel, (stacked, base, *rest) = rest[: len(lefts)], rest[len(lefts) :]
                sparse, dual, *outs, left_part, sems = rest[len(before) :]
                if p:
                    moves = put(rest[:1], outs, 0, s, sems)
                    tops = panel[0]
                else:
                    value, stack = tops_of(inverse, panel)
                    tops = outs[1]
                    tops[...] = stack
                    for i in range(steps):
                        left_part[:, pl.ds(gal_at(i, s), tall)] = value[:, chunk(i)]
                    moves = [pltpu.make_async_copy(left_part, outs[0], sems.at[0, 0])]
                    moves[0].start()
                _, wides = wides_of(inverse, stacked)
                for i in range(steps):
                    value = base[chunk(i), :] - dot(tops[:, chunk(i)], wides, ((0,), (0,)))
                    scaled = jnp.clip(value, -TAU, TAU)
                    sparse[chunk(i), :] = value - scaled
                    dual[chunk(i), :] = MU * scaled
                for move in moves:
                    move.wait()

            ins = [(a, pltpu.VMEM) for a in (inverse, *lefts, stacked, base, *before)]
            outs = [((n_rows, half), F32, pltpu.VMEM)] * 2
            if p:
                outs += [((n_rows, n_cols), F32, pltpu.HBM)]
            else:
                outs += [((rank, n_rows), F32, pltpu.HBM), tops_out]
            scratch = [pltpu.VMEM((rank, n_rows), F32), pltpu.SemaphoreType.DMA((steps, 1))]
            cost = (3 * rank * n_rows * n_cols, 4 * n_rows * n_cols)
            return call(body, "final", ins, outs, scratch, cost=cost)

        def widen(inverse, own, other):
            def body(inverse, own, other, wide_own, wide_other, out):
                grams = []
                for stacked, wide in ((own, wide_own), (other, wide_other)):
                    value = dot(inverse[...], unstack(stacked), ((1,), (0,)), HIGH)
                    wide[...] = value
                    grams.append(dot(value, value, ((1,), (1,)), HIGH))
                out[...] = pack(grams[0] + grams[1])

            ins = [(a, pltpu.VMEM) for a in (inverse, own, other)]
            outs = [((rank, half), F32, pltpu.VMEM)] * 2 + [((gram_rows, LANES), F32, pltpu.VMEM)]
            return call(body, "widen", ins, outs, cost=(10**8, MIB), limit=8)

        def finish(one, two, wide, made, first_dual, sparse):
            def body(*refs):
                one, two, own, other, sparse_1, dual_1, dual_0, _ = refs[:8]
                out, sparse_out, dual_out, inverse, right, sem, sems, dual_sems = refs[8:]
                s = place()
                moves = put((sparse_1, dual_1), (sparse_out, dual_out), 1, s, sems)
                moves += put((dual_0,), (dual_out,), 0, s, dual_sems)
                invert(one[...] + two[...], inverse)
                for p, value in enumerate((own, other)):
                    at = pl.ds(pix_at(p, s), half)
                    right[:, at] = dot(inverse[...], value[...], ((1,), (0,)), HIGH)
                    move = pltpu.make_async_copy(right.at[:, at], out.at[:, at], sem.at[p])
                    move.start()
                    moves.append(move)
                for move in moves:
                    move.wait()

            ins = [(a, pltpu.VMEM) for a in (one, two, *wide, *made, first_dual)] + [(sparse, pltpu.HBM)]
            results = [((rank, n_cols), F32, pltpu.HBM)] + [((n_rows, n_cols), F32, pltpu.HBM)] * 2
            scratch = [pltpu.VMEM((rank, rank), F32), pltpu.VMEM((rank, n_cols), F32)]
            scratch += [pltpu.SemaphoreType.DMA(shape) for shape in ((2,), (steps, 2), (steps, 1))]
            return call(body, "finish", ins, results, scratch, {7: 1}, cost=(10**8, 8 * MIB))

        seen, pulls, own, other, part = first(right_init)
        base = [None, None]
        for step in range(ITERS):
            panel = sum_gal(part)
            inverse, own_wide, other_wide = sum_pix(panel, own, other)
            if step < ITERS - 1:
                given = own_wide, seen, pulls
                base[0], own, part, tops = middle(0, (0, 1), inverse, panel, *given, None)
                given = inverse, tops, other_wide, seen, pulls, part
                base[1], other, away = middle(1, (0,), *given)
                base[1], other, mine = middle(1, (1,), *given, (base[1], *other))
                part = away + mine
            else:
                *wide, gram = widen(inverse, own_wide, other_wide)
                *made, left, tops = final(0, inverse, panel, own_wide, base[0])
                bit = 1
                while 2 * bit < n_gal:
                    gram = add(gram, swap(gram, "gal", bit))
                    bit *= 2
                got = swap(gram, "gal", bit)
                *later, sparse = final(1, inverse, tops, other_wide, base[1], made[:1])
                right, sparse, dual = finish(gram, got, wide, later, made[1], sparse)
        return sparse, dual, left, right

    return jax.shard_map(
        per_device,
        mesh=mesh,
        in_specs=(P("pix", "gal"), P("pix", "gal"), P("pix", "gal"), P(None, "gal")),
        out_specs=(P("pix", "gal"), P("pix", "gal"), P(None, "pix"), P(None, "gal")),
        check_vma=False,
    )
```

```python
import jax
import jax.numpy as jnp
from jax import lax
from jax.experimental import pallas as pl
from jax.experimental.pallas import tpu as pltpu
from jax.sharding import PartitionSpec as P

ITERS = 2


MU = 1.25
TAU = 0.6 / 1.25
HIGH = lax.Precision.HIGHEST
CORES = 2
LANES = 128
F32, BF16 = jnp.float32, jnp.bfloat16
MIB = 1 << 20


def split(value):
    high = value.astype(BF16)
    return high, (value - high.astype(F32)).astype(BF16)


def dot(a, b, dims, precision=None):
    return lax.dot_general(a, b, (dims, ((), ())), precision=precision, preferred_element_type=F32)


def dot_nt(a, b):
    rows = a[0].shape[0]
    both = dot(jnp.concatenate(a, axis=0), b[0], ((1,), (1,)))
    return both[:rows] + both[rows:] + dot(a[0], b[1], ((1,), (1,)))


def dot_nn(a, b):
    rows = a[0].shape[0]
    both = dot(jnp.concatenate(a, axis=0), b[0], ((1,), (0,)))
    return both[:rows] + both[rows:] + dot(a[0], b[1], ((1,), (0,)))


def call(body, name, ins, outs, scratch=(), aliases=None, cost=(0, 0), limit=16):
    return pl.pallas_call(
        body,
        name=name,
        in_specs=[pl.BlockSpec(memory_space=space) for _, space in ins],
        out_specs=[pl.BlockSpec(memory_space=space) for _, _, space in outs],
        out_shape=[jax.ShapeDtypeStruct(shape, dtype) for shape, dtype, _ in outs],
        scratch_shapes=list(scratch),
        input_output_aliases=aliases or {},
        compiler_params=pltpu.CompilerParams(vmem_limit_bytes=limit * MIB),
        cost_estimate=pl.CostEstimate(flops=cost[0], bytes_accessed=cost[1], transcendentals=0),
    )(*[pltpu.with_memory_space_constraint(a, pltpu.HBM) if m is pltpu.HBM else a for a, m in ins])


def invert(packed, out):
    gram_rows, rank = packed.shape[0], out.shape[0]
    full = (8, LANES)
    lane = lax.broadcasted_iota(jnp.int32, full, 1)
    sub = lax.broadcasted_iota(jnp.int32, full, 0)
    turned = pltpu.roll(packed, LANES // 2, 1)
    rows = []
    for j in range(rank // 8):
        source = packed if 8 * j < gram_rows else turned
        at = 8 * j % gram_rows
        eye = jnp.where(lane - rank == sub + 8 * j, 1.0, 0.0)
        rows.append(jnp.where(lane < rank, source[at : at + 8], eye))
    wide = 8
    for k in range(0, rank, wide):
        r, at = divmod(k, 8)
        after = range(r if at + wide < 8 else r + 1, rank // 8)
        lines = [jnp.broadcast_to(rows[r][at + p : at + p + 1, :], full) for p in range(wide)]
        core = {
            (p, q): jnp.broadcast_to(lines[p][:, k + q : k + q + 1], full)
            for p in range(wide)
            for q in range(p, wide)
        }
        columns = {
            (j, p): jnp.broadcast_to(rows[j][:, k + p : k + p + 1], full) for j in after for p in range(wide)
        }
        for p in range(wide):
            inverse = 1.0 / core[p, p]
            factors = [core[p, q] * inverse for q in range(p + 1, wide)]
            for q, factor in zip(range(p + 1, wide), factors):
                for t in range(q, wide):
                    core[q, t] = core[q, t] - factor * core[p, t]
            scaled = lines[p] * inverse
            for q in range(p + 1, wide):
                lines[q] = lines[q] - core[p, q] * scaled
            for j in after:
                column = columns[j, p]
                if j == r:
                    column = jnp.where(sub >= at + wide, column, 0.0)
                rows[j] = rows[j] - column * scaled
                for q, factor in zip(range(p + 1, wide), factors):
                    columns[j, q] = columns[j, q] - factor * columns[j, p]
            done = lines[p] * lax.rsqrt(core[p, p])
            out[k + p : k + p + 1, :] = done[0:1, rank:]


def pack(gram):
    rows = gram.shape[0] // 2
    return jnp.concatenate([gram[:rows], gram[rows:]], axis=1)


def unstack(ref):
    blocks = ref.shape[0] // 64
    return jnp.concatenate([ref[64 * t : 64 * (t + 1), :] for t in range(blocks)], axis=1)


def solution(mesh):
    n_gal, n_pix = mesh.shape["gal"], mesh.shape["pix"]
    levels = n_pix.bit_length() - 1

    def swap(value, axis, bit):
        n = mesh.shape[axis]
        return lax.ppermute(value, axis, [(i, i ^ bit) for i in range(n)])

    def per_device(observed, sparse_init, dual_init, right_init):
        rank = right_init.shape[0]
        n_rows, n_cols = observed.shape
        half = n_cols // 2
        tall = min(256, n_rows // 2)
        steps = n_rows // tall
        quarter = rank * (half // LANES) // 2
        gram_rows = rank * rank // LANES

        def place():
            pix = lax.axis_index("pix")
            return [lax.rem(lax.axis_index("gal"), CORES)] + [lax.rem(pix >> level, 2) for level in range(levels)]

        def gal_at(i, s):
            turn = (1 - s[0]) * (steps // 2)
            return pl.multiple_of(lax.rem(i + turn, steps) * tall, tall)

        def pix_at(p, s):
            return pl.multiple_of(lax.rem(s[1] + p, 2) * half, half)

        def chunk(i):
            return slice(tall * i, tall * (i + 1))

        def join(pair):
            return jnp.concatenate([half[...] for half in pair], axis=1)

        def small(body, name, ins, rows, scratch=()):
            outs = [((n, LANES), F32, pltpu.VMEM) for n in rows]
            return call(body, name, ins, outs, scratch, cost=(10**5, 10**6), limit=4)

        def add(*arrays):
            def body(*refs):
                *ins, out = refs
                total = ins[0][...]
                for ref in ins[1:]:
                    total = total + ref[...]
                out[...] = total

            out = (arrays[0].shape, F32, pltpu.VMEM)
            return call(body, "add", [(a, pltpu.VMEM) for a in arrays], [out], cost=(10**5, 10**6), limit=4)[0]

        def first(right):
            def body(o_in, s_in, d_in, r_in, o, u, h0, l0, h1, l1, away, mine, sp, d, right, r_sem, sems):
                s = place()
                right_move = pltpu.make_async_copy(r_in, right, r_sem)
                right_move.start()
                moves = {}
                for i in range(steps):
                    for a, (source, target) in enumerate(((o_in, o), (s_in, sp), (d_in, d))):
                        block = source.at[pl.ds(gal_at(i, s), tall), :]
                        move = pltpu.make_async_copy(block, target.at[chunk(i), :], sems.at[i, a])
                        move.start(priority=(i + a) % 2)
                        moves[i, a] = move
                right_move.wait()
                rights = [split(right[:, pl.ds(pix_at(p, s), half)]) for p in (0, 1)]
                for i in range(steps):
                    total = None
                    for a in range(3):
                        moves[i, a].wait()
                    for p, (h, l) in enumerate(((h0, l0), (h1, l1))):
                        at = chunk(i), pl.ds(pix_at(p, s), half)
                        pulled = o[at] + d[at] * (1 / MU)
                        u[at] = pulled
                        pair = split(pulled - sp[at])
                        h[chunk(i), :], l[chunk(i), :] = pair
                        term = dot_nt(rights[p], pair)
                        total = term if total is None else total + term
                    out = away if i < steps // 2 else mine
                    out[:, chunk(i % (steps // 2))] = total

            ins = [(a, pltpu.HBM) for a in (observed, sparse_init, dual_init, right)]
            outs = [((n_rows, n_cols), F32, pltpu.VMEM)] * 2 + [((n_rows, half), BF16, pltpu.VMEM)] * 4
            outs += [((rank, n_rows // 2), F32, pltpu.VMEM)] * 2
            scratch = [pltpu.VMEM((n_rows, n_cols), F32)] * 2 + [pltpu.VMEM((rank, n_cols), F32)]
            scratch += [pltpu.SemaphoreType.DMA(()), pltpu.SemaphoreType.DMA((steps, 3))]
            cost = (6 * rank * n_rows * n_cols, 16 * n_rows * n_cols)
            got = call(body, "first", ins, outs, scratch, cost=cost)
            return got[0], got[1], got[2:4], got[4:6], got[6:8]

        def sum_gal(part):
            away, mine = part
            mine = add(mine, swap(away, "gal", 1))
            got = [
                lax.ppermute(mine, "gal", [(i, (i + CORES * k) % n_gal) for i in range(n_gal)])
                for k in range(1, n_gal // CORES)
            ]
            mine = add(mine, *got)
            return swap(mine, "gal", 1), mine

        def multiply_mine(mine, pair, other_pair):
            def body(mine, high, low, high_other, low_other, own, other, gram):
                panel = split(mine[...])
                for at, out in (((high, low), own), ((high_other, low_other), other)):
                    put_stack(dot_nn(panel, [ref[n_rows // 2 :, :] for ref in at]), out)
                gram[...] = pack(dot(mine[...], mine[...], ((1,), (1,)), HIGH))

            ins = [(a, pltpu.VMEM) for a in (mine, *pair, *other_pair)]
            outs = [((rows, LANES), F32, pltpu.VMEM) for rows in (2 * quarter, 2 * quarter, gram_rows)]
            cost = (3 * rank * n_rows * n_cols, 2 * n_rows * n_cols)
            return call(body, "multiply_mine", ins, outs, cost=cost)

        def multiply_other(away, pair, before, gram):
            def body(away, high, low, before, gram, straight, across, stack):
                s = place()
                pairs = [ref[: n_rows // 2, :] for ref in (high, low)]
                put_stack(dot_nn(split(away[...]), pairs), stack)
                total = gram[...] + pack(dot(away[...], away[...], ((1,), (1,)), HIGH))
                for side, out in ((s[2], straight), (1 - s[2], across)):
                    out[:quarter, :] = stack[rows_at(side), :] + before[rows_at(side), :]
                    out[quarter:, :] = total

            ins = [(a, pltpu.VMEM) for a in (away, *pair, before, gram)]
            outs = [((quarter + gram_rows, LANES), F32, pltpu.VMEM)] * 2
            cost = (2 * rank * n_rows * n_cols, n_rows * n_cols)
            return call(body, "multiply_other", ins, outs, [pltpu.VMEM((2 * quarter, LANES), F32)], cost=cost)

        def multiply_own(away, pair, before, sent):
            def body(away, high, low, before, sent, keep, out, stack):
                s = place()
                pairs = [ref[: n_rows // 2, :] for ref in (high, low)]
                put_stack(dot_nn(split(away[...]), pairs), stack)
                for side, ref in ((s[2], keep), (1 - s[2], out)):
                    ref[:quarter, :] = stack[rows_at(side), :] + before[rows_at(side), :]
                out[quarter:, :] = sent[quarter:, :]

            ins = [(a, pltpu.VMEM) for a in (away, *pair, before, sent)]
            outs = [((rows, LANES), F32, pltpu.VMEM) for rows in (quarter, quarter + gram_rows)]
            cost = (10**9, 8 * MIB)
            return call(body, "multiply_own", ins, outs, [pltpu.VMEM((2 * quarter, LANES), F32)], cost=cost)

        def put_stack(value, stack):
            for t in range(half // LANES):
                stack[rank * t : rank * (t + 1), :] = value[:, LANES * t : LANES * (t + 1)]

        def rows_at(side):
            return pl.ds(pl.multiple_of(side * quarter, quarter), quarter)

        def eliminate(one, two):
            def body(one, two, out):
                invert(one[-gram_rows:, :] + two[-gram_rows:, :], out)

            ins = [(one, pltpu.VMEM), (two, pltpu.VMEM)]
            outs = [((rank, rank), F32, pltpu.VMEM)]
            return call(body, "eliminate", ins, outs, cost=(10**8, 8 * MIB), limit=4)[0]

        def collect(keep, sent, gots):
            rows = keep.shape[0]

            def body(keep, sent, *refs):
                *gots, out = refs
                top, low = keep[...], sent[rows:, :]
                for got in gots:
                    top, low = top + got[:rows, :], low + got[rows:, :]
                out[:rows, :] = top
                out[rows:, :] = low

            ins = [(a, pltpu.VMEM) for a in (keep, sent, *gots)]
            return small(body, "collect", ins, [rows + gram_rows])[0]

        def divide(level, total):
            rows = (total.shape[0] - gram_rows) // 2

            def body(total, keep, out):
                s = place()
                for side, ref in ((s[1 + level], keep), (1 - s[1 + level], out)):
                    ref[:rows, :] = total[pl.ds(pl.multiple_of(side * rows, rows), rows), :]
                out[rows:, :] = total[2 * rows :, :]

            return small(body, "divide", [(total, pltpu.VMEM)], [rows, rows + gram_rows])

        def unfold(level, value, got):
            rows = value.shape[0]

            def body(value, got, out):
                s = place()
                for side, ref in ((s[1 + level], value), (1 - s[1 + level], got)):
                    out[pl.ds(pl.multiple_of(side * rows, rows), rows), :] = ref[...]

            ins = [(value, pltpu.VMEM), (got, pltpu.VMEM)]
            return small(body, "unfold", ins, [2 * rows])[0]

        def top(one, two):
            rows = one.shape[0] - gram_rows

            def body(one, two, out):
                out[...] = one[:rows, :] + two[:rows, :]

            return small(body, "top", [(one, pltpu.VMEM), (two, pltpu.VMEM)], [rows])[0]

        def sum_pix(panel, own, other):
            away, mine = panel
            own_before, other_before, gram = multiply_mine(mine, own, other)
            straight, across = multiply_other(away, other, other_before, gram)
            gots = [swap(straight, "pix", 1), swap(across, "pix", 3)]
            keep, beside = multiply_own(away, own, own_before, straight)
            total = collect(keep, straight, gots + [swap(beside, "pix", 2)])
            for level in range(2, levels - 1):
                keep, sent = divide(level, total)
                total = collect(keep, sent, [swap(sent, "pix", 1 << level)])
            got = swap(total, "pix", 1 << (levels - 1))
            value = top(total, got)
            inverse = eliminate(total, got)
            for level in range(levels - 2, 1, -1):
                value = unfold(level, value, swap(value, "pix", 1 << level))
            beside, straight, across = [swap(value, "pix", bit) for bit in (2, 1, 3)]
            return inverse, unfold(1, value, beside), (straight, across)

        def tops_of(inverse, panel):
            left = dot(inverse[...], join(panel), ((1,), (0,)), HIGH)
            high, low = split(left)
            return left, jnp.concatenate([high, low, high], axis=0)

        def wides_of(inverse, stacked):
            high, low = split(dot(inverse[...], unstack(stacked), ((1,), (0,)), HIGH))
            return (high, low), jnp.concatenate([high, high, low], axis=0)

        tops_out = (3 * rank, n_rows), BF16, pltpu.VMEM

        def middle(p, sides, inverse, left, stacked, o, u, before, arrays=()):
            n = len(sides)
            blocks = [i for i in range(steps) if i // (steps // 2) in sides]
            lefts = [left] if p else list(left)

            def body(inverse, *rest):
                s = place()
                panel, (stacked, o, u, *rest) = rest[: len(lefts)], rest[len(lefts) :]
                base, high, low, *after = rest[n * p + len(arrays) :]
                if p:
                    tops = panel[0]
                else:
                    tops = after[n]
                    tops[...] = tops_of(inverse, panel)[1]
                right, wides = wides_of(inverse, stacked)
                for k, i in enumerate(blocks):
                    lowrank = dot(tops[:, chunk(i)], wides, ((0,), (0,)))
                    at = chunk(i), pl.ds(pix_at(p, s), half)
                    value = u[at] - lowrank
                    scaled = jnp.clip(value, -TAU, TAU)
                    moved = o[at] + scaled
                    base[chunk(i), :] = moved
                    pair = split(moved + (scaled - value))
                    high[chunk(i), :], low[chunk(i), :] = pair
                    term = dot_nt(right, pair)
                    side, block = divmod(k, steps // 2)
                    after[side][:, chunk(block)] = rest[side][:, chunk(block)] + term if p else term

            ins = [inverse, *lefts, stacked, o, u]
            ins += [before[side] for side in sides] if p else []
            aliases = {len(ins) + k: k for k in range(len(arrays))}
            outs = [((n_rows, half), F32, pltpu.VMEM)] + [((n_rows, half), BF16, pltpu.VMEM)] * 2
            outs += [((rank, n_rows // 2), F32, pltpu.VMEM)] * n + [tops_out] * (1 - p)
            cost = (9 * rank * n_rows * n_cols // (3 - n), 4 * n_rows * n_cols // (3 - n))
            ins = [(a, pltpu.VMEM) for a in (*ins, *arrays)]
            base, high, low, *rest = call(body, "middle", ins, outs, aliases=aliases, cost=cost)
            return base, (high, low), *((rest,) if p else (rest[:n], rest[n]))

        def put(sources, targets, p, s, sems):
            def moves(i):
                for a, (source, target) in enumerate(zip(sources, targets)):
                    block = target.at[pl.ds(gal_at(i, s), tall), pl.ds(pix_at(p, s), half)]
                    rows = pl.ds(pl.multiple_of(i * tall, tall), tall)
                    yield pltpu.make_async_copy(source.at[rows, :], block, sems.at[i, a])

            def start(i, carry):
                for a, move in enumerate(moves(i)):
                    move.start(priority=a)
                return carry

            lax.fori_loop(0, steps, start, 0)
            return [move for i in range(steps) for move in moves(i)]

        def final(p, inverse, left, stacked, base, before=()):
            lefts = [left] if p else list(left)

            def body(inverse, *rest):
                s = place()
                panel, (stacked, base, *rest) = rest[: len(lefts)], rest[len(lefts) :]
                sparse, dual, *outs, left_part, sems = rest[len(before) :]
                if p:
                    moves = put(rest[:1], outs, 0, s, sems)
                    tops = panel[0]
                else:
                    value, stack = tops_of(inverse, panel)
                    tops = outs[1]
                    tops[...] = stack
                    for i in range(steps):
                        left_part[:, pl.ds(gal_at(i, s), tall)] = value[:, chunk(i)]
                    moves = [pltpu.make_async_copy(left_part, outs[0], sems.at[0, 0])]
                    moves[0].start()
                _, wides = wides_of(inverse, stacked)
                for i in range(steps):
                    value = base[chunk(i), :] - dot(tops[:, chunk(i)], wides, ((0,), (0,)))
                    scaled = jnp.clip(value, -TAU, TAU)
                    sparse[chunk(i), :] = value - scaled
                    dual[chunk(i), :] = MU * scaled
                for move in moves:
                    move.wait()

            ins = [(a, pltpu.VMEM) for a in (inverse, *lefts, stacked, base, *before)]
            outs = [((n_rows, half), F32, pltpu.VMEM)] * 2
            if p:
                outs += [((n_rows, n_cols), F32, pltpu.HBM)]
            else:
                outs += [((rank, n_rows), F32, pltpu.HBM), tops_out]
            scratch = [pltpu.VMEM((rank, n_rows), F32), pltpu.SemaphoreType.DMA((steps, 1))]
            cost = (3 * rank * n_rows * n_cols, 4 * n_rows * n_cols)
            return call(body, "final", ins, outs, scratch, cost=cost)

        def widen(inverse, own, other):
            def body(inverse, own, other, wide_own, wide_other, out):
                grams = []
                for stacked, wide in ((own, wide_own), (other, wide_other)):
                    value = dot(inverse[...], unstack(stacked), ((1,), (0,)), HIGH)
                    wide[...] = value
                    grams.append(dot(value, value, ((1,), (1,)), HIGH))
                out[...] = pack(grams[0] + grams[1])

            ins = [(a, pltpu.VMEM) for a in (inverse, own, other)]
            outs = [((rank, half), F32, pltpu.VMEM)] * 2 + [((gram_rows, LANES), F32, pltpu.VMEM)]
            return call(body, "widen", ins, outs, cost=(10**8, MIB), limit=8)

        def finish(one, two, wide, made, first_dual, sparse):
            def body(*refs):
                one, two, own, other, sparse_1, dual_1, dual_0, _ = refs[:8]
                out, sparse_out, dual_out, inverse, right, sem, sems, dual_sems = refs[8:]
                s = place()
                moves = put((sparse_1, dual_1), (sparse_out, dual_out), 1, s, sems)
                moves += put((dual_0,), (dual_out,), 0, s, dual_sems)
                invert(one[...] + two[...], inverse)
                for p, value in enumerate((own, other)):
                    at = pl.ds(pix_at(p, s), half)
                    right[:, at] = dot(inverse[...], value[...], ((1,), (0,)), HIGH)
                    move = pltpu.make_async_copy(right.at[:, at], out.at[:, at], sem.at[p])
                    move.start()
                    moves.append(move)
                for move in moves:
                    move.wait()

            ins = [(a, pltpu.VMEM) for a in (one, two, *wide, *made, first_dual)] + [(sparse, pltpu.HBM)]
            results = [((rank, n_cols), F32, pltpu.HBM)] + [((n_rows, n_cols), F32, pltpu.HBM)] * 2
            scratch = [pltpu.VMEM((rank, rank), F32), pltpu.VMEM((rank, n_cols), F32)]
            scratch += [pltpu.SemaphoreType.DMA(shape) for shape in ((2,), (steps, 2), (steps, 1))]
            return call(body, "finish", ins, results, scratch, {7: 1}, cost=(10**8, 8 * MIB))

        seen, pulls, own, other, part = first(right_init)
        base = [None, None]
        for step in range(ITERS):
            panel = sum_gal(part)
            inverse, own_wide, quarters = sum_pix(panel, own, other)
            if step < ITERS - 1:
                given = own_wide, seen, pulls
                base[0], own, part, tops = middle(0, (0, 1), inverse, panel, *given, None)
                quarters, tops = lax.optimization_barrier((quarters, tops))
                given = inverse, tops, unfold(1, *quarters), seen, pulls, part
                base[1], other, away = middle(1, (0,), *given)
                base[1], other, mine = middle(1, (1,), *given, (base[1], *other))
                part = away + mine
            else:
                other_wide = unfold(1, *quarters)
                *wide, gram = widen(inverse, own_wide, other_wide)
                *made, left, tops = final(0, inverse, panel, own_wide, base[0])
                bit = 1
                while 2 * bit < n_gal:
                    gram = add(gram, swap(gram, "gal", bit))
                    bit *= 2
                got = swap(gram, "gal", bit)
                *later, sparse = final(1, inverse, tops, other_wide, base[1], made[:1])
                right, sparse, dual = finish(gram, got, wide, later, made[1], sparse)
        return sparse, dual, left, right

    return jax.shard_map(
        per_device,
        mesh=mesh,
        in_specs=(P("pix", "gal"), P("pix", "gal"), P("pix", "gal"), P(None, "gal")),
        out_specs=(P("pix", "gal"), P("pix", "gal"), P(None, "pix"), P(None, "gal")),
        check_vma=False,
    )
```

```python
import jax
import jax.numpy as jnp
from jax import lax
from jax.experimental import pallas as pl
from jax.experimental.pallas import tpu as pltpu
from jax.sharding import PartitionSpec as P

ITERS = 2


MU = 1.25
TAU = 0.6 / 1.25
HIGH = lax.Precision.HIGHEST
CORES = 2
LANES = 128
F32, BF16 = jnp.float32, jnp.bfloat16
MIB = 1 << 20


def split(value):
    high = value.astype(BF16)
    return high, (value - high.astype(F32)).astype(BF16)


def dot(a, b, dims, precision=None):
    return lax.dot_general(a, b, (dims, ((), ())), precision=precision, preferred_element_type=F32)


def dot_nt(a, b):
    rows = a[0].shape[0]
    both = dot(jnp.concatenate(a, axis=0), b[0], ((1,), (1,)))
    return both[:rows] + both[rows:] + dot(a[0], b[1], ((1,), (1,)))


def dot_nn(a, b):
    rows = a[0].shape[0]
    both = dot(jnp.concatenate(a, axis=0), b[0], ((1,), (0,)))
    return both[:rows] + both[rows:] + dot(a[0], b[1], ((1,), (0,)))


def call(body, name, ins, outs, scratch=(), aliases=None, cost=(0, 0), limit=16):
    return pl.pallas_call(
        body,
        name=name,
        in_specs=[pl.BlockSpec(memory_space=space) for _, space in ins],
        out_specs=[pl.BlockSpec(memory_space=space) for _, _, space in outs],
        out_shape=[jax.ShapeDtypeStruct(shape, dtype) for shape, dtype, _ in outs],
        scratch_shapes=list(scratch),
        input_output_aliases=aliases or {},
        compiler_params=pltpu.CompilerParams(vmem_limit_bytes=limit * MIB),
        cost_estimate=pl.CostEstimate(flops=cost[0], bytes_accessed=cost[1], transcendentals=0),
    )(*[pltpu.with_memory_space_constraint(a, pltpu.HBM) if m is pltpu.HBM else a for a, m in ins])


def invert(packed, out):
    gram_rows, rank = packed.shape[0], out.shape[0]
    full = (8, LANES)
    lane = lax.broadcasted_iota(jnp.int32, full, 1)
    sub = lax.broadcasted_iota(jnp.int32, full, 0)
    turned = pltpu.roll(packed, LANES // 2, 1)
    rows = []
    for j in range(rank // 8):
        source = packed if 8 * j < gram_rows else turned
        at = 8 * j % gram_rows
        eye = jnp.where(lane - rank == sub + 8 * j, 1.0, 0.0)
        rows.append(jnp.where(lane < rank, source[at : at + 8], eye))
    wide = 8
    for k in range(0, rank, wide):
        r, at = divmod(k, 8)
        after = range(r if at + wide < 8 else r + 1, rank // 8)
        lines = [jnp.broadcast_to(rows[r][at + p : at + p + 1, :], full) for p in range(wide)]
        core = {
            (p, q): jnp.broadcast_to(lines[p][:, k + q : k + q + 1], full)
            for p in range(wide)
            for q in range(p, wide)
        }
        columns = {
            (j, p): jnp.broadcast_to(rows[j][:, k + p : k + p + 1], full) for j in after for p in range(wide)
        }
        for p in range(wide):
            inverse = 1.0 / core[p, p]
            factors = [core[p, q] * inverse for q in range(p + 1, wide)]
            for q, factor in zip(range(p + 1, wide), factors):
                for t in range(q, wide):
                    core[q, t] = core[q, t] - factor * core[p, t]
            scaled = lines[p] * inverse
            for q in range(p + 1, wide):
                lines[q] = lines[q] - core[p, q] * scaled
            for j in after:
                column = columns[j, p]
                if j == r:
                    column = jnp.where(sub >= at + wide, column, 0.0)
                rows[j] = rows[j] - column * scaled
                for q, factor in zip(range(p + 1, wide), factors):
                    columns[j, q] = columns[j, q] - factor * columns[j, p]
            done = lines[p] * lax.rsqrt(core[p, p])
            out[k + p : k + p + 1, :] = done[0:1, rank:]


def pack(gram):
    rows = gram.shape[0] // 2
    return jnp.concatenate([gram[:rows], gram[rows:]], axis=1)


def unstack(ref):
    blocks = ref.shape[0] // 64
    return jnp.concatenate([ref[64 * t : 64 * (t + 1), :] for t in range(blocks)], axis=1)


def solution(mesh):
    n_gal, n_pix = mesh.shape["gal"], mesh.shape["pix"]
    levels = n_pix.bit_length() - 1

    def swap(value, axis, bit):
        n = mesh.shape[axis]
        return lax.ppermute(value, axis, [(i, i ^ bit) for i in range(n)])

    def per_device(observed, sparse_init, dual_init, right_init):
        rank = right_init.shape[0]
        n_rows, n_cols = observed.shape
        half = n_cols // 2
        tall = min(256, n_rows // 2)
        steps = n_rows // tall
        quarter = rank * (half // LANES) // 2
        gram_rows = rank * rank // LANES

        def place():
            pix = lax.axis_index("pix")
            return [lax.rem(lax.axis_index("gal"), CORES)] + [lax.rem(pix >> level, 2) for level in range(levels)]

        def gal_at(i, s):
            turn = (1 - s[0]) * (steps // 2)
            return pl.multiple_of(lax.rem(i + turn, steps) * tall, tall)

        def pix_at(p, s):
            return pl.multiple_of(lax.rem(s[1] + p, 2) * half, half)

        def chunk(i):
            return slice(tall * i, tall * (i + 1))

        def join(pair):
            return jnp.concatenate([half[...] for half in pair], axis=1)

        def small(body, name, ins, rows, scratch=()):
            outs = [((n, LANES), F32, pltpu.VMEM) for n in rows]
            return call(body, name, ins, outs, scratch, cost=(10**5, 10**6), limit=4)

        def add(*arrays):
            def body(*refs):
                *ins, out = refs
                total = ins[0][...]
                for ref in ins[1:]:
                    total = total + ref[...]
                out[...] = total

            out = (arrays[0].shape, F32, pltpu.VMEM)
            return call(body, "add", [(a, pltpu.VMEM) for a in arrays], [out], cost=(10**5, 10**6), limit=4)[0]

        def first(right):
            def body(o_in, s_in, d_in, r_in, o, u, h0, l0, h1, l1, away, mine, sp, d, right, r_sem, sems):
                s = place()
                right_move = pltpu.make_async_copy(r_in, right, r_sem)
                right_move.start()
                moves = {}
                for i in range(steps):
                    for a, (source, target) in enumerate(((o_in, o), (s_in, sp), (d_in, d))):
                        block = source.at[pl.ds(gal_at(i, s), tall), :]
                        move = pltpu.make_async_copy(block, target.at[chunk(i), :], sems.at[i, a])
                        move.start(priority=(i + a) % 2)
                        moves[i, a] = move
                right_move.wait()
                rights = [split(right[:, pl.ds(pix_at(p, s), half)]) for p in (0, 1)]
                for i in range(steps):
                    total = None
                    for a in range(3):
                        moves[i, a].wait()
                    for p, (h, l) in enumerate(((h0, l0), (h1, l1))):
                        at = chunk(i), pl.ds(pix_at(p, s), half)
                        pulled = o[at] + d[at] * (1 / MU)
                        u[at] = pulled
                        pair = split(pulled - sp[at])
                        h[chunk(i), :], l[chunk(i), :] = pair
                        term = dot_nt(rights[p], pair)
                        total = term if total is None else total + term
                    out = away if i < steps // 2 else mine
                    out[:, chunk(i % (steps // 2))] = total

            ins = [(a, pltpu.HBM) for a in (observed, sparse_init, dual_init, right)]
            outs = [((n_rows, n_cols), F32, pltpu.VMEM)] * 2 + [((n_rows, half), BF16, pltpu.VMEM)] * 4
            outs += [((rank, n_rows // 2), F32, pltpu.VMEM)] * 2
            scratch = [pltpu.VMEM((n_rows, n_cols), F32)] * 2 + [pltpu.VMEM((rank, n_cols), F32)]
            scratch += [pltpu.SemaphoreType.DMA(()), pltpu.SemaphoreType.DMA((steps, 3))]
            cost = (6 * rank * n_rows * n_cols, 16 * n_rows * n_cols)
            got = call(body, "first", ins, outs, scratch, cost=cost)
            return got[0], got[1], got[2:4], got[4:6], got[6:8]

        def sum_gal(part):
            away, mine = part
            mine = add(mine, swap(away, "gal", 1))
            got = [
                lax.ppermute(mine, "gal", [(i, (i + CORES * k) % n_gal) for i in range(n_gal)])
                for k in range(1, n_gal // CORES)
            ]
            mine = add(mine, *got)
            return swap(mine, "gal", 1), mine

        def multiply_mine(mine, pair, other_pair):
            def body(mine, high, low, high_other, low_other, own, other, gram):
                panel = split(mine[...])
                for at, out in (((high, low), own), ((high_other, low_other), other)):
                    put_stack(dot_nn(panel, [ref[n_rows // 2 :, :] for ref in at]), out)
                gram[...] = pack(dot(mine[...], mine[...], ((1,), (1,)), HIGH))

            ins = [(a, pltpu.VMEM) for a in (mine, *pair, *other_pair)]
            outs = [((rows, LANES), F32, pltpu.VMEM) for rows in (2 * quarter, 2 * quarter, gram_rows)]
            cost = (3 * rank * n_rows * n_cols, 2 * n_rows * n_cols)
            return call(body, "multiply_mine", ins, outs, cost=cost)

        def multiply_other(away, pair, before, gram):
            def body(away, high, low, before, gram, straight, across, stack):
                s = place()
                pairs = [ref[: n_rows // 2, :] for ref in (high, low)]
                put_stack(dot_nn(split(away[...]), pairs), stack)
                total = gram[...] + pack(dot(away[...], away[...], ((1,), (1,)), HIGH))
                for side, out in ((s[2], straight), (1 - s[2], across)):
                    out[:quarter, :] = stack[rows_at(side), :] + before[rows_at(side), :]
                    out[quarter:, :] = total

            ins = [(a, pltpu.VMEM) for a in (away, *pair, before, gram)]
            outs = [((quarter + gram_rows, LANES), F32, pltpu.VMEM)] * 2
            cost = (2 * rank * n_rows * n_cols, n_rows * n_cols)
            return call(body, "multiply_other", ins, outs, [pltpu.VMEM((2 * quarter, LANES), F32)], cost=cost)

        def multiply_own(away, pair, before, sent):
            def body(away, high, low, before, sent, keep, out, stack):
                s = place()
                pairs = [ref[: n_rows // 2, :] for ref in (high, low)]
                put_stack(dot_nn(split(away[...]), pairs), stack)
                for side, ref in ((s[2], keep), (1 - s[2], out)):
                    ref[:quarter, :] = stack[rows_at(side), :] + before[rows_at(side), :]
                out[quarter:, :] = sent[quarter:, :]

            ins = [(a, pltpu.VMEM) for a in (away, *pair, before, sent)]
            outs = [((rows, LANES), F32, pltpu.VMEM) for rows in (quarter, quarter + gram_rows)]
            cost = (10**9, 8 * MIB)
            return call(body, "multiply_own", ins, outs, [pltpu.VMEM((2 * quarter, LANES), F32)], cost=cost)

        def put_stack(value, stack):
            for t in range(half // LANES):
                stack[rank * t : rank * (t + 1), :] = value[:, LANES * t : LANES * (t + 1)]

        def rows_at(side):
            return pl.ds(pl.multiple_of(side * quarter, quarter), quarter)

        def eliminate(one, two):
            def body(one, two, out):
                invert(one[-gram_rows:, :] + two[-gram_rows:, :], out)

            ins = [(one, pltpu.VMEM), (two, pltpu.VMEM)]
            outs = [((rank, rank), F32, pltpu.VMEM)]
            return call(body, "eliminate", ins, outs, cost=(10**8, 8 * MIB), limit=4)[0]

        def collect(keep, sent, gots):
            rows = keep.shape[0]

            def body(keep, sent, *refs):
                *gots, out = refs
                top, low = keep[...], sent[rows:, :]
                for got in gots:
                    top, low = top + got[:rows, :], low + got[rows:, :]
                out[:rows, :] = top
                out[rows:, :] = low

            ins = [(a, pltpu.VMEM) for a in (keep, sent, *gots)]
            return small(body, "collect", ins, [rows + gram_rows])[0]

        def divide(level, total):
            rows = (total.shape[0] - gram_rows) // 2

            def body(total, keep, out):
                s = place()
                for side, ref in ((s[1 + level], keep), (1 - s[1 + level], out)):
                    ref[:rows, :] = total[pl.ds(pl.multiple_of(side * rows, rows), rows), :]
                out[rows:, :] = total[2 * rows :, :]

            return small(body, "divide", [(total, pltpu.VMEM)], [rows, rows + gram_rows])

        def unfold(level, value, got):
            rows = value.shape[0]

            def body(value, got, out):
                s = place()
                for side, ref in ((s[1 + level], value), (1 - s[1 + level], got)):
                    out[pl.ds(pl.multiple_of(side * rows, rows), rows), :] = ref[...]

            ins = [(value, pltpu.VMEM), (got, pltpu.VMEM)]
            return small(body, "unfold", ins, [2 * rows])[0]

        def top(one, two):
            rows = one.shape[0] - gram_rows

            def body(one, two, out):
                out[...] = one[:rows, :] + two[:rows, :]

            return small(body, "top", [(one, pltpu.VMEM), (two, pltpu.VMEM)], [rows])[0]

        def sum_pix(panel, own, other):
            away, mine = panel
            own_before, other_before, gram = multiply_mine(mine, own, other)
            straight, across = multiply_other(away, other, other_before, gram)
            gots = [swap(straight, "pix", 1), swap(across, "pix", 3)]
            keep, beside = multiply_own(away, own, own_before, straight)
            total = collect(keep, straight, gots + [swap(beside, "pix", 2)])
            for level in range(2, levels - 1):
                keep, sent = divide(level, total)
                total = collect(keep, sent, [swap(sent, "pix", 1 << level)])
            got = swap(total, "pix", 1 << (levels - 1))
            value = top(total, got)
            inverse = eliminate(total, got)
            for level in range(levels - 2, 1, -1):
                value = unfold(level, value, swap(value, "pix", 1 << level))
            beside, straight, across = [swap(value, "pix", bit) for bit in (2, 1, 3)]
            return inverse, unfold(1, value, beside), (straight, across)

        def tops_of(inverse, panel):
            left = dot(inverse[...], join(panel), ((1,), (0,)), HIGH)
            high, low = split(left)
            return left, jnp.concatenate([high, low, high], axis=0)

        def wides_of(inverse, stacked):
            high, low = split(dot(inverse[...], unstack(stacked), ((1,), (0,)), HIGH))
            return (high, low), jnp.concatenate([high, high, low], axis=0)

        tops_out = (3 * rank, n_rows), BF16, pltpu.VMEM

        def middle(p, sides, inverse, left, stacked, o, u, before, arrays=()):
            n = len(sides)
            blocks = [i for i in range(steps) if i // (steps // 2) in sides]
            lefts = [left] if p else list(left)

            def body(inverse, *rest):
                s = place()
                panel, (stacked, o, u, *rest) = rest[: len(lefts)], rest[len(lefts) :]
                base, high, low, *after = rest[n * p + len(arrays) :]
                if p:
                    tops = panel[0]
                else:
                    tops = after[n]
                    tops[...] = tops_of(inverse, panel)[1]
                right, wides = wides_of(inverse, stacked)
                for k, i in enumerate(blocks):
                    lowrank = dot(tops[:, chunk(i)], wides, ((0,), (0,)))
                    at = chunk(i), pl.ds(pix_at(p, s), half)
                    value = u[at] - lowrank
                    scaled = jnp.clip(value, -TAU, TAU)
                    moved = o[at] + scaled
                    base[chunk(i), :] = moved
                    pair = split(moved + (scaled - value))
                    high[chunk(i), :], low[chunk(i), :] = pair
                    term = dot_nt(right, pair)
                    side, block = divmod(k, steps // 2)
                    after[side][:, chunk(block)] = rest[side][:, chunk(block)] + term if p else term

            ins = [inverse, *lefts, stacked, o, u]
            ins += [before[side] for side in sides] if p else []
            aliases = {len(ins) + k: k for k in range(len(arrays))}
            outs = [((n_rows, half), F32, pltpu.VMEM)] + [((n_rows, half), BF16, pltpu.VMEM)] * 2
            outs += [((rank, n_rows // 2), F32, pltpu.VMEM)] * n + [tops_out] * (1 - p)
            cost = (9 * rank * n_rows * n_cols // (3 - n), 4 * n_rows * n_cols // (3 - n))
            ins = [(a, pltpu.VMEM) for a in (*ins, *arrays)]
            base, high, low, *rest = call(body, "middle", ins, outs, aliases=aliases, cost=cost)
            return base, (high, low), *((rest,) if p else (rest[:n], rest[n]))

        def put(sources, targets, p, s, sems):
            def moves(i):
                for a, (source, target) in enumerate(zip(sources, targets)):
                    block = target.at[pl.ds(gal_at(i, s), tall), pl.ds(pix_at(p, s), half)]
                    rows = pl.ds(pl.multiple_of(i * tall, tall), tall)
                    yield pltpu.make_async_copy(source.at[rows, :], block, sems.at[i, a])

            def start(i, carry):
                for a, move in enumerate(moves(i)):
                    move.start(priority=a)
                return carry

            lax.fori_loop(0, steps, start, 0)
            return [move for i in range(steps) for move in moves(i)]

        def final(p, inverse, left, stacked, base, before=()):
            lefts = [left] if p else list(left)

            def body(inverse, *rest):
                s = place()
                panel, (stacked, base, *rest) = rest[: len(lefts)], rest[len(lefts) :]
                sparse, dual, *outs, left_part, sems = rest[len(before) :]
                if p:
                    moves = put(rest[:1], outs, 0, s, sems)
                    tops = panel[0]
                else:
                    value, stack = tops_of(inverse, panel)
                    tops = outs[1]
                    tops[...] = stack
                    for i in range(steps):
                        left_part[:, pl.ds(gal_at(i, s), tall)] = value[:, chunk(i)]
                    moves = [pltpu.make_async_copy(left_part, outs[0], sems.at[0, 0])]
                    moves[0].start()
                _, wides = wides_of(inverse, stacked)
                for i in range(steps):
                    value = base[chunk(i), :] - dot(tops[:, chunk(i)], wides, ((0,), (0,)))
                    scaled = jnp.clip(value, -TAU, TAU)
                    sparse[chunk(i), :] = value - scaled
                    dual[chunk(i), :] = MU * scaled
                for move in moves:
                    move.wait()

            ins = [(a, pltpu.VMEM) for a in (inverse, *lefts, stacked, base, *before)]
            outs = [((n_rows, half), F32, pltpu.VMEM)] * 2
            if p:
                outs += [((n_rows, n_cols), F32, pltpu.HBM)]
            else:
                outs += [((rank, n_rows), F32, pltpu.HBM), tops_out]
            scratch = [pltpu.VMEM((rank, n_rows), F32), pltpu.SemaphoreType.DMA((steps, 1))]
            cost = (3 * rank * n_rows * n_cols, 4 * n_rows * n_cols)
            return call(body, "final", ins, outs, scratch, cost=cost)

        def widen(inverse, stacked, gram=None):
            def body(inverse, stacked, *rest):
                *before, wide, out = rest
                value = dot(inverse[...], unstack(stacked), ((1,), (0,)), HIGH)
                wide[...] = value
                term = pack(dot(value, value, ((1,), (1,)), HIGH))
                out[...] = before[0][...] + term if before else term

            arrays = (inverse, stacked) if gram is None else (inverse, stacked, gram)
            outs = [((rank, half), F32, pltpu.VMEM), ((gram_rows, LANES), F32, pltpu.VMEM)]
            return call(body, "widen", [(a, pltpu.VMEM) for a in arrays], outs, cost=(10**8, MIB), limit=8)

        def finish(one, two, wide, made, first_dual, sparse):
            def body(*refs):
                one, two, own, other, sparse_1, dual_1, dual_0, _ = refs[:8]
                out, sparse_out, dual_out, inverse, right, sem, sems, dual_sems = refs[8:]
                s = place()
                moves = put((sparse_1, dual_1), (sparse_out, dual_out), 1, s, sems)
                moves += put((dual_0,), (dual_out,), 0, s, dual_sems)
                invert(one[...] + two[...], inverse)
                for p, value in enumerate((own, other)):
                    at = pl.ds(pix_at(p, s), half)
                    right[:, at] = dot(inverse[...], value[...], ((1,), (0,)), HIGH)
                    move = pltpu.make_async_copy(right.at[:, at], out.at[:, at], sem.at[p])
                    move.start()
                    moves.append(move)
                for move in moves:
                    move.wait()

            ins = [(a, pltpu.VMEM) for a in (one, two, *wide, *made, first_dual)] + [(sparse, pltpu.HBM)]
            results = [((rank, n_cols), F32, pltpu.HBM)] + [((n_rows, n_cols), F32, pltpu.HBM)] * 2
            scratch = [pltpu.VMEM((rank, rank), F32), pltpu.VMEM((rank, n_cols), F32)]
            scratch += [pltpu.SemaphoreType.DMA(shape) for shape in ((2,), (steps, 2), (steps, 1))]
            return call(body, "finish", ins, results, scratch, {7: 1}, cost=(10**8, 8 * MIB))

        seen, pulls, own, other, part = first(right_init)
        base = [None, None]
        for step in range(ITERS):
            panel = sum_gal(part)
            inverse, own_wide, quarters = sum_pix(panel, own, other)
            if step < ITERS - 1:
                given = own_wide, seen, pulls
                base[0], own, part, tops = middle(0, (0, 1), inverse, panel, *given, None)
                quarters, tops = lax.optimization_barrier((quarters, tops))
                given = inverse, tops, unfold(1, *quarters), seen, pulls, part
                base[1], other, away = middle(1, (0,), *given)
                base[1], other, mine = middle(1, (1,), *given, (base[1], *other))
                part = away + mine
            else:
                wide_own, gram = widen(inverse, own_wide)
                quarters, gram = lax.optimization_barrier((quarters, gram))
                other_wide = unfold(1, *quarters)
                wide_other, gram = widen(inverse, other_wide, gram)
                wide = wide_own, wide_other
                *made, left, tops = final(0, inverse, panel, own_wide, base[0])
                bit = 1
                while 2 * bit < n_gal:
                    gram = add(gram, swap(gram, "gal", bit))
                    bit *= 2
                got = swap(gram, "gal", bit)
                *later, sparse = final(1, inverse, tops, other_wide, base[1], made[:1])
                right, sparse, dual = finish(gram, got, wide, later, made[1], sparse)
        return sparse, dual, left, right

    return jax.shard_map(
        per_device,
        mesh=mesh,
        in_specs=(P("pix", "gal"), P("pix", "gal"), P("pix", "gal"), P(None, "gal")),
        out_specs=(P("pix", "gal"), P("pix", "gal"), P(None, "pix"), P(None, "gal")),
        check_vma=False,
    )
```

```python
import jax
import jax.numpy as jnp
from jax import lax
from jax.experimental import pallas as pl
from jax.experimental.pallas import tpu as pltpu
from jax.sharding import PartitionSpec as P

ITERS = 2


MU = 1.25
TAU = 0.6 / 1.25
HIGH = lax.Precision.HIGHEST
CORES = 2
LANES = 128
F32, BF16 = jnp.float32, jnp.bfloat16
MIB = 1 << 20


def split(value):
    high = value.astype(BF16)
    return high, (value - high.astype(F32)).astype(BF16)


def dot(a, b, dims, precision=None):
    return lax.dot_general(a, b, (dims, ((), ())), precision=precision, preferred_element_type=F32)


def dot_nt(a, b):
    rows = a[0].shape[0]
    both = dot(jnp.concatenate(a, axis=0), b[0], ((1,), (1,)))
    return both[:rows] + both[rows:] + dot(a[0], b[1], ((1,), (1,)))


def dot_nn(a, b):
    rows = a[0].shape[0]
    both = dot(jnp.concatenate(a, axis=0), b[0], ((1,), (0,)))
    return both[:rows] + both[rows:] + dot(a[0], b[1], ((1,), (0,)))


def call(body, name, ins, outs, scratch=(), aliases=None, cost=(0, 0), limit=16):
    return pl.pallas_call(
        body,
        name=name,
        in_specs=[pl.BlockSpec(memory_space=space) for _, space in ins],
        out_specs=[pl.BlockSpec(memory_space=space) for _, _, space in outs],
        out_shape=[jax.ShapeDtypeStruct(shape, dtype) for shape, dtype, _ in outs],
        scratch_shapes=list(scratch),
        input_output_aliases=aliases or {},
        compiler_params=pltpu.CompilerParams(vmem_limit_bytes=limit * MIB),
        cost_estimate=pl.CostEstimate(flops=cost[0], bytes_accessed=cost[1], transcendentals=0),
    )(*[pltpu.with_memory_space_constraint(a, pltpu.HBM) if m is pltpu.HBM else a for a, m in ins])


def invert(packed, out):
    gram_rows, rank = packed.shape[0], out.shape[0]
    full = (8, LANES)
    lane = lax.broadcasted_iota(jnp.int32, full, 1)
    sub = lax.broadcasted_iota(jnp.int32, full, 0)
    turned = pltpu.roll(packed, LANES // 2, 1)
    rows = []
    for j in range(rank // 8):
        source = packed if 8 * j < gram_rows else turned
        at = 8 * j % gram_rows
        eye = jnp.where(lane - rank == sub + 8 * j, 1.0, 0.0)
        rows.append(jnp.where(lane < rank, source[at : at + 8], eye))
    wide = 8
    for k in range(0, rank, wide):
        r, at = divmod(k, 8)
        after = range(r if at + wide < 8 else r + 1, rank // 8)
        lines = [jnp.broadcast_to(rows[r][at + p : at + p + 1, :], full) for p in range(wide)]
        core = {
            (p, q): jnp.broadcast_to(lines[p][:, k + q : k + q + 1], full)
            for p in range(wide)
            for q in range(p, wide)
        }
        columns = {
            (j, p): jnp.broadcast_to(rows[j][:, k + p : k + p + 1], full) for j in after for p in range(wide)
        }
        for p in range(wide):
            inverse = 1.0 / core[p, p]
            factors = [core[p, q] * inverse for q in range(p + 1, wide)]
            for q, factor in zip(range(p + 1, wide), factors):
                for t in range(q, wide):
                    core[q, t] = core[q, t] - factor * core[p, t]
            scaled = lines[p] * inverse
            for q in range(p + 1, wide):
                lines[q] = lines[q] - core[p, q] * scaled
            for j in after:
                column = columns[j, p]
                if j == r:
                    column = jnp.where(sub >= at + wide, column, 0.0)
                rows[j] = rows[j] - column * scaled
                for q, factor in zip(range(p + 1, wide), factors):
                    columns[j, q] = columns[j, q] - factor * columns[j, p]
            done = lines[p] * lax.rsqrt(core[p, p])
            out[k + p : k + p + 1, :] = done[0:1, rank:]


def pack(gram):
    rows = gram.shape[0] // 2
    return jnp.concatenate([gram[:rows], gram[rows:]], axis=1)


def unstack(ref):
    blocks = ref.shape[0] // 64
    return jnp.concatenate([ref[64 * t : 64 * (t + 1), :] for t in range(blocks)], axis=1)


def solution(mesh):
    n_gal, n_pix = mesh.shape["gal"], mesh.shape["pix"]
    levels = n_pix.bit_length() - 1

    def swap(value, axis, bit):
        n = mesh.shape[axis]
        return lax.ppermute(value, axis, [(i, i ^ bit) for i in range(n)])

    def per_device(observed, sparse_init, dual_init, right_init):
        rank = right_init.shape[0]
        n_rows, n_cols = observed.shape
        half = n_cols // 2
        tall = min(256, n_rows // 2)
        steps = n_rows // tall
        quarter = rank * (half // LANES) // 2
        gram_rows = rank * rank // LANES

        def place():
            pix = lax.axis_index("pix")
            return [lax.rem(lax.axis_index("gal"), CORES)] + [lax.rem(pix >> level, 2) for level in range(levels)]

        def gal_at(i, s):
            turn = (1 - s[0]) * (steps // 2)
            return pl.multiple_of(lax.rem(i + turn, steps) * tall, tall)

        def pix_at(p, s):
            return pl.multiple_of(lax.rem(s[1] + p, 2) * half, half)

        def chunk(i):
            return slice(tall * i, tall * (i + 1))

        def join(pair):
            return jnp.concatenate([half[...] for half in pair], axis=1)

        def small(body, name, ins, rows, scratch=()):
            outs = [((n, LANES), F32, pltpu.VMEM) for n in rows]
            return call(body, name, ins, outs, scratch, cost=(10**5, 10**6), limit=4)

        def add(*arrays):
            def body(*refs):
                *ins, out = refs
                total = ins[0][...]
                for ref in ins[1:]:
                    total = total + ref[...]
                out[...] = total

            out = (arrays[0].shape, F32, pltpu.VMEM)
            return call(body, "add", [(a, pltpu.VMEM) for a in arrays], [out], cost=(10**5, 10**6), limit=4)[0]

        def first(right):
            fine, blocks = tall // 2, 2 * steps

            def rows(i):
                return slice(fine * i, fine * (i + 1))

            def body(o_in, s_in, d_in, r_in, o, u, h0, l0, h1, l1, away, mine, sp, d, right, r_sem, sems):
                s = place()
                right_move = pltpu.make_async_copy(r_in, right, r_sem)
                right_move.start()
                moves = {}
                for i in range(blocks):
                    for a, (source, target) in enumerate(((o_in, o), (s_in, sp), (d_in, d))):
                        at = pl.multiple_of(gal_at(i // 2, s) + i % 2 * fine, fine)
                        block = source.at[pl.ds(at, fine), :]
                        move = pltpu.make_async_copy(block, target.at[rows(i), :], sems.at[i, a])
                        move.start(priority=(i + a) % 2)
                        moves[i, a] = move
                right_move.wait()
                rights = [split(right[:, pl.ds(pix_at(p, s), half)]) for p in (0, 1)]
                for i in range(blocks):
                    total = None
                    for a in range(3):
                        moves[i, a].wait()
                    for p, (h, l) in enumerate(((h0, l0), (h1, l1))):
                        at = rows(i), pl.ds(pix_at(p, s), half)
                        pulled = o[at] + d[at] * (1 / MU)
                        u[at] = pulled
                        pair = split(pulled - sp[at])
                        h[rows(i), :], l[rows(i), :] = pair
                        term = dot_nt(rights[p], pair)
                        total = term if total is None else total + term
                    out = away if i < steps else mine
                    out[:, rows(i % steps)] = total

            ins = [(a, pltpu.HBM) for a in (observed, sparse_init, dual_init, right)]
            outs = [((n_rows, n_cols), F32, pltpu.VMEM)] * 2 + [((n_rows, half), BF16, pltpu.VMEM)] * 4
            outs += [((rank, n_rows // 2), F32, pltpu.VMEM)] * 2
            scratch = [pltpu.VMEM((n_rows, n_cols), F32)] * 2 + [pltpu.VMEM((rank, n_cols), F32)]
            scratch += [pltpu.SemaphoreType.DMA(()), pltpu.SemaphoreType.DMA((blocks, 3))]
            cost = (6 * rank * n_rows * n_cols, 16 * n_rows * n_cols)
            got = call(body, "first", ins, outs, scratch, cost=cost)
            return got[0], got[1], got[2:4], got[4:6], got[6:8]

        def sum_gal(part):
            away, mine = part
            mine = add(mine, swap(away, "gal", 1))
            got = [
                lax.ppermute(mine, "gal", [(i, (i + CORES * k) % n_gal) for i in range(n_gal)])
                for k in range(1, n_gal // CORES)
            ]
            mine = add(mine, *got)
            return swap(mine, "gal", 1), mine

        def multiply_mine(mine, pair, other_pair):
            def body(mine, high, low, high_other, low_other, own, other, gram):
                panel = split(mine[...])
                for at, out in (((high, low), own), ((high_other, low_other), other)):
                    put_stack(dot_nn(panel, [ref[n_rows // 2 :, :] for ref in at]), out)
                gram[...] = pack(dot(mine[...], mine[...], ((1,), (1,)), HIGH))

            ins = [(a, pltpu.VMEM) for a in (mine, *pair, *other_pair)]
            outs = [((rows, LANES), F32, pltpu.VMEM) for rows in (2 * quarter, 2 * quarter, gram_rows)]
            cost = (3 * rank * n_rows * n_cols, 2 * n_rows * n_cols)
            return call(body, "multiply_mine", ins, outs, cost=cost)

        def multiply_other(away, pair, before, gram):
            def body(away, high, low, before, gram, straight, across, stack):
                s = place()
                pairs = [ref[: n_rows // 2, :] for ref in (high, low)]
                put_stack(dot_nn(split(away[...]), pairs), stack)
                total = gram[...] + pack(dot(away[...], away[...], ((1,), (1,)), HIGH))
                for side, out in ((s[2], straight), (1 - s[2], across)):
                    out[:quarter, :] = stack[rows_at(side), :] + before[rows_at(side), :]
                    out[quarter:, :] = total

            ins = [(a, pltpu.VMEM) for a in (away, *pair, before, gram)]
            outs = [((quarter + gram_rows, LANES), F32, pltpu.VMEM)] * 2
            cost = (2 * rank * n_rows * n_cols, n_rows * n_cols)
            return call(body, "multiply_other", ins, outs, [pltpu.VMEM((2 * quarter, LANES), F32)], cost=cost)

        def multiply_own(away, pair, before, sent):
            def body(away, high, low, before, sent, keep, out, stack):
                s = place()
                pairs = [ref[: n_rows // 2, :] for ref in (high, low)]
                put_stack(dot_nn(split(away[...]), pairs), stack)
                for side, ref in ((s[2], keep), (1 - s[2], out)):
                    ref[:quarter, :] = stack[rows_at(side), :] + before[rows_at(side), :]
                out[quarter:, :] = sent[quarter:, :]

            ins = [(a, pltpu.VMEM) for a in (away, *pair, before, sent)]
            outs = [((rows, LANES), F32, pltpu.VMEM) for rows in (quarter, quarter + gram_rows)]
            cost = (10**9, 8 * MIB)
            return call(body, "multiply_own", ins, outs, [pltpu.VMEM((2 * quarter, LANES), F32)], cost=cost)

        def put_stack(value, stack):
            for t in range(half // LANES):
                stack[rank * t : rank * (t + 1), :] = value[:, LANES * t : LANES * (t + 1)]

        def rows_at(side):
            return pl.ds(pl.multiple_of(side * quarter, quarter), quarter)

        def eliminate(one, two):
            def body(one, two, out):
                invert(one[-gram_rows:, :] + two[-gram_rows:, :], out)

            ins = [(one, pltpu.VMEM), (two, pltpu.VMEM)]
            outs = [((rank, rank), F32, pltpu.VMEM)]
            return call(body, "eliminate", ins, outs, cost=(10**8, 8 * MIB), limit=4)[0]

        def collect(keep, sent, gots):
            rows = keep.shape[0]

            def body(keep, sent, *refs):
                *gots, out = refs
                top, low = keep[...], sent[rows:, :]
                for got in gots:
                    top, low = top + got[:rows, :], low + got[rows:, :]
                out[:rows, :] = top
                out[rows:, :] = low

            ins = [(a, pltpu.VMEM) for a in (keep, sent, *gots)]
            return small(body, "collect", ins, [rows + gram_rows])[0]

        def divide(level, total):
            rows = (total.shape[0] - gram_rows) // 2

            def body(total, keep, out):
                s = place()
                for side, ref in ((s[1 + level], keep), (1 - s[1 + level], out)):
                    ref[:rows, :] = total[pl.ds(pl.multiple_of(side * rows, rows), rows), :]
                out[rows:, :] = total[2 * rows :, :]

            return small(body, "divide", [(total, pltpu.VMEM)], [rows, rows + gram_rows])

        def unfold(level, value, got):
            rows = value.shape[0]

            def body(value, got, out):
                s = place()
                for side, ref in ((s[1 + level], value), (1 - s[1 + level], got)):
                    out[pl.ds(pl.multiple_of(side * rows, rows), rows), :] = ref[...]

            ins = [(value, pltpu.VMEM), (got, pltpu.VMEM)]
            return small(body, "unfold", ins, [2 * rows])[0]

        def top(one, two):
            rows = one.shape[0] - gram_rows

            def body(one, two, out):
                out[...] = one[:rows, :] + two[:rows, :]

            return small(body, "top", [(one, pltpu.VMEM), (two, pltpu.VMEM)], [rows])[0]

        def sum_pix(panel, own, other):
            away, mine = panel
            own_before, other_before, gram = multiply_mine(mine, own, other)
            straight, across = multiply_other(away, other, other_before, gram)
            gots = [swap(straight, "pix", 1), swap(across, "pix", 3)]
            keep, beside = multiply_own(away, own, own_before, straight)
            total = collect(keep, straight, gots + [swap(beside, "pix", 2)])
            for level in range(2, levels - 1):
                keep, sent = divide(level, total)
                total = collect(keep, sent, [swap(sent, "pix", 1 << level)])
            got = swap(total, "pix", 1 << (levels - 1))
            value = top(total, got)
            inverse = eliminate(total, got)
            for level in range(levels - 2, 1, -1):
                value = unfold(level, value, swap(value, "pix", 1 << level))
            beside, straight, across = [swap(value, "pix", bit) for bit in (2, 1, 3)]
            return inverse, unfold(1, value, beside), (straight, across)

        def tops_of(inverse, panel):
            left = dot(inverse[...], join(panel), ((1,), (0,)), HIGH)
            high, low = split(left)
            return left, jnp.concatenate([high, low, high], axis=0)

        def wides_of(inverse, stacked):
            high, low = split(dot(inverse[...], unstack(stacked), ((1,), (0,)), HIGH))
            return (high, low), jnp.concatenate([high, high, low], axis=0)

        tops_out = (3 * rank, n_rows), BF16, pltpu.VMEM

        def middle(p, sides, inverse, left, stacked, o, u, before, arrays=()):
            n = len(sides)
            blocks = [i for i in range(steps) if i // (steps // 2) in sides]
            lefts = [left] if p else list(left)

            def body(inverse, *rest):
                s = place()
                panel, (stacked, o, u, *rest) = rest[: len(lefts)], rest[len(lefts) :]
                base, high, low, *after = rest[n * p + len(arrays) :]
                if p:
                    tops = panel[0]
                else:
                    tops = after[n]
                    tops[...] = tops_of(inverse, panel)[1]
                right, wides = wides_of(inverse, stacked)
                for k, i in enumerate(blocks):
                    lowrank = dot(tops[:, chunk(i)], wides, ((0,), (0,)))
                    at = chunk(i), pl.ds(pix_at(p, s), half)
                    value = u[at] - lowrank
                    scaled = jnp.clip(value, -TAU, TAU)
                    moved = o[at] + scaled
                    base[chunk(i), :] = moved
                    pair = split(moved + (scaled - value))
                    high[chunk(i), :], low[chunk(i), :] = pair
                    term = dot_nt(right, pair)
                    side, block = divmod(k, steps // 2)
                    after[side][:, chunk(block)] = rest[side][:, chunk(block)] + term if p else term

            ins = [inverse, *lefts, stacked, o, u]
            ins += [before[side] for side in sides] if p else []
            aliases = {len(ins) + k: k for k in range(len(arrays))}
            outs = [((n_rows, half), F32, pltpu.VMEM)] + [((n_rows, half), BF16, pltpu.VMEM)] * 2
            outs += [((rank, n_rows // 2), F32, pltpu.VMEM)] * n + [tops_out] * (1 - p)
            cost = (9 * rank * n_rows * n_cols // (3 - n), 4 * n_rows * n_cols // (3 - n))
            ins = [(a, pltpu.VMEM) for a in (*ins, *arrays)]
            base, high, low, *rest = call(body, "middle", ins, outs, aliases=aliases, cost=cost)
            return base, (high, low), *((rest,) if p else (rest[:n], rest[n]))

        def put(sources, targets, p, s, sems):
            def moves(i):
                for a, (source, target) in enumerate(zip(sources, targets)):
                    block = target.at[pl.ds(gal_at(i, s), tall), pl.ds(pix_at(p, s), half)]
                    rows = pl.ds(pl.multiple_of(i * tall, tall), tall)
                    yield pltpu.make_async_copy(source.at[rows, :], block, sems.at[i, a])

            def start(i, carry):
                for a, move in enumerate(moves(i)):
                    move.start(priority=a)
                return carry

            lax.fori_loop(0, steps, start, 0)
            return [move for i in range(steps) for move in moves(i)]

        def final(p, inverse, left, stacked, base, before=()):
            lefts = [left] if p else list(left)

            def body(inverse, *rest):
                s = place()
                panel, (stacked, base, *rest) = rest[: len(lefts)], rest[len(lefts) :]
                sparse, dual, *outs, left_part, sems = rest[len(before) :]
                if p:
                    moves = put(rest[:1], outs, 0, s, sems)
                    tops = panel[0]
                else:
                    value, stack = tops_of(inverse, panel)
                    tops = outs[1]
                    tops[...] = stack
                    for i in range(steps):
                        left_part[:, pl.ds(gal_at(i, s), tall)] = value[:, chunk(i)]
                    moves = [pltpu.make_async_copy(left_part, outs[0], sems.at[0, 0])]
                    moves[0].start()
                _, wides = wides_of(inverse, stacked)
                for i in range(steps):
                    value = base[chunk(i), :] - dot(tops[:, chunk(i)], wides, ((0,), (0,)))
                    scaled = jnp.clip(value, -TAU, TAU)
                    sparse[chunk(i), :] = value - scaled
                    dual[chunk(i), :] = MU * scaled
                for move in moves:
                    move.wait()

            ins = [(a, pltpu.VMEM) for a in (inverse, *lefts, stacked, base, *before)]
            outs = [((n_rows, half), F32, pltpu.VMEM)] * 2
            if p:
                outs += [((n_rows, n_cols), F32, pltpu.HBM)]
            else:
                outs += [((rank, n_rows), F32, pltpu.HBM), tops_out]
            scratch = [pltpu.VMEM((rank, n_rows), F32), pltpu.SemaphoreType.DMA((steps, 1))]
            cost = (3 * rank * n_rows * n_cols, 4 * n_rows * n_cols)
            return call(body, "final", ins, outs, scratch, cost=cost)

        def widen(inverse, stacked, gram=None):
            def body(inverse, stacked, *rest):
                *before, wide, out = rest
                value = dot(inverse[...], unstack(stacked), ((1,), (0,)), HIGH)
                wide[...] = value
                term = pack(dot(value, value, ((1,), (1,)), HIGH))
                out[...] = before[0][...] + term if before else term

            arrays = (inverse, stacked) if gram is None else (inverse, stacked, gram)
            outs = [((rank, half), F32, pltpu.VMEM), ((gram_rows, LANES), F32, pltpu.VMEM)]
            return call(body, "widen", [(a, pltpu.VMEM) for a in arrays], outs, cost=(10**8, MIB), limit=8)

        def finish(one, two, wide, made, first_dual, sparse):
            def body(*refs):
                one, two, own, other, sparse_1, dual_1, dual_0, _ = refs[:8]
                out, sparse_out, dual_out, inverse, right, sem, sems, dual_sems = refs[8:]
                s = place()
                moves = put((sparse_1, dual_1), (sparse_out, dual_out), 1, s, sems)
                moves += put((dual_0,), (dual_out,), 0, s, dual_sems)
                invert(one[...] + two[...], inverse)
                for p, value in enumerate((own, other)):
                    at = pl.ds(pix_at(p, s), half)
                    right[:, at] = dot(inverse[...], value[...], ((1,), (0,)), HIGH)
                    move = pltpu.make_async_copy(right.at[:, at], out.at[:, at], sem.at[p])
                    move.start()
                    moves.append(move)
                for move in moves:
                    move.wait()

            ins = [(a, pltpu.VMEM) for a in (one, two, *wide, *made, first_dual)] + [(sparse, pltpu.HBM)]
            results = [((rank, n_cols), F32, pltpu.HBM)] + [((n_rows, n_cols), F32, pltpu.HBM)] * 2
            scratch = [pltpu.VMEM((rank, rank), F32), pltpu.VMEM((rank, n_cols), F32)]
            scratch += [pltpu.SemaphoreType.DMA(shape) for shape in ((2,), (steps, 2), (steps, 1))]
            return call(body, "finish", ins, results, scratch, {7: 1}, cost=(10**8, 8 * MIB))

        seen, pulls, own, other, part = first(right_init)
        base = [None, None]
        for step in range(ITERS):
            panel = sum_gal(part)
            inverse, own_wide, quarters = sum_pix(panel, own, other)
            if step < ITERS - 1:
                given = own_wide, seen, pulls
                base[0], own, part, tops = middle(0, (0, 1), inverse, panel, *given, None)
                quarters, tops = lax.optimization_barrier((quarters, tops))
                given = inverse, tops, unfold(1, *quarters), seen, pulls, part
                base[1], other, away = middle(1, (0,), *given)
                base[1], other, mine = middle(1, (1,), *given, (base[1], *other))
                part = away + mine
            else:
                wide_own, gram = widen(inverse, own_wide)
                quarters, gram = lax.optimization_barrier((quarters, gram))
                other_wide = unfold(1, *quarters)
                wide_other, gram = widen(inverse, other_wide, gram)
                wide = wide_own, wide_other
                *made, left, tops = final(0, inverse, panel, own_wide, base[0])
                bit = 1
                while 2 * bit < n_gal:
                    gram = add(gram, swap(gram, "gal", bit))
                    bit *= 2
                got = swap(gram, "gal", bit)
                *later, sparse = final(1, inverse, tops, other_wide, base[1], made[:1])
                right, sparse, dual = finish(gram, got, wide, later, made[1], sparse)
        return sparse, dual, left, right

    return jax.shard_map(
        per_device,
        mesh=mesh,
        in_specs=(P("pix", "gal"), P("pix", "gal"), P("pix", "gal"), P(None, "gal")),
        out_specs=(P("pix", "gal"), P("pix", "gal"), P(None, "pix"), P(None, "gal")),
        check_vma=False,
    )
```
